32 devices in a mesh: section: 2 (over x), dp: 16 (over z, y, core).
Axes of the slice: x: 2, y: 2, z: 4, core: 2. Of those that a mesh axis runs over, the one named last changes fastest.
Arguments:
- inputs: bfloat16 [2, 16, 256, 768], P(None, 'dp'), may hold values from -6 to 6
- cotangent: bfloat16 [2, 16, 256, 768], P(None, 'dp'), may hold values from -6 to 6
- lengths: int32 [2, 16], P(None, 'dp'), may hold values from 1 to 256, 3072 in all within a row
- norm_one_gain: bfloat16 [2, 768], P('section', 'dp'), may hold values from 0.5 to 1.5
- norm_one_bias: bfloat16 [2, 768], P('section', 'dp'), may hold values from -1.75 to 1.75
- query_key_weight: bfloat16 [2, 768, 1536], P('section', 'dp'), may hold values from -0.21875 to 0.21875
- value_weight: bfloat16 [2, 768, 384], P('section', 'dp'), may hold values from -0.21875 to 0.21875
- out_weight: bfloat16 [2, 768, 768], P('section', 'dp'), may hold values from -1.75 to 1.75
- norm_two_gain: bfloat16 [2, 768], P('section', 'dp'), may hold values from 0.5 to 1.5
- norm_two_bias: bfloat16 [2, 768], P('section', 'dp'), may hold values from -1.75 to 1.75
- up_weight: bfloat16 [2, 768, 3072], P('section', 'dp'), may hold values from -0.21875 to 0.21875
- down_weight: bfloat16 [2, 3072, 768], P('section', 'dp'), may hold values from -0.109375 to 0.109375
- first_value_weight: bfloat16 [768, 384], P('dp', 'section'), may hold values from -0.21875 to 0.21875
Outputs:
- layer_outputs: bfloat16 [2, 2, 16, 256, 768], P('section', None, 'dp')
- layer_input_grads: bfloat16 [2, 2, 16, 256, 768], P('section', None, 'dp')
- norm_one_gain_grad: float32 [2, 768], P('section', 'dp')
- norm_one_bias_grad: float32 [2, 768], P('section', 'dp')
- query_key_weight_grad: float32 [2, 768, 1536], P('section', 'dp')
- value_weight_grad: float32 [2, 768, 384], P('section', 'dp')
- out_weight_grad: float32 [2, 768, 768], P('section', 'dp')
- norm_two_gain_grad: float32 [2, 768], P('section', 'dp')
- norm_two_bias_grad: float32 [2, 768], P('section', 'dp')
- up_weight_grad: float32 [2, 768, 3072], P('section', 'dp')
- down_weight_grad: float32 [2, 3072, 768], P('section', 'dp')
- first_value_grad: float32 [768, 384], P('dp', 'section')
The draws below stay inside these ranges and needn't reach their ends.
Inputs may be any that keep to these rules, and one draw needn't show every extreme that they name: In each micro-batch the 16 lengths sum to 3072, and one of them is exactly 256.
All inputs are finite; a program needn't handle non-finite values. No bound on the sum of `lengths` on one device may be relied on, other than what follows from the above.
Results may differ from the reference program's by a relative error of at most 0.02.
Values may be sent and summed in bfloat16 or wider, within the bound.
A program may use at most 192 MiB of HBM per device.

```python
import math
import jax
import jax.numpy as jnp
import numpy as np
from jax import lax

D = 768
HEADS = 12
HD = 64
FF = 3072
MB = 2
LEN = 256
HALF = 384
SEQS = 16


def spiked(values, rng, source, target, parts, factor):
    def block_of(axis_at):
        return (jnp.arange(values.shape[axis_at]) // (values.shape[axis_at] // parts)).reshape((-1,) + (1,) * (values.ndim - 1 - axis_at))

    first = jax.random.permutation(rng, parts)[block_of(target)]
    second = (block_of(target) + parts // 2) % parts
    return jnp.where((block_of(source) == first) | (block_of(source) == second), factor * values, values)


def level_of(rng, extent, cuts, low, high):
    loudness = 1.0
    for dim, parts in cuts:
        draws = jax.random.uniform(jax.random.fold_in(jax.random.fold_in(rng, 6), dim), (parts,), jnp.float32, low / len(cuts), high / len(cuts))
        loudness = loudness * jnp.repeat(jnp.exp(draws), extent[dim] // parts).reshape((-1,) + (1,) * (len(extent) - 1 - dim))
    return loudness


def profile(number_of, total, most, lean):
    loads = [(1 << 20) // math.isqrt(rank ** lean) + 1 for rank in range(2, number_of + 1)]
    spare, holding = total - most - (number_of - 1), [1] * (number_of - 1)
    while spare > 0:
        movable = [i for i in range(number_of - 1) if holding[i] < most]
        mass, left = sum([loads[i] for i in movable]), spare
        for i in movable:
            more = min(most - holding[i], max(1, left * loads[i] // mass), spare)
            holding[i] = holding[i] + more
            spare = spare - more
    return np.array([most] + holding)


def ragged(key, number_of, total, bound, skew):
    if number_of == 2:
        one = jax.random.randint(key, (), max(1, total - bound), min(bound, total - 1) + 1)
        return jnp.stack([one, total - one])
    tallies = jnp.asarray(profile(number_of, total, bound, skew), jnp.int32)
    twos = (number_of - 1) // 2
    donor, sink = tallies[1:1 + 2 * twos:2], tallies[2:2 + 2 * twos:2]
    room = jnp.minimum(donor - 1, bound - sink)
    moved = jax.random.randint(jax.random.fold_in(key, 1), (twos,), 0, 1 << 20) % (room + 1)
    tallies = tallies.at[1:1 + 2 * twos:2].set(donor - moved).at[2:2 + 2 * twos:2].set(sink + moved)
    return tallies[jax.random.permutation(jax.random.fold_in(key, 2), number_of)]


def gaussian(rng, shape, spread, reach, cuts=(), dtype=jnp.bfloat16):
    factor_of = level_of(rng, shape, cuts, -0.22, 0.18) if cuts else 1.0
    result = jax.random.normal(rng, shape, jnp.float32) * spread * factor_of
    return jnp.minimum(jnp.maximum(result, -reach), reach).astype(dtype)


def noise_with(own_key, extent, deviation, limit, shards, heavy, held_as=jnp.bfloat16):
    drawn = deviation * jax.random.normal(own_key, extent, jnp.float32)
    if shards:
        drawn = drawn * level_of(own_key, extent, shards, -0.22, 0.18)
    return jnp.clip(spiked(drawn, jax.random.fold_in(own_key, 3), *heavy), -limit, limit).astype(held_as)


def setup_inputs(seed: int = 0) -> dict:
    key_list = jax.random.split(jax.random.key(seed), 14)
    inputs = noise_with(key_list[0], (MB, SEQS, LEN, D), 1.0, 6.0, ((1, 16),), (1, 3, 16, 2.0))
    cotangent = gaussian(key_list[1], (MB, SEQS, LEN, D), 1.0, 6.0, ((1, 16),))
    lengths = jax.vmap(lambda own: ragged(own, SEQS, SEQS * LEN * 3 // 4, LEN, 2))(jax.random.split(key_list[2], MB)).reshape((MB, SEQS)).astype(jnp.int32)
    norm_one_gain = jnp.clip(1.0 + 0.1 * jax.random.normal(key_list[3], (2, D), jnp.float32), 0.5, 1.5).astype(jnp.bfloat16)
    norm_one_bias = gaussian(key_list[4], (2, D), 0.3, 1.75, ((0, 2), (1, 16)))
    query_key_weight = gaussian(key_list[5], (2, D, 2 * D), D ** -0.5, 0.21875, ((0, 2), (1, 16)))
    value_weight = gaussian(key_list[6], (2, D, HALF), D ** -0.5, 0.21875, ((0, 2), (1, 16)))
    out_weight = gaussian(key_list[7], (2, D, D), (D * 4 // LEN) ** -0.5, 1.75, ((0, 2), (1, 16)))
    norm_two_gain = jnp.clip(1.0 + 0.1 * jax.random.normal(key_list[8], (2, D), jnp.float32), 0.5, 1.5).astype(jnp.bfloat16)
    norm_two_bias = gaussian(key_list[9], (2, D), 0.3, 1.75, ((0, 2), (1, 16)))
    up_weight = gaussian(key_list[10], (2, D, FF), D ** -0.5, 0.21875, ((0, 2), (1, 16)))
    down_weight = gaussian(key_list[11], (2, FF, D), FF ** -0.5, 0.109375, ((0, 2), (1, 16)))
    first_value_weight = gaussian(key_list[12], (D, HALF), D ** -0.5, 0.21875, ((0, 16), (1, 2)))
    return {"inputs": inputs, "cotangent": cotangent, "lengths": lengths, "norm_one_gain": norm_one_gain, "norm_one_bias": norm_one_bias, "query_key_weight": query_key_weight, "value_weight": value_weight, "out_weight": out_weight, "norm_two_gain": norm_two_gain, "norm_two_bias": norm_two_bias, "up_weight": up_weight, "down_weight": down_weight, "first_value_weight": first_value_weight}


@jax.custom_vjp
def low(v):
    return lax.optimization_barrier(v.astype(jnp.bfloat16)).astype(jnp.float32)

@jax.custom_vjp
def low_back(v):
    return v

def low_keep(v):
    return (low(v), None)

def low_pass(kept, grad):
    return (grad,)

def back_keep(v):
    return (v, None)

def back_low(kept, grad):
    return (low(grad),)
low.defvjp(low_keep, low_pass)
low_back.defvjp(back_keep, back_low)
highest = lax.Precision.HIGHEST
epsilon = 1e-05

def layer_norm(hidden, norm_gain, norm_bias):
    average = lax.optimization_barrier(jnp.mean(hidden, axis=-1, keepdims=True))
    centred = hidden - average
    variance = lax.optimization_barrier(jnp.mean(centred * centred, axis=-1, keepdims=True))
    return centred * lax.rsqrt(variance + epsilon) * norm_gain + norm_bias

def project(left_side, right_side):
    return jnp.matmul(left_side, right_side, precision=highest)

def attend(queries, key_rows, values, lengths):
    positions = queries.shape[1]
    scores = jnp.einsum('gqhd,gkhd->ghqk', queries, key_rows, precision=highest) * HD ** (-0.5)
    scores = low_back(scores)
    places = jnp.arange(positions)
    causal = places[None, :] <= places[:, None]
    live = places[None, :] < lengths[:, None]
    allowed = causal[None, None, :, :] & live[:, None, None, :]
    scores = jnp.where(allowed, scores, -1e+30)
    soft_weights = low(jax.nn.softmax(scores, axis=-1))
    return jnp.einsum('ghqk,gkhd->gqhd', soft_weights, values, precision=highest)

def residual_block(hidden, parameters, shared, lengths, first_layer):
    one_gain, one_bias, query_key, value_matrix, output_matrix, two_gain, two_bias, up_matrix, down_matrix, first_matrix = parameters
    groups, positions, features = hidden.shape
    normed = low(layer_norm(hidden, one_gain, one_bias))
    query_rows = low_back(low(project(normed, query_key)))
    fresh_values = low_back(low(project(normed, value_matrix)))
    if first_layer:
        shared = low_back(low(project(normed, first_matrix)))
        handed = low_back(shared)
    else:
        handed = shared
    values = jnp.concatenate([fresh_values, shared], axis=-1).reshape(groups, positions, HEADS, HD)
    split_rows = query_rows.reshape(groups, positions, 2, HEADS, HD)
    attended = attend(split_rows[:, :, 0], split_rows[:, :, 1], values, lengths)
    attended = low_back(low(attended.reshape(groups, positions, features)))
    middle = hidden + low_back(project(attended, output_matrix))
    mixed_rows = low(layer_norm(middle, two_gain, two_bias))
    upper_rows = low_back(project(mixed_rows, up_matrix))
    active = low(jax.nn.gelu(upper_rows, approximate=True))
    return (middle + low_back(project(active, down_matrix)), handed)

def forward(stacked, first_matrix, entering, probe, lengths):
    micro_count, total, positions, features = entering.shape
    group_size = math.gcd(micro_count * total, max(1, 4096 // positions))
    count_groups = micro_count * total // group_size
    layer_one = tuple((array[0] for array in stacked)) + (first_matrix,)
    layer_two = tuple((array[1] for array in stacked)) + (first_matrix,)

    def group_pass(pieces):
        group_input, group_probe, group_lengths = pieces
        first_out, shared = residual_block(group_input, layer_one, None, group_lengths, True)
        sent = low_back(low(first_out) + group_probe)
        second_out, unused = residual_block(sent, layer_two, shared, group_lengths, False)
        return (first_out, second_out)
    shape_groups = (count_groups, group_size, positions, features)
    first_all, second_all = lax.map(jax.checkpoint(group_pass), (entering.reshape(shape_groups), probe.reshape(shape_groups), lengths.reshape(count_groups, group_size)))
    return (first_all.reshape(entering.shape), second_all.reshape(entering.shape))

def reference(inputs, cotangent, lengths, norm_one_gain, norm_one_bias, query_key_weight, value_weight, out_weight, norm_two_gain, norm_two_bias, up_weight, down_weight, first_value_weight):
    stacked = tuple((array.astype(jnp.float32) for array in (norm_one_gain, norm_one_bias, query_key_weight, value_weight, out_weight, norm_two_gain, norm_two_bias, up_weight, down_weight)))
    first_matrix = first_value_weight.astype(jnp.float32)
    entering = inputs.astype(jnp.float32)
    probe = jnp.zeros_like(entering)

    def whole_pass(stacked_arrays, first_values, entering_values, probe_values):
        return forward(stacked_arrays, first_values, entering_values, probe_values, lengths)
    (first_all, second_all), pullback = jax.vjp(whole_pass, stacked, first_matrix, entering, probe)
    places = jnp.arange(LEN)
    live = (places[None, None, :] < lengths[:, :, None]).astype(jnp.float32)
    seed_grad = cotangent.astype(jnp.float32) * live[..., None]
    stacked_grads, first_grad, input_grad, probe_grad = pullback((jnp.zeros_like(first_all), seed_grad))
    layer_outputs = jnp.stack([first_all, second_all]).astype(jnp.bfloat16)
    layer_input_grads = jnp.stack([input_grad, probe_grad]).astype(jnp.bfloat16)
    return (layer_outputs, layer_input_grads, stacked_grads[0], stacked_grads[1], stacked_grads[2], stacked_grads[3], stacked_grads[4], stacked_grads[5], stacked_grads[6], stacked_grads[7], stacked_grads[8], first_grad)
```

```python
import functools

import jax
import jax.numpy as jnp
from jax import lax
from jax.experimental import pallas as pl
from jax.experimental.pallas import tpu as pltpu
from jax.sharding import PartitionSpec as P

HEADS = 12
HD = 64
EPSILON = 1e-05
BF = jnp.bfloat16
F32 = jnp.float32
MESH = pl.DeviceIdType.MESH

GROUPS = ("zxy", "zyx", "yzx", "xzy")
ARRIVALS = (
    0, 1000, 2000, 3000, 1, 100, 10, 1001, 1010, 1100, 2010, 2001, 2100, 2, 1002, 3100, 3001,
    3010, 101, 2002, 11, 110, 1110, 1101, 2011, 1011, 3002, 102, 12, 3, 1102, 3101, 1003,
    1012, 2110, 2101, 3110, 3011, 2003, 2012, 2102, 111, 3012, 112, 1111, 2111, 103, 3003,
    3102, 13, 1103, 1013, 3111, 1112, 2013, 3103, 2103, 2112, 113, 3013, 3112, 1113, 2113,
    3113,
)
EVENTS = [(n // 1000, n // 100 % 10, n // 10 % 10, n % 10) for n in ARRIVALS]


class Place:
    def __init__(self):
        self.s = lax.axis_index("section")
        dp = lax.axis_index("dp")
        self.z = dp // 4
        self.y = (dp // 2) % 2
        self.c = dp % 2
        self.mid = (self.z == 1) | (self.z == 2)

    def device(self, s, z, y, c):
        return (s, z * 4 + y * 2 + c)

    def neighbour(self, link):
        s, z, y, c = self.s, self.z, self.y, self.c
        if link == "x":
            return self.device(1 - s, z, y, c)
        if link == "y":
            return self.device(s, z, 1 - y, c)
        if link == "near":
            return self.device(s, z + 1 - 2 * (z % 2), y, c)
        if link == "far":
            return self.device(s, 3 - z, y, c)
        return self.device(s, z, y, 1 - c)

    def along_z(self, j):
        z = self.z
        return (z, z + 1 - 2 * (z % 2), 2 - z // 2, 3 - 3 * (z // 2))[j]

    def layer(self, rx):
        return self.s if rx == 0 else 1 - self.s

    def block(self, ry, j):
        y = self.y if ry == 0 else 1 - self.y
        return self.along_z(j) * 2 + y


def branches(order, rx, ry, j):
    apart = {"x": rx != 0, "y": ry != 0, "z": j != 0}
    last = max([i for i, axis in enumerate(order) if apart[axis]], default=-1)
    links = []
    for i, axis in enumerate(order):
        if i < last:
            continue
        if axis != "z":
            if i > last:
                links.append((axis, False))
        elif i > last:
            links += [("near", False), ("far", True)]
        else:
            links.append(("far" if j == 1 else "near", True))
    return links


def guarded(place, middle_only, action):
    if middle_only:
        pl.when(place.mid)(action)
    else:
        action()


def greet(place):
    barrier = pltpu.get_barrier_semaphore()
    for link in ("x", "y", "near", "core"):
        pl.semaphore_signal(barrier, 1, device_id=place.neighbour(link), device_id_type=MESH)

    @pl.when(place.mid)
    def _():
        pl.semaphore_signal(barrier, 1, device_id=place.neighbour("far"), device_id_type=MESH)
        pl.semaphore_wait(barrier, 5)

    @pl.when(jnp.logical_not(place.mid))
    def _():
        pl.semaphore_wait(barrier, 4)


def gather_kernel(rows, *refs):
    own, whole = refs[:4], refs[4:8]
    send_sem, recv_sem, core_sem, local_sem = refs[8:]
    place = Place()
    greet(place)

    def part(g, rx, ry, j, core):
        layer, block = place.layer(rx), place.block(ry, j)
        start = pl.multiple_of((block * 2 + core) * rows[g], rows[g])
        return whole[g].at[layer, pl.ds(start, rows[g])], layer, block

    def copy(k, event, link):
        g, rx, ry, j = event
        target, layer, block = part(g, rx, ry, j, place.c)
        source = own[g] if (rx, ry, j) == (0, 0, 0) else target
        index = ("x", "y", "near", "far", "core").index(link)
        sems = core_sem if link == "core" else recv_sem
        return pltpu.make_async_remote_copy(
            src_ref=source,
            dst_ref=target,
            send_sem=send_sem.at[k, index],
            recv_sem=sems.at[g, layer, block],
            device_id=place.neighbour(link),
            device_id_type=MESH,
        )

    locals_ = [
        pltpu.make_async_copy(own[g], part(g, 0, 0, 0, place.c)[0], local_sem.at[g])
        for g in range(4)
    ]
    for k, event in enumerate(EVENTS):
        g, rx, ry, j = event
        if (rx, ry, j) != (0, 0, 0):
            pltpu.make_async_remote_copy(
                src_ref=part(g, rx, ry, j, place.c)[0],
                dst_ref=part(g, rx, ry, j, place.c)[0],
                send_sem=send_sem.at[k, 0],
                recv_sem=recv_sem.at[g, place.layer(rx), place.block(ry, j)],
                device_id=place.neighbour("x"),
                device_id_type=MESH,
            ).wait_recv()
        for link, middle_only in branches(GROUPS[g], rx, ry, j):
            guarded(place, middle_only, lambda: copy(k, event, link).start())
        copy(k, event, "core").start()
    for one in locals_:
        one.start()
    for k, event in enumerate(EVENTS):
        g, rx, ry, j = event
        for link, middle_only in branches(GROUPS[g], rx, ry, j):
            guarded(place, middle_only, lambda: copy(k, event, link).wait_send())
        mine = copy(k, event, "core")
        mine.wait_send()
        other, layer, block = part(g, rx, ry, j, 1 - place.c)
        pltpu.make_async_remote_copy(
            src_ref=other,
            dst_ref=other,
            send_sem=send_sem.at[k, 0],
            recv_sem=core_sem.at[g, layer, block],
            device_id=place.neighbour("core"),
            device_id_type=MESH,
        ).wait_recv()
    for one in locals_:
        one.wait()


def gather_by_kernel(blocks):
    rows = tuple(block.shape[0] for block in blocks)
    return pl.pallas_call(
        functools.partial(gather_kernel, rows),
        out_shape=[
            jax.ShapeDtypeStruct((2, 16 * block.shape[0], block.shape[1]), BF) for block in blocks
        ],
        in_specs=[pl.BlockSpec(memory_space=pl.ANY)] * 4,
        out_specs=[pl.BlockSpec(memory_space=pl.ANY)] * 4,
        scratch_shapes=[
            pltpu.SemaphoreType.DMA((len(EVENTS), 5)),
            pltpu.SemaphoreType.DMA((4, 2, 8)),
            pltpu.SemaphoreType.DMA((4, 2, 8)),
            pltpu.SemaphoreType.DMA((4,)),
        ],
        compiler_params=pltpu.CompilerParams(collective_id=0, has_side_effects=True),
    )(*blocks)


def scatter_layout():
    slots, counts = {}, [0, 0, 0, 0]
    for g, rx, ry, j in EVENTS:
        for link, _ in branches(GROUPS[g], rx, ry, j):
            slots[g, rx, ry, j, link] = counts[g]
            counts[g] += 1
    return slots, counts


def add_rows(target, sources, rows):
    @pl.loop(0, rows // 16)
    def _(i):
        at = pl.ds(pl.multiple_of(i * 16, 16), 16)
        total = sources[0][at, :].astype(F32)
        for source in sources[1:]:
            total = total + source[at, :].astype(F32)
        target[at, :] = total.astype(target.dtype)


def scatter_kernel(rows, slots, *refs):
    partial = refs[:8]
    result = refs[8:12]
    held, from_core, arrived, summed = refs[12:16], refs[16:20], refs[20:24], refs[24:28]
    load_sem, core_send, core_recv, send_sem, recv_sem, out_sem = refs[28:]
    place = Place()
    greet(place)
    order = EVENTS[::-1]
    number = {event: k for k, event in enumerate(EVENTS)}

    def per_layer(event, action):
        g, rx, ry, j = event
        for layer in range(2):
            pl.when(place.layer(rx) == layer)(lambda: action(partial[2 * g + layer]))

    def slab(ref, event, core):
        g, rx, ry, j = event
        start = pl.multiple_of((place.block(ry, j) * 2 + core) * rows[g], rows[g])
        return ref.at[pl.ds(start, rows[g])]

    def slot_of(event):
        g, rx, ry, j = event
        return rx * 8 + ry * 4 + j

    def load(event, ref):
        g = event[0]
        return pltpu.make_async_copy(
            slab(ref, event, place.c), held[g].at[slot_of(event)], load_sem.at[number[event]]
        )

    def hand_over(event, ref):
        g = event[0]
        return pltpu.make_async_remote_copy(
            src_ref=slab(ref, event, 1 - place.c),
            dst_ref=from_core[g].at[slot_of(event)],
            send_sem=core_send.at[number[event]],
            recv_sem=core_recv.at[number[event]],
            device_id=place.neighbour("core"),
            device_id_type=MESH,
        )

    def parent(event):
        g, rx, ry, j = event
        apart = {"x": rx != 0, "y": ry != 0, "z": j != 0}
        axis = [axis for axis in GROUPS[g] if apart[axis]][-1]
        return axis

    def send(event, link, there):
        g, rx, ry, j = event
        return pltpu.make_async_remote_copy(
            src_ref=held[g].at[slot_of(event)],
            dst_ref=arrived[g].at[slots[there + (link,)]],
            send_sem=send_sem.at[number[event]],
            recv_sem=recv_sem.at[g, slots[there + (link,)]],
            device_id=place.neighbour(link),
            device_id_type=MESH,
        )

    def sends(event):
        g, rx, ry, j = event
        axis = parent(event)
        if axis == "x":
            return [(None, "x", (g, 0, ry, j))]
        if axis == "y":
            return [(None, "y", (g, rx, 0, j))]
        ends = jnp.logical_not(place.mid)
        if j == 1:
            return [(None, "near", (g, rx, ry, 0))]
        if j == 2:
            return [
                (place.mid, "far", (g, rx, ry, 0)),
                (ends, "near", (g, rx, ry, 2)),
            ]
        return [(place.mid, "far", (g, rx, ry, 1)), (ends, "near", (g, rx, ry, 3))]

    for event in order:
        per_layer(event, lambda ref: hand_over(event, ref).start())
        per_layer(event, lambda ref: load(event, ref).start())

    for event in order:
        g, rx, ry, j = event
        first = partial[2 * g]
        load(event, first).wait()
        hand_over(event, first).wait_recv()
        links = branches(GROUPS[g], rx, ry, j)
        for link, middle_only in links:
            guarded(
                place,
                middle_only,
                lambda: pltpu.make_async_remote_copy(
                    src_ref=held[g].at[0],
                    dst_ref=arrived[g].at[slots[event + (link,)]],
                    send_sem=send_sem.at[0],
                    recv_sem=recv_sem.at[g, slots[event + (link,)]],
                    device_id=place.neighbour(link),
                    device_id_type=MESH,
                ).wait_recv(),
            )
        mine = held[g].at[slot_of(event)]
        always = [mine, from_core[g].at[slot_of(event)]]
        always += [arrived[g].at[slots[event + (link,)]] for link, middle in links if not middle]
        extra = [arrived[g].at[slots[event + (link,)]] for link, middle in links if middle]
        final = (rx, ry, j) == (0, 0, 0)
        target = summed[g] if final else mine
        if extra:
            pl.when(place.mid)(lambda: add_rows(target, always + extra, rows[g]))
            pl.when(jnp.logical_not(place.mid))(lambda: add_rows(target, always, rows[g]))
        else:
            add_rows(target, always, rows[g])
        if final:
            pltpu.make_async_copy(summed[g], result[g], out_sem.at[g]).start()
        else:
            for condition, link, there in sends(event):
                if condition is None:
                    send(event, link, there).start()
                else:
                    pl.when(condition)(lambda: send(event, link, there).start())

    for event in order:
        g, rx, ry, j = event
        hand_over(event, partial[2 * g]).wait_send()
        if (rx, ry, j) == (0, 0, 0):
            pltpu.make_async_copy(summed[g], result[g], out_sem.at[g]).wait()
        else:
            send(event, *sends(event)[0][1:]).wait_send()


def scatter_by_kernel(partials):
    rows = tuple(pair[0].shape[0] // 16 for pair in partials)
    widths = tuple(pair[0].shape[1] for pair in partials)
    slots, counts = scatter_layout()
    blocks = list(zip(rows, widths))
    return pl.pallas_call(
        functools.partial(scatter_kernel, rows, slots),
        out_shape=[jax.ShapeDtypeStruct(block, F32) for block in blocks],
        in_specs=[pl.BlockSpec(memory_space=pl.ANY)] * 8,
        out_specs=[pl.BlockSpec(memory_space=pl.ANY)] * 4,
        scratch_shapes=[pltpu.VMEM((16,) + block, BF) for block in blocks]
        + [pltpu.VMEM((16,) + block, BF) for block in blocks]
        + [pltpu.VMEM((count,) + block, BF) for count, block in zip(counts, blocks)]
        + [pltpu.VMEM(block, F32) for block in blocks]
        + [
            pltpu.SemaphoreType.DMA((len(EVENTS),)),
            pltpu.SemaphoreType.DMA((len(EVENTS),)),
            pltpu.SemaphoreType.DMA((len(EVENTS),)),
            pltpu.SemaphoreType.DMA((len(EVENTS),)),
            pltpu.SemaphoreType.DMA((4, max(counts))),
            pltpu.SemaphoreType.DMA((4,)),
        ],
        compiler_params=pltpu.CompilerParams(
            collective_id=1, has_side_effects=True, vmem_limit_bytes=60 * 2**20
        ),
    )(*[half for pair in partials for half in pair])


def gather(blocks, by_kernel):
    if by_kernel:
        return gather_by_kernel(blocks)
    return [
        lax.all_gather(lax.all_gather(block, "dp", axis=0, tiled=True), "section", axis=0)
        for block in blocks
    ]


def scatter(partials, by_kernel):
    if by_kernel:
        return scatter_by_kernel(partials)
    results = []
    for pair in partials:
        both = lax.psum_scatter(jnp.stack(pair), "section", scatter_dimension=0, tiled=False)
        results.append(
            lax.psum_scatter(both.astype(F32), "dp", scatter_dimension=0, tiled=True)
        )
    return results


def normalized(rows):
    average = jnp.mean(rows, axis=-1, keepdims=True)
    centred = rows - average
    scale = lax.rsqrt(jnp.mean(centred * centred, axis=-1, keepdims=True) + EPSILON)
    return centred * scale, scale


def norm_back(grad, unit, scale, gain):
    scaled = grad * gain
    inner = scaled - jnp.mean(scaled, axis=-1, keepdims=True)
    inner = inner - unit * jnp.mean(scaled * unit, axis=-1, keepdims=True)
    return jnp.sum(grad * unit, axis=0), jnp.sum(grad, axis=0), scale * inner


def product(left, right):
    return jnp.dot(left, right, preferred_element_type=F32)


def outer_sum(left, right):
    return lax.dot_general(left, right, (((0,), (0,)), ((), ())), preferred_element_type=F32)


def times_transposed(left, right):
    return lax.dot_general(left, right, (((1,), (1,)), ((), ())), preferred_element_type=F32)


def by_head(rows):
    return rows.reshape(rows.shape[0], -1, HD)


def forward(hidden, weights, shared, allowed):
    query_key, value, out, up, down, first, norms = weights
    unit_one, scale_one = normalized(hidden)
    normed = (unit_one * norms[0] + norms[1]).astype(BF)
    qk = product(normed, query_key).astype(BF)
    fresh = product(normed, value).astype(BF)
    if shared is None:
        shared = product(normed, first).astype(BF)
    features = hidden.shape[1]
    queries, keys = by_head(qk[:, :features]), by_head(qk[:, features:])
    values = by_head(jnp.concatenate([fresh, shared], axis=1))
    scores = jnp.einsum("qhd,khd->hqk", queries, keys, preferred_element_type=F32) * HD**-0.5
    scores = jnp.where(allowed, scores, -1e30)
    raised = jnp.exp(scores - jnp.max(scores, axis=-1, keepdims=True))
    soft = raised / jnp.sum(raised, axis=-1, keepdims=True)
    probs = soft.astype(BF)
    attended = jnp.einsum("hqk,khd->qhd", probs, values, preferred_element_type=F32)
    attended = attended.reshape(hidden.shape).astype(BF)
    middle = hidden + product(attended, out)
    unit_two, scale_two = normalized(middle)
    mixed = (unit_two * norms[2] + norms[3]).astype(BF)
    upper = product(mixed, up)
    active = jax.nn.gelu(upper, approximate=True).astype(BF)
    output = middle + product(active, down)
    kept = (normed, queries, keys, values, soft, attended, unit_one, scale_one)
    return output, shared, kept + (unit_two, scale_two, mixed, upper, active)


def backward(grad, weights, kept, grad_shared_next):
    query_key, value, out, up, down, first, norms = weights
    normed, queries, keys, values, soft, attended, unit_one, scale_one = kept[:8]
    unit_two, scale_two, mixed, upper, active = kept[8:]
    positions, features = grad.shape
    half = value.shape[1]
    grad_low = grad.astype(BF)
    down_grad = outer_sum(active, grad_low)
    _, gelu_pull = jax.vjp(lambda u: jax.nn.gelu(u, approximate=True), upper)
    grad_upper = gelu_pull(times_transposed(grad_low, down))[0].astype(BF)
    up_grad = outer_sum(mixed, grad_upper)
    grad_mixed = times_transposed(grad_upper, up)
    two_gain, two_bias, through = norm_back(grad_mixed, unit_two, scale_two, norms[2])
    grad_middle = grad + through
    grad_attn = grad_middle.astype(BF)
    out_grad = outer_sum(attended, grad_attn)
    grad_attended = by_head(times_transposed(grad_attn, out).astype(BF))
    grad_soft = jnp.einsum("qhd,khd->hqk", grad_attended, values, preferred_element_type=F32)
    grad_values = jnp.einsum(
        "hqk,qhd->khd", soft.astype(BF), grad_attended, preferred_element_type=F32
    ).reshape(positions, features)
    grad_scores = soft * (grad_soft - jnp.sum(soft * grad_soft, axis=-1, keepdims=True))
    grad_scores = grad_scores.astype(BF)
    grad_queries = jnp.einsum("hqk,khd->qhd", grad_scores, keys, preferred_element_type=F32)
    grad_keys = jnp.einsum("hqk,qhd->khd", grad_scores, queries, preferred_element_type=F32)
    grad_qk = jnp.concatenate(
        [grad_queries.reshape(positions, features), grad_keys.reshape(positions, features)], axis=1
    )
    grad_qk = (grad_qk * HD**-0.5).astype(BF)
    grad_fresh = grad_values[:, :half].astype(BF)
    grad_shared = grad_values[:, half:]
    grad_normed = times_transposed(grad_qk, query_key) + times_transposed(grad_fresh, value)
    if grad_shared_next is not None:
        grad_shared = (grad_shared + grad_shared_next.astype(F32)).astype(BF)
        first_grad = outer_sum(normed, grad_shared)
        grad_normed = grad_normed + times_transposed(grad_shared, first)
    else:
        grad_shared = grad_shared.astype(BF)
        first_grad = None
    one_gain, one_bias, through = norm_back(grad_normed, unit_one, scale_one, norms[0])
    grad_input = (grad_middle + through).astype(BF)
    query_key_grad = outer_sum(normed, grad_qk)
    value_grad = outer_sum(normed, grad_fresh)
    gains = jnp.stack([one_gain, one_bias, two_gain, two_bias], axis=1)
    return grad_input, grad_shared, (
        query_key_grad, value_grad, out_grad, up_grad, down_grad, first_grad, gains
    )


def swapped(block):
    return lax.ppermute(block, "section", [(0, 1), (1, 0)])


def on_device(
    by_kernel,
    inputs,
    cotangent,
    lengths,
    norm_one_gain,
    norm_one_bias,
    query_key_weight,
    value_weight,
    out_weight,
    norm_two_gain,
    norm_two_bias,
    up_weight,
    down_weight,
    first_value_weight,
):
    section = lax.axis_index("section")
    first_half = section == 0
    half = value_weight.shape[2]
    features = out_weight.shape[2]
    quarter = first_value_weight.shape[1]
    own_rows = query_key_weight.shape[1]
    norms = jnp.stack([norm_one_gain[0], norm_one_bias[0], norm_two_gain[0], norm_two_bias[0]], axis=1)
    padding = -(half + features + quarter + 4) % 128
    attention = jnp.concatenate(
        [
            value_weight[0],
            out_weight[0],
            first_value_weight,
            norms,
            jnp.zeros((own_rows, padding), BF),
        ],
        axis=1,
    )
    whole = gather([query_key_weight[0], attention, up_weight[0], down_weight[0]], by_kernel)
    after = half + features
    first_matrix = jnp.concatenate(
        [whole[1][0, :, after : after + quarter], whole[1][1, :, after : after + quarter]], axis=1
    )

    def layer_weights(layer):
        packed = whole[1][layer]
        gains = packed[:, after + quarter : after + quarter + 4].astype(F32).T
        return (
            whole[0][layer],
            packed[:, :half],
            packed[:, half:after],
            whole[2][layer],
            whole[3][layer],
            first_matrix,
            gains,
        )

    weights = [layer_weights(0), layer_weights(1)]
    batch_sequences, positions = inputs.shape[1:3]
    hidden = lax.dynamic_index_in_dim(inputs, section, 0, keepdims=False)[0]
    grad = lax.dynamic_index_in_dim(cotangent, section, 0, keepdims=False)[0]
    length = lax.dynamic_index_in_dim(lengths, section, 0, keepdims=False)[0]
    places = jnp.arange(positions)
    live = places < length
    allowed = (places[None, :] <= places[:, None]) & live[None, :]
    output_one, shared, kept_one = forward(hidden.astype(F32), weights[0], None, allowed)
    low_one = output_one.astype(BF)
    output_two, _, kept_two = forward(low_one.astype(F32), weights[1], shared, allowed)
    low_two = output_two.astype(BF)
    outputs_there = swapped(jnp.where(first_half, low_two, low_one))
    outputs_here = jnp.where(first_half, low_one, low_two)
    grad = jnp.where(live[:, None], grad.astype(F32), 0.0)
    grad_one, grad_shared, sums_two = backward(grad, weights[1], kept_two, None)
    grad_zero, _, sums_one = backward(grad_one.astype(F32), weights[0], kept_one, grad_shared)
    grads_there = swapped(jnp.where(first_half, grad_one, grad_zero))
    grads_here = jnp.where(first_half, grad_zero, grad_one)
    first_grad = sums_one[5]

    def packed_sums(sums, first_part):
        return jnp.concatenate(
            [
                sums[1],
                sums[2],
                first_part,
                sums[6],
                jnp.zeros((first_part.shape[0], padding), F32),
            ],
            axis=1,
        ).astype(BF)

    partials = [
        (sums_one[0].astype(BF), sums_two[0].astype(BF)),
        (
            packed_sums(sums_one, first_grad[:, :quarter]),
            packed_sums(sums_two, first_grad[:, quarter:]),
        ),
        (sums_one[3].astype(BF), sums_two[3].astype(BF)),
        (sums_one[4].astype(BF), sums_two[4].astype(BF)),
    ]
    query_key_grad, packed_grad, up_grad, down_grad = scatter(partials, by_kernel)
    gains = packed_grad[:, after + quarter : after + quarter + 4].T

    def both(here, there):
        return jnp.stack(
            [jnp.where(first_half, here, there), jnp.where(first_half, there, here)]
        )[None, :, None]

    return (
        both(outputs_here, outputs_there),
        both(grads_here, grads_there),
        gains[0][None],
        gains[1][None],
        query_key_grad[None],
        packed_grad[:, :half][None],
        packed_grad[:, half:after][None],
        gains[2][None],
        gains[3][None],
        up_grad[None],
        down_grad[None],
        packed_grad[:, after : after + quarter],
    )


def solution(mesh):
    placed = (
        P(None, "dp", None, None),
        P(None, "dp", None, None),
        P(None, "dp"),
        P("section", "dp"),
        P("section", "dp"),
        P("section", "dp", None),
        P("section", "dp", None),
        P("section", "dp", None),
        P("section", "dp"),
        P("section", "dp"),
        P("section", "dp", None),
        P("section", "dp", None),
        P("dp", "section"),
    )
    by_kernel = mesh.shape["dp"] == 16 and mesh.shape["section"] == 2
    return jax.shard_map(
        functools.partial(on_device, by_kernel),
        mesh=mesh,
        in_specs=placed,
        out_specs=(
            P("section", None, "dp", None, None),
            P("section", None, "dp", None, None),
            P("section", "dp"),
            P("section", "dp"),
            P("section", "dp", None),
            P("section", "dp", None),
            P("section", "dp", None),
            P("section", "dp"),
            P("section", "dp"),
            P("section", "dp", None),
            P("section", "dp", None),
            P("dp", "section"),
        ),
        check_vma=False,
    )
```

```python
import functools

import jax
import jax.numpy as jnp
from jax import lax
from jax.experimental import pallas as pl
from jax.experimental.pallas import tpu as pltpu
from jax.sharding import PartitionSpec as P

HEADS = 12
HD = 64
EPSILON = 1e-05
BF = jnp.bfloat16
F32 = jnp.float32
MESH = pl.DeviceIdType.MESH
LEN = 256
FEATURES = 768
HALF = 384
HIDDEN = 3072
PACK = 1408
FIRST = HALF + FEATURES
NORMS = FIRST + 192
LINKS = ("x", "y", "near", "far")


class Place:
    def __init__(self):
        self.s = lax.axis_index("section")
        dp = lax.axis_index("dp")
        self.z = dp // 4
        self.y = (dp // 2) % 2
        self.c = dp % 2
        self.mid = (self.z == 1) | (self.z == 2)

    def device(self, s, z, y, c):
        return (s, z * 4 + y * 2 + c)

    def neighbour(self, link):
        s, z, y, c = self.s, self.z, self.y, self.c
        if link == "x":
            return self.device(1 - s, z, y, c)
        if link == "y":
            return self.device(s, z, 1 - y, c)
        if link == "near":
            return self.device(s, z + 1 - 2 * (z % 2), y, c)
        if link == "far":
            return self.device(s, 3 - z, y, c)
        return self.device(s, z, y, 1 - c)

    def along_z(self, j):
        z = self.z
        return (z, z + 1 - 2 * (z % 2), 2 - z // 2, 3 - 3 * (z // 2))[j]

    def block(self, ry, j):
        y = self.y if ry == 0 else 1 - self.y
        return self.along_z(j) * 2 + y

    def is_class(self, k):
        middle = self.mid if k % 2 else jnp.logical_not(self.mid)
        return (self.s == k // 2) & middle


def greet(place):
    barrier = pltpu.get_barrier_semaphore()
    for link in ("x", "y", "near", "core"):
        pl.semaphore_signal(barrier, 1, device_id=place.neighbour(link), device_id_type=MESH)

    @pl.when(place.mid)
    def _():
        pl.semaphore_signal(barrier, 1, device_id=place.neighbour("far"), device_id_type=MESH)
        pl.semaphore_wait(barrier, 5)

    @pl.when(jnp.logical_not(place.mid))
    def _():
        pl.semaphore_wait(barrier, 4)


def remote(source, target, send_sem, recv_sem, device):
    return pltpu.make_async_remote_copy(
        src_ref=source,
        dst_ref=target,
        send_sem=send_sem,
        recv_sem=recv_sem,
        device_id=device,
        device_id_type=MESH,
    )


def product(left, right):
    return jnp.dot(left, right, preferred_element_type=F32)


def times_transposed(left, right):
    return lax.dot_general(left, right, (((1,), (1,)), ((), ())), preferred_element_type=F32)


def transposed_times(left, right):
    return lax.dot_general(left, right, (((0,), (0,)), ((), ())), preferred_element_type=F32)


def normalized(rows):
    average = jnp.mean(rows, axis=-1, keepdims=True)
    centred = rows - average
    scale = lax.rsqrt(jnp.mean(centred * centred, axis=-1, keepdims=True) + EPSILON)
    return centred * scale, scale


def lane_index(shape):
    return lax.broadcasted_iota(jnp.int32, shape, 1)


def flat(block):
    return block.reshape(-1, block.shape[-1])


ARRAY_OF = (0, 1, 2, 2, 3, 3)
ROWS = (48, 48, 48, 192)
WIDTH = (2 * FEATURES, PACK, HIDDEN, FEATURES)


def piece_of(ref, g):
    lead = (slice(None),) * (len(ref.shape) - 2)
    if g in (2, 3):
        return ref.at[lead + (slice(None), pl.ds((g - 2) * (HIDDEN // 2), HIDDEN // 2))]
    if g in (4, 5):
        return ref.at[lead + (pl.ds((g - 4) * 96, 96), slice(None))]
    return ref


def forward_kernel(
    schedule,
    own_qk, own_pack, own_up, own_down, inputs, length,
    out_qk, out_pack, out_up, out_down,
    kept_qk, kept_values, kept_probs, kept_slope, kept_middle, kept_low,
    turned_normed, turned_attended, turned_mixed, turned_active,
    w_qk, w_pack, w_up, w_down,
    x_ref, normed, qk, values, probs, attended, middle, mixed, active, slope, low,
    t_normed, t_attended, t_mixed, t_active,
    recv_sem, send_sem, core_send, core_recv, local_sem, keep_sem, turn_send, turn_recv, fetch_sem,
):
    place = Place()
    s, c = place.s, place.c
    own = (own_qk, own_pack, own_up, own_down)
    whole = (w_qk, w_pack, w_up, w_down)
    whole_out = (out_qk, out_pack, out_up, out_down)

    fetch = pltpu.make_async_copy(inputs.at[s, 0], x_ref, fetch_sem.at[0])
    fetch.start()
    greet(place)

    def spot(g, layer, ry, j):
        return piece_of(whole[ARRAY_OF[g]].at[layer, place.block(ry, j), c], g)

    mine = [
        pltpu.make_async_copy(
            piece_of(own[ARRAY_OF[g]].at[0], g), spot(g, s, 0, 0), local_sem.at[g]
        )
        for g in range(6)
    ]
    for one in mine:
        one.start()

    def weight_copy(k, item):
        link, g, layer, ry, j = item
        target = spot(g, layer, ry, j)
        source = target
        if (ry, j) == (0, 0) and layer == k // 2:
            source = piece_of(own[ARRAY_OF[g]].at[0], g)
        return remote(
            source,
            target,
            send_sem.at[LINKS.index(link), g, layer, ry * 4 + j],
            recv_sem.at[g, layer, place.block(ry, j)],
            place.neighbour(link),
        )

    def hand_over(g, layer):
        part = piece_of(whole[ARRAY_OF[g]].at[layer, :, c], g)
        return remote(
            part, part, core_send.at[g, layer], core_recv.at[g, layer], place.neighbour("core")
        )

    def from_core(g, layer):
        part = piece_of(whole[ARRAY_OF[g]].at[layer, :, 1 - c], g)
        return remote(
            part, part, core_send.at[g, layer], core_recv.at[g, layer], place.neighbour("core")
        )

    missing = [{(g, l): 8 for g in range(6) for l in range(2)} for k in range(4)]
    begun = [set() for k in range(4)]

    def run_items(k, items):
        for item in items:
            link, g, layer, ry, j = item
            if link is not None:
                weight_copy(k, item).start()
                continue
            if (ry, j) == (0, 0) and layer == k // 2:
                mine[g].wait()
            else:
                remote(
                    spot(g, layer, ry, j),
                    spot(g, layer, ry, j),
                    send_sem.at[0, 0, 0, 0],
                    recv_sem.at[g, layer, place.block(ry, j)],
                    place.neighbour("x"),
                ).wait_recv()
            missing[k][g, layer] -= 1
            if missing[k][g, layer] == 0:
                hand_over(g, layer).start()

    kept = []

    def keep(source, target):
        copy = pltpu.make_async_copy(source, target, keep_sem.at[len(kept)])
        kept.append(copy)
        copy.start()

    turned = []

    def turn_over(number, layer, source, target):
        copy = pltpu.make_async_copy(source.at[:, c], target.at[layer, 0], keep_sem.at[len(kept)])
        kept.append(copy)
        copy.start()
        other = remote(
            source.at[:, 1 - c],
            target.at[layer, 1],
            turn_send.at[number, layer],
            turn_recv.at[number, layer],
            place.neighbour("core"),
        )
        other.start()
        turned.append(other)

    def norm_vectors(layer):
        window = flat(w_pack[layer, :, :, :, NORMS - 64 : NORMS + 64]).astype(F32)
        rows = window.T
        return [rows[64 + i : 65 + i, :] for i in range(4)]

    def residual(layer):
        return (x_ref if layer == 0 else low.at[0])[...].astype(F32)

    def front(layer):
        for g, l in ((0, 0), (1, 0), (1, 1)) if layer == 0 else ((0, 1),):
            from_core(g, l).wait_recv()
            keep(whole[g].at[l], whole_out[g].at[l])
        if layer == 0:
            fetch.wait()
        vectors = norm_vectors(layer)
        unit, _ = normalized(residual(layer))
        rows = (unit * vectors[0] + vectors[1]).astype(BF)
        normed[...] = rows
        for i in range(3):
            at = slice(i * 512, (i + 1) * 512)
            qk[layer, :, at] = product(rows, flat(w_qk[layer, :, :, :, at])).astype(BF)
        keep(qk.at[layer], kept_qk.at[layer])
        values[layer, :, :HALF] = product(rows, flat(w_pack[layer, :, :, :, :HALF])).astype(BF)
        if layer == 0:
            window = slice(FIRST, FIRST + 256)
            part = [product(rows, flat(w_pack[l, :, :, :, window])) for l in range(2)]
            moved = pltpu.roll(part[1], 64, 1)
            between = jnp.where(lane_index((LEN, 128)) < 64, part[0][:, 128:], moved[:, :128])
            values[0, :, HALF : HALF + 128] = part[0][:, :128].astype(BF)
            values[0, :, HALF + 128 : HALF + 256] = between.astype(BF)
            values[0, :, HALF + 256 :] = moved[:, 128:].astype(BF)
        else:
            values[1, :, HALF:] = values[0, :, HALF:]
        keep(values.at[layer], kept_values.at[layer])
        t_normed[layer] = rows.T.reshape(8, 2, 48, LEN)
        turn_over(0, layer, t_normed.at[layer], turned_normed)

    def attend(layer, pairs):
        count = length[s, 0]
        key = lax.broadcasted_iota(jnp.int32, (LEN, LEN), 0)
        query = lax.broadcasted_iota(jnp.int32, (LEN, LEN), 1)
        allowed = (key <= query) & (key < count)
        left = lane_index((LEN, 128)) < 64
        for pair in pairs:
            at = slice(pair * 128, (pair + 1) * 128)
            queries = qk[layer, :, at] * jnp.asarray(HD**-0.5, BF)
            keys = qk[layer, :, FEATURES + pair * 128 : FEATURES + (pair + 1) * 128]
            head_values = values[layer, :, at]
            parts = []
            for head in range(2):
                chosen = left if head == 0 else jnp.logical_not(left)
                scores = times_transposed(jnp.where(chosen, keys, jnp.zeros_like(keys)), queries)
                scores = jnp.where(allowed, scores, -1e30)
                raised = jnp.exp(scores - jnp.max(scores, axis=0, keepdims=True))
                soft = (raised / jnp.sum(raised, axis=0, keepdims=True)).astype(BF)
                probs[layer, 2 * pair + head] = soft
                parts.append(transposed_times(soft, head_values))
            attended[:, at] = jnp.where(left, parts[0], parts[1]).astype(BF)

    def project_out(layer):
        keep(probs.at[layer], kept_probs.at[layer])
        rows = attended[...]
        total = residual(layer) + product(
            rows, flat(w_pack[layer, :, :, :, HALF : HALF + FEATURES])
        )
        middle[layer] = total
        keep(middle.at[layer], kept_middle.at[layer])
        vectors = norm_vectors(layer)
        unit, _ = normalized(total)
        after = (unit * vectors[2] + vectors[3]).astype(BF)
        mixed[...] = after
        t_attended[layer] = rows.T.reshape(8, 2, 48, LEN)
        turn_over(1, layer, t_attended.at[layer], turned_attended)
        t_mixed[layer] = after.T.reshape(8, 2, 48, LEN)
        turn_over(2, layer, t_mixed.at[layer], turned_mixed)

    def widen(layer, i):
        if i % 2 == 0:
            from_core(2 + i // 2, layer).wait_recv()
        at = slice(i * 768, (i + 1) * 768)
        upper = product(mixed[...], flat(w_up[layer, :, :, :, at]))
        inner = upper * (0.7978845608028654 + 0.03567740813636141 * (upper * upper))
        bent = jnp.tanh(inner)
        half = 0.5 * (1.0 + bent)
        grown = (upper * half).astype(BF)
        active[:, at] = grown
        steep = 0.7978845608028654 + 0.10703222440908423 * (upper * upper)
        slope[layer, :, at] = (half + 0.5 * upper * (1.0 - bent * bent) * steep).astype(BF)
        t_active[layer, 2 * i : 2 * i + 2] = grown.T.reshape(2, 2, 192, LEN)

    def narrow(layer):
        keep(slope.at[layer], kept_slope.at[layer])
        turn_over(3, layer, t_active.at[layer], turned_active)
        keep(w_up.at[layer], out_up.at[layer])
        from_core(4, layer).wait_recv()
        from_core(5, layer).wait_recv()
        keep(w_down.at[layer], out_down.at[layer])
        total = middle[layer] + product(active[...], flat(w_down[layer]))
        low[layer] = total.astype(BF)
        keep(low.at[layer], kept_low.at[layer])

    steps = []
    for layer in range(2):
        steps.append(functools.partial(front, layer))
        for i in range(3):
            steps.append(functools.partial(attend, layer, (2 * i, 2 * i + 1)))
        steps.append(functools.partial(project_out, layer))
        for i in range(4):
            steps.append(functools.partial(widen, layer, i))
        steps.append(functools.partial(narrow, layer))

    for number in range(len(steps) + 1):
        for k in range(4):
            if schedule[k][number]:
                pl.when(place.is_class(k))(
                    functools.partial(run_items, k, schedule[k][number])
                )
        if number < len(steps):
            steps[number]()

    for k in range(4):

        def finish(k=k):
            for items in schedule[k]:
                for item in items:
                    if item[0] is not None:
                        weight_copy(k, item).wait_send()

        pl.when(place.is_class(k))(finish)
    for g in range(6):
        for layer in range(2):
            hand_over(g, layer).wait_send()
    for copy in kept:
        copy.wait()
    for copy in turned:
        copy.wait()


def forward_call(schedule, own, inputs, length):
    def hbm(shape, dtype=BF):
        return jax.ShapeDtypeStruct(shape, dtype)

    def turn(rows):
        return (2, 2, 8, rows, LEN)

    weights = [(2, 8, 2, ROWS[a], WIDTH[a]) for a in range(4)]
    kept = [
        hbm((2, LEN, 2 * FEATURES)),
        hbm((2, LEN, FEATURES)),
        hbm((2, HEADS, LEN, LEN)),
        hbm((2, LEN, HIDDEN)),
        hbm((2, LEN, FEATURES), F32),
        hbm((2, LEN, FEATURES)),
    ]
    outs = [hbm(shape) for shape in weights] + kept
    outs += [hbm(turn(48)), hbm(turn(48)), hbm(turn(48)), hbm(turn(192))]
    scratch = [pltpu.VMEM(shape, BF) for shape in weights]
    scratch += [
        pltpu.VMEM((LEN, FEATURES), BF),
        pltpu.VMEM((LEN, FEATURES), BF),
        pltpu.VMEM((2, LEN, 2 * FEATURES), BF),
        pltpu.VMEM((2, LEN, FEATURES), BF),
        pltpu.VMEM((2, HEADS, LEN, LEN), BF),
        pltpu.VMEM((LEN, FEATURES), BF),
        pltpu.VMEM((2, LEN, FEATURES), F32),
        pltpu.VMEM((LEN, FEATURES), BF),
        pltpu.VMEM((LEN, HIDDEN), BF),
        pltpu.VMEM((2, LEN, HIDDEN), BF),
        pltpu.VMEM((2, LEN, FEATURES), BF),
        pltpu.VMEM((2, 8, 2, 48, LEN), BF),
        pltpu.VMEM((2, 8, 2, 48, LEN), BF),
        pltpu.VMEM((2, 8, 2, 48, LEN), BF),
        pltpu.VMEM((2, 8, 2, 192, LEN), BF),
        pltpu.SemaphoreType.DMA((6, 2, 8)),
        pltpu.SemaphoreType.DMA((4, 6, 2, 8)),
        pltpu.SemaphoreType.DMA((6, 2)),
        pltpu.SemaphoreType.DMA((6, 2)),
        pltpu.SemaphoreType.DMA((6,)),
        pltpu.SemaphoreType.DMA((32,)),
        pltpu.SemaphoreType.DMA((4, 2)),
        pltpu.SemaphoreType.DMA((4, 2)),
        pltpu.SemaphoreType.DMA((1,)),
    ]
    anywhere = pl.BlockSpec(memory_space=pl.ANY)
    return pl.pallas_call(
        functools.partial(forward_kernel, schedule),
        out_shape=outs,
        in_specs=[anywhere] * 5 + [pl.BlockSpec(memory_space=pltpu.SMEM)],
        out_specs=[anywhere] * len(outs),
        scratch_shapes=scratch,
        compiler_params=pltpu.CompilerParams(
            collective_id=0, has_side_effects=True, vmem_limit_bytes=62 * 2**20
        ),
    )(*own, inputs, length)


def schedule_of(codes):
    result = []
    for per_class in codes:
        result.append([])
        for numbers in per_class:
            items = []
            for n in numbers:
                link = None if n < 10000 else LINKS[n // 10000 - 1]
                items.append((link, n // 1000 % 10, n // 100 % 10, n // 10 % 10, n % 10))
            result[-1].append(items)
    return result


def branches(order, rx, ry, j):
    apart = {"x": rx != 0, "y": ry != 0, "z": j != 0}
    last = max([i for i, axis in enumerate(order) if apart[axis]], default=-1)
    links = []
    for i, axis in enumerate(order):
        if i < last:
            continue
        if axis != "z":
            if i > last:
                links.append((axis, False))
        elif i > last:
            links += [("near", False), ("far", True)]
        else:
            links.append(("far" if j == 1 else "near", True))
    return links


def slot_table(orders):
    table, counts = {}, []
    for g in range(6):
        number = 0
        for rx in range(2):
            for ry in range(2):
                for j in range(4):
                    links = []
                    for layer in range(2):
                        for link, _ in branches(orders[g, layer], rx, ry, j):
                            if link not in links:
                                links.append(link)
                    for link in links:
                        table[g, rx, ry, j, link] = number
                        number += 1
        counts.append(number)
    return table, counts


def towards_owner(order, k, rx, ry, j):
    apart = {"x": rx != 0, "y": ry != 0, "z": j != 0}
    axis = [axis for axis in order if apart[axis]][-1]
    if axis == "x":
        return "x", (0, ry, j)
    if axis == "y":
        return "y", (rx, 0, j)
    if j == 1:
        return "near", (rx, ry, 0)
    if k % 2:
        return "far", (rx, ry, 0 if j == 2 else 1)
    return "near", (rx, ry, j)


def backward_kernel(
    schedule, orders, slots,
    w_qk, w_pack, w_up, w_down,
    kept_qk, kept_values, kept_probs, kept_slope, kept_middle, kept_low,
    turned_normed, turned_attended, turned_mixed, turned_active,
    inputs, cotangent, length,
    out_qk, out_pack, out_up, out_down, out_grads, swapped_low, swapped_grad,
    m_qk, m_pack, m_wide,
    qk, values, probs, slope, middle, entering, t_normed, t_attended, t_mixed, t_active,
    cot,
    dy, du, da, dqk, dv,
    far_dy, far_du, far_da, far_dqk, far_dv,
    total, d_mixed, d_attended, shared_two, grads, vectors, far_vectors, columns,
    h_qk, h_pack, h_up, h_down,
    arrived_0, arrived_1, arrived_2, arrived_3, arrived_4, arrived_5,
    r_qk, r_pack, r_up, r_down,
    load_sem, pair_send, pair_recv, credit, swap_send, swap_recv, sum_send, sum_recv, out_sem,
):
    place = Place()
    s, c = place.s, place.c
    held = (h_qk, h_pack, h_up, h_down)
    arrived = (arrived_0, arrived_1, arrived_2, arrived_3, arrived_4, arrived_5)
    result = (r_qk, r_pack, r_up, r_down)
    outs = (out_qk, out_pack, out_up, out_down)

    sources = {
        "qk_matrix": (m_qk, lambda l: w_qk.at[l]),
        "pack0": (m_pack.at[0], lambda l: w_pack.at[0]),
        "pack1": (m_pack.at[1], lambda l: w_pack.at[1]),
        "down": (m_wide, lambda l: w_down.at[l]),
        "up0": (m_wide.at[0:16], lambda l: w_up.at[l, :, :, pl.ds(0, 768)]),
        "up1": (m_wide.at[16:32], lambda l: w_up.at[l, :, :, pl.ds(768, 768)]),
        "up2": (m_wide.at[32:48], lambda l: w_up.at[l, :, :, pl.ds(1536, 768)]),
        "up3": (m_wide.at[48:64], lambda l: w_up.at[l, :, :, pl.ds(2304, 768)]),
        "qk": (qk, lambda l: kept_qk.at[l]),
        "values": (values, lambda l: kept_values.at[l]),
        "probs": (probs, lambda l: kept_probs.at[l]),
        "slope": (slope, lambda l: kept_slope.at[l]),
        "middle": (middle, lambda l: kept_middle.at[l]),
        "entering": (entering, lambda l: inputs.at[s, 0] if l == 0 else kept_low.at[0]),
        "normed": (t_normed, lambda l: turned_normed.at[l]),
        "attended": (t_attended, lambda l: turned_attended.at[l]),
        "mixed": (t_mixed, lambda l: turned_mixed.at[l]),
        "active": (t_active, lambda l: turned_active.at[l]),
        "cotangent": (cot, lambda l: cotangent.at[s, 0]),
    }
    names = list(sources)

    def loading(name, layer):
        target, source = sources[name]
        return pltpu.make_async_copy(
            source(layer), target, load_sem.at[names.index(name), layer]
        )

    def load(*which, layer):
        for name in which:
            loading(name, layer).start()

    def loaded(*which, layer):
        for name in which:
            loading(name, layer).wait()

    load("cotangent", "down", "slope", "active", "mixed", "middle", "pack1", layer=1)
    load("qk", "values", "probs", "attended", "entering", "qk_matrix", "normed", layer=1)
    load("pack0", layer=0)
    greet(place)

    across = place.neighbour("x")
    low_swap = remote(kept_low.at[1 - s], swapped_low, swap_send.at[0], swap_recv.at[0], across)
    low_swap.start()
    grad_swap = remote(grads.at[1 - s], swapped_grad, swap_send.at[1], swap_recv.at[1], across)

    shared = {
        "dy": (dy, far_dy),
        "du0": (du.at[:, 0:1536], far_du.at[:, 0:1536]),
        "du1": (du.at[:, 1536:3072], far_du.at[:, 1536:3072]),
        "da": (da, far_da),
        "dqk": (dqk, far_dqk),
        "dv": (dv, far_dv),
        "vectors": (vectors, far_vectors),
    }
    shared_names = list(shared)

    def exchange(name, layer):
        n = shared_names.index(name)
        return remote(
            *shared[name], pair_send.at[n, layer], pair_recv.at[n, layer], place.neighbour("core")
        )

    def hand(name, layer):
        if layer == 0:
            pl.semaphore_wait(credit.at[shared_names.index(name)], 1)
        exchange(name, layer).start()

    def done_with(name, layer):
        if layer == 1:
            pl.semaphore_signal(
                credit.at[shared_names.index(name)],
                1,
                device_id=place.neighbour("core"),
                device_id_type=MESH,
            )

    def free_to_write(name, layer):
        if layer == 0:
            exchange(name, 1).wait_send()

    def summed(left, right, far_right):
        return product(flat3(left[0]), right) + product(flat3(left[1]), far_right)

    def flat3(block):
        return block.reshape(-1, block.shape[-1])

    def norm_rows(layer):
        window = flat(m_pack[layer, :, :, :, NORMS - 64 : NORMS + 64]).astype(F32)
        rows = window.T
        return [rows[64 + i : 65 + i, :] for i in range(4)]

    def norm_back(grad, rows, gain):
        unit, scale = normalized(rows)
        scaled = grad * gain
        inner = scaled - jnp.mean(scaled, axis=-1, keepdims=True)
        inner = inner - unit * jnp.mean(scaled * unit, axis=-1, keepdims=True)
        return (
            jnp.sum(grad * unit, axis=0, keepdims=True),
            jnp.sum(grad, axis=0, keepdims=True),
            scale * inner,
        )

    def begin(layer):
        if layer == 1:
            vectors[...] = jnp.zeros_like(vectors)
            loaded("cotangent", layer=1)
            position = lax.broadcasted_iota(jnp.int32, (LEN, FEATURES), 0)
            grad = jnp.where(position < length[s, 0], cot[...].astype(F32), 0.0)
        else:
            grad = grads[1].astype(F32)
        free_to_write("dy", layer)
        total[...] = grad
        dy[...] = grad.astype(BF)
        hand("dy", layer)

    def through_active(layer, i):
        if i == 0:
            loaded("down", "slope", layer=layer)
        if i % 2 == 0:
            free_to_write("du%d" % (i // 2), layer)
        at = slice(i * 768, (i + 1) * 768)
        grad = times_transposed(dy[...], flat3(m_wide[16 * i : 16 * i + 16]))
        du[:, at] = (grad * slope[:, at].astype(F32)).astype(BF)
        if i % 2 == 1:
            hand("du%d" % (i // 2), layer)
        if i == 3:
            load("up0", "up1", "up2", "up3", layer=layer)
            if layer == 1:
                load("slope", layer=0)

    def sum_down(layer, half):
        if half == 0:
            loaded("active", layer=layer)
            exchange("dy", layer).wait_recv()
        rows = slice(half * 96, half * 96 + 96)
        sums = summed(t_active[:, :, rows, :], dy[...], far_dy[...])
        h_down[layer, :, rows, :] = sums.astype(BF).reshape(8, 96, FEATURES)
        if half == 1:
            done_with("dy", layer)
            if layer == 1:
                load("active", layer=0)

    def to_mixed(layer):
        for q in range(4):
            loaded("up%d" % q, layer=layer)
            part = times_transposed(
                du[:, q * 768 : (q + 1) * 768], flat3(m_wide[16 * q : 16 * q + 16])
            )
            d_mixed[...] = part if q == 0 else d_mixed[...] + part
        if layer == 1:
            load("down", layer=0)

    def sum_up(layer, q):
        if q == 0:
            loaded("mixed", layer=layer)
        if q % 2 == 0:
            exchange("du%d" % (q // 2), layer).wait_recv()
        at = slice(q * 768, (q + 1) * 768)
        sums = summed(t_mixed[...], du[:, at], far_du[:, at])
        h_up[layer, :, :, at] = sums.astype(BF).reshape(8, 48, 768)
        if q % 2 == 1:
            done_with("du%d" % (q // 2), layer)
        if q == 3 and layer == 1:
            load("mixed", layer=0)

    def second_norm(layer):
        loaded("middle", "pack%d" % layer, layer=layer)
        free_to_write("vectors", layer)
        free_to_write("da", layer)
        gain, bias, through = norm_back(d_mixed[...], middle[...], norm_rows(layer)[2])
        vectors[2:3, :] = gain
        vectors[3:4, :] = bias
        grad = total[...] + through
        total[...] = grad
        da[...] = grad.astype(BF)
        hand("da", layer)
        matrix = flat(m_pack[layer, :, :, :, HALF:FIRST])
        d_attended[...] = times_transposed(da[...], matrix).astype(BF)
        if layer == 1:
            load("middle", layer=0)

    def through_attention(layer, pair):
        if pair == 0:
            loaded("qk", "values", "probs", layer=layer)
            free_to_write("dqk", layer)
            free_to_write("dv", layer)
        left = lane_index((LEN, 128)) < 64
        at = slice(pair * 128, (pair + 1) * 128)
        key_at = slice(FEATURES + pair * 128, FEATURES + (pair + 1) * 128)
        queries, keys, head_values = qk[:, at], qk[:, key_at], values[:, at]
        grad = d_attended[:, at]
        parts = []
        for head in range(2):
            chosen = left if head == 0 else jnp.logical_not(left)
            soft = probs[2 * pair + head]
            to_soft = times_transposed(
                jnp.where(chosen, head_values, jnp.zeros_like(head_values)), grad
            )
            exact = soft.astype(F32)
            inner = jnp.sum(exact * to_soft, axis=0, keepdims=True)
            to_scores = (exact * (to_soft - inner)).astype(BF)
            parts.append(
                (
                    transposed_times(to_scores, keys),
                    product(to_scores, queries),
                    product(soft, grad),
                )
            )
        of_queries, of_keys, of_values = [
            jnp.where(left, one, other) for one, other in zip(*parts)
        ]
        dqk[:, at] = (of_queries * HD**-0.5).astype(BF)
        dqk[:, key_at] = (of_keys * HD**-0.5).astype(BF)
        if pair < 3:
            dv[:, at] = of_values.astype(BF)
        else:
            there = slice((pair - 3) * 128, (pair - 2) * 128)
            if layer == 1:
                shared_two[:, there] = of_values.astype(BF)
            else:
                dv[:, at] = (of_values + shared_two[:, there].astype(F32)).astype(BF)
        if pair == 5:
            hand("dqk", layer)
            hand("dv", layer)
            if layer == 1:
                load("qk", "values", "probs", layer=0)

    def first_window(part):
        if part == 0:
            window = lambda ref: ref[:, HALF : HALF + 256]
        else:
            window = lambda ref: pltpu.roll(
                ref[:, HALF + 128 :].astype(F32), 192, 1
            ).astype(BF)
        inside = lane_index((LEN, 256)) < 192
        return [
            jnp.where(inside, window(ref), jnp.zeros((LEN, 256), BF)) for ref in (dv, far_dv)
        ]

    def first_norm(layer):
        loaded("qk_matrix", "entering", layer=layer)
        grad = times_transposed(dqk[...], flat(m_qk[...]))
        grad = grad + times_transposed(dv[:, :HALF], flat(m_pack[layer, :, :, :, :HALF]))
        if layer == 0:
            for part in range(2):
                grad = grad + times_transposed(
                    first_window(part)[0], flat(m_pack[part, :, :, :, FIRST : FIRST + 256])
                )
        rows = entering[...].astype(F32)
        gain, bias, through = norm_back(grad, rows, norm_rows(layer)[0])
        vectors[0:1, :] = gain
        vectors[1:2, :] = bias
        hand("vectors", layer)
        grads[layer] = (total[...] + through).astype(BF)
        if layer == 1:
            load("qk_matrix", "entering", layer=0)
        pl.when(s == 1 - layer)(grad_swap.start)

    def sum_out(layer):
        loaded("attended", layer=layer)
        exchange("da", layer).wait_recv()
        sums = summed(t_attended[...], da[...], far_da[...])
        h_pack[layer, :, :, HALF:FIRST] = sums.astype(BF).reshape(8, 48, FEATURES)
        done_with("da", layer)
        if layer == 1:
            load("attended", layer=0)

    def sum_qk(layer):
        loaded("normed", layer=layer)
        exchange("dqk", layer).wait_recv()
        for q in range(2):
            at = slice(q * FEATURES, (q + 1) * FEATURES)
            sums = summed(t_normed[...], dqk[:, at], far_dqk[:, at])
            h_qk[layer, :, :, at] = sums.astype(BF).reshape(8, 48, FEATURES)
        done_with("dqk", layer)

    def sum_pack(layer):
        exchange("dv", layer).wait_recv()
        exchange("vectors", layer).wait_recv()
        sums = summed(t_normed[...], dv[:, :HALF], far_dv[:, :HALF])
        h_pack[layer, :, :, :HALF] = sums.astype(BF).reshape(8, 48, HALF)
        both = vectors[...] + far_vectors[...]
        nothing = jnp.zeros((64, FEATURES), F32)
        tall = jnp.concatenate([nothing, both, nothing[:56]], axis=0)
        columns[layer] = tall.T.reshape(8, 2, 48, 128)
        if layer == 0:
            for part in range(2):
                sums = summed(t_normed[...], *first_window(part)).reshape(8, 48, 256)
                h_pack[part, :, :, FIRST : FIRST + 128] = sums[:, :, :128].astype(BF)
                h_pack[part, :, :, FIRST + 128 :] = (
                    sums[:, :, 128:] + columns[part, :, c]
                ).astype(BF)
        done_with("dv", layer)
        done_with("vectors", layer)
        if layer == 1:
            load("normed", layer=0)

    steps = []

    def step(action, *arguments):
        steps.append(functools.partial(action, *arguments))

    for layer in (1, 0):
        step(begin, layer)
        for i in range(4):
            step(through_active, layer, i)
        for half in range(2):
            step(sum_down, layer, half)
        step(to_mixed, layer)
        for q in range(4):
            step(sum_up, layer, q)
        step(second_norm, layer)
        for pair in range(6):
            step(through_attention, layer, pair)
        step(sum_out, layer)
        step(first_norm, layer)
        step(sum_qk, layer)
        step(sum_pack, layer)

    def sum_copy(k, item):
        g, layer, ry, j = item
        rx = int(k // 2 != layer)
        link, there = towards_owner(orders[g, layer], k, rx, ry, j)
        return remote(
            piece_of(held[ARRAY_OF[g]].at[layer, place.block(ry, j)], g),
            arrived[g].at[slots[(g,) + there + (link,)]],
            sum_send.at[g, layer, ry * 4 + j],
            sum_recv.at[g, slots[(g,) + there + (link,)]],
            place.neighbour(link),
        )

    def run_items(k, items):
        for item in items:
            g, layer, ry, j = item
            rx = int(k // 2 != layer)
            mine = piece_of(held[ARRAY_OF[g]].at[layer, place.block(ry, j)], g)
            terms = []
            for link, middle_only in branches(orders[g, layer], rx, ry, j):
                if middle_only and not k % 2:
                    continue
                slot = slots[g, rx, ry, j, link]
                remote(
                    mine,
                    arrived[g].at[slot],
                    sum_send.at[g, layer, ry * 4 + j],
                    sum_recv.at[g, slot],
                    place.neighbour(link),
                ).wait_recv()
                terms.append(arrived[g].at[slot])
            final = (rx, ry, j) == (0, 0, 0)
            target = piece_of(result[ARRAY_OF[g]], g) if final else mine
            if terms or final:
                add_up(target, [mine] + terms)
            if not final:
                sum_copy(k, item).start()
                continue
            out = piece_of(outs[ARRAY_OF[g]], g)
            pltpu.make_async_copy(target, out, out_sem.at[g]).start()

    def add_up(target, terms):
        @pl.loop(0, target.shape[0] // 16)
        def _(i):
            at = pl.ds(pl.multiple_of(i * 16, 16), 16)
            sums = terms[0][at, :].astype(F32)
            for term in terms[1:]:
                sums = sums + term[at, :].astype(F32)
            target[at, :] = sums.astype(target.dtype)

    for number in range(len(steps) + 1):
        for k in range(4):
            if schedule[k][number]:
                pl.when(place.is_class(k))(
                    functools.partial(run_items, k, schedule[k][number])
                )
        if number < len(steps):
            steps[number]()

    for k in range(4):

        def finish(k=k):
            for items in schedule[k]:
                for item in items:
                    g, layer, ry, j = item
                    if (k // 2 != layer, ry, j) == (False, 0, 0):
                        pltpu.make_async_copy(
                            piece_of(result[ARRAY_OF[g]], g),
                            piece_of(outs[ARRAY_OF[g]], g),
                            out_sem.at[g],
                        ).wait()
                    else:
                        sum_copy(k, item).wait_send()

        pl.when(place.is_class(k))(finish)
    own_grads = pltpu.make_async_copy(grads, out_grads, out_sem.at[6])
    own_grads.start()
    for name in shared_names:
        exchange(name, 0).wait_send()
    low_swap.wait()
    grad_swap.wait()
    own_grads.wait()


def backward_call(schedule, orders, weights, kept, turned, inputs, cotangent, lengths):
    slots, counts = slot_table(orders)
    blocks = [(48, 2 * FEATURES), (48, PACK), (48, HIDDEN), (192, FEATURES)]
    pieces = [(48, 1536), (48, PACK), (48, 1536), (48, 1536), (96, FEATURES), (96, FEATURES)]
    rows = (LEN, FEATURES)
    outs = [jax.ShapeDtypeStruct(block, F32) for block in blocks]
    outs += [jax.ShapeDtypeStruct((2,) + rows, BF)] + [jax.ShapeDtypeStruct(rows, BF)] * 2
    pair = [rows, (LEN, HIDDEN), rows, (LEN, 2 * FEATURES), rows]
    scratch = [
        pltpu.VMEM((8, 2, 48, 2 * FEATURES), BF),
        pltpu.VMEM((2, 8, 2, 48, PACK), BF),
        pltpu.VMEM((64, 48, FEATURES), BF),
        pltpu.VMEM((LEN, 2 * FEATURES), BF),
        pltpu.VMEM(rows, BF),
        pltpu.VMEM((HEADS, LEN, LEN), BF),
        pltpu.VMEM((LEN, HIDDEN), BF),
        pltpu.VMEM(rows, F32),
        pltpu.VMEM(rows, BF),
        pltpu.VMEM((2, 8, 48, LEN), BF),
        pltpu.VMEM((2, 8, 48, LEN), BF),
        pltpu.VMEM((2, 8, 48, LEN), BF),
        pltpu.VMEM((2, 8, 192, LEN), BF),
        pltpu.VMEM(rows, BF),
    ]
    scratch += [pltpu.VMEM(shape, BF) for shape in pair + pair]
    scratch += [
        pltpu.VMEM(rows, F32),
        pltpu.VMEM(rows, F32),
        pltpu.VMEM(rows, BF),
        pltpu.VMEM((LEN, HALF), BF),
        pltpu.VMEM((2,) + rows, BF),
        pltpu.VMEM((8, FEATURES), F32),
        pltpu.VMEM((8, FEATURES), F32),
        pltpu.VMEM((2, 8, 2, 48, 128), F32),
    ]
    scratch += [pltpu.VMEM((2, 8) + block, BF) for block in blocks]
    scratch += [pltpu.VMEM((count,) + piece, BF) for count, piece in zip(counts, pieces)]
    scratch += [pltpu.VMEM(block, F32) for block in blocks]
    scratch += [
        pltpu.SemaphoreType.DMA((19, 2)),
        pltpu.SemaphoreType.DMA((7, 2)),
        pltpu.SemaphoreType.DMA((7, 2)),
        pltpu.SemaphoreType.REGULAR((7,)),
        pltpu.SemaphoreType.DMA((2,)),
        pltpu.SemaphoreType.DMA((2,)),
        pltpu.SemaphoreType.DMA((6, 2, 8)),
        pltpu.SemaphoreType.DMA((6, max(counts))),
        pltpu.SemaphoreType.DMA((7,)),
    ]
    anywhere = pl.BlockSpec(memory_space=pl.ANY)
    operands = [
        weights[0],
        weights[1],
        weights[2].reshape(2, 16, 48, HIDDEN),
        weights[3].reshape(2, 64, 48, FEATURES),
    ]
    operands += list(kept) + list(turned) + [inputs, cotangent]
    return pl.pallas_call(
        functools.partial(backward_kernel, schedule, orders, slots),
        out_shape=outs,
        in_specs=[anywhere] * len(operands) + [pl.BlockSpec(memory_space=pltpu.SMEM)],
        out_specs=[anywhere] * len(outs),
        scratch_shapes=scratch,
        compiler_params=pltpu.CompilerParams(
            collective_id=1, has_side_effects=True, vmem_limit_bytes=63 * 2**20
        ),
    )(*operands, lengths)


GATHER = (
    (
        (20000, 30000, 10000, 23000, 33000, 13000, 21000, 31000, 11000, 1, 10, 100, 24000,
        30010, 0, 1000, 2000, 3000, 4000, 5000, 10001, 1100, 3001, 3010, 21100, 34000, 13001,
        3100, 1001, 1010, 23100, 31010, 11010, 101, 2, 4010, 23001, 32000, 10010, 1110, 110,
        3002, 23002, 35000, 13002, 3110, 1101, 1002, 21101, 10002, 1011, 3011, 102, 22000,
        14000, 3003, 3012, 111, 23003, 13003, 1003, 1111, 1102, 21102, 12000, 1012, 2010, 103,
        25000, 15000, 11, 3013, 112, 10011, 1013, 1112, 1103, 21103, 3, 10003, 5010, 113, 35010,
        12, 10012, 3101, 23101, 1113, 13, 10013, 3102, 23102, 4001, 14001, 3103, 23103, 3111,
        4002, 14002, 2100, 24001, 3112, 4003, 14003, 2101, 24002),
        (3113, 2001, 15010),
        (2102, 24003, 4011),
        (2002, 2103, 22001),
        (4012, 2003),
        (4100, 22002, 4013, 5001, 15001, 2110, 22003, 2011, 5011, 15011, 4101, 24100, 2012,
        5002, 15002, 4102, 24101, 2013, 5003, 15003, 4103, 24102, 4110, 5012, 15012, 5100,
        24103, 4111, 5013, 15013, 5101, 25100, 4112, 5102, 25101),
        (4113,),
        (),
        (2113, 25102, 5110),
        (2111,),
        (5111,),
        (5103, 25103, 5112),
        (2112,),
        (),
        (5113,),
        (),
        (),
        (),
        (),
        (),
        (),
    ),
    (
        (20000, 30000, 40000, 10000, 23000, 33000, 43000, 13000, 21000, 31000, 41000, 11000, 1,
        2, 0, 1000, 2000, 3000, 4000, 5000, 10, 100, 24000, 30002, 40001, 10001, 1100, 3001,
        3002, 3010, 21100, 33002, 43001, 13001, 3100, 1001, 1002, 1010, 23100, 31002, 41001,
        13002, 101, 11, 3, 4010, 23001, 31010, 41010, 11010, 1110, 102, 4001, 3003, 33003,
        40010, 23002, 13003, 3110, 1011, 1003, 110, 31003, 41011, 23003, 10002, 1012, 3011,
        2001, 103, 31012, 40011, 24001, 10010, 12, 3012, 5001, 111, 30010, 44000, 22000, 10011,
        1013, 3013, 112, 31013, 44001, 22001, 10003, 13, 4011, 113, 30003, 42000, 25000, 10012,
        4002, 2010, 1101, 30012, 42001, 21101, 10013, 4003, 1102, 2011, 30013, 45000, 21102,
        14000, 2002, 1103, 5010, 34000, 45001, 21103, 14001, 2003, 3101, 1111, 34002, 23101,
        45010, 14002, 5002, 3102, 1112, 5011, 34003, 23102, 45011, 14003, 1113, 5003, 3103,
        32000, 23103, 12000, 3111, 5012, 2100, 32002, 24002, 15000, 3112, 5013, 2101),
        (32003, 24003, 15001, 3113),
        (2102, 35000, 22002),
        (15010, 4012, 2103),
        (35010, 22003, 15002, 4013),
        (4100, 35002, 24100, 15011, 2012, 4101, 35003, 24101, 15003, 2013, 4102, 35012, 24102,
        15012, 4110, 2111, 35013, 15013, 4111, 4103, 24103, 4112, 5100, 25100, 2113, 4113,
        2110),
        (5110,),
        (),
        (5101, 25101),
        (2112,),
        (),
        (5102, 25102, 5111),
        (5103, 25103),
        (),
        (5112,),
        (),
        (5113,),
        (),
        (),
        (),
        (),
    ),
    (
        (30100, 20100, 10100, 31100, 21100, 11100, 33100, 23100, 13100, 0, 101, 110, 32100,
        20101, 100, 1100, 2100, 3100, 4100, 5100, 10101, 1101, 1110, 3000, 34100, 21101, 10110,
        3101, 3110, 1000, 23101, 31000, 11101, 102, 111, 1, 20102, 35100, 10102, 1102, 1111,
        3001, 21102, 10111, 3102, 3111, 1010, 31010, 23102, 11102, 103, 112, 10, 20103, 10103,
        1103, 1112, 3002, 21103, 10112, 3103, 3112, 2, 23103, 11103, 1001, 113, 4000, 23000,
        10113, 1002, 1113, 3003, 23001, 13101, 1011, 3113, 2000, 32000, 23002, 13102, 1003,
        3010, 5000, 23003, 13103, 1012, 3011, 11, 1013, 24000, 12100, 3012, 3, 2101, 22000,
        12101, 3013, 12, 2102, 22100, 12102, 4010, 13, 2103, 24100, 12103, 2010, 4001),
        (4101, 24001, 14100),
        (2110, 32110, 4002, 2003),
        (24002, 12110, 4110, 4003),
        (4102, 24003, 14101),
        (4011, 5010, 2001, 22003, 14102, 4012, 4103, 22001, 14103, 4013, 5101, 24101, 15100,
        2013, 5001, 2002, 22002, 15101, 2011, 5011, 5102, 24102, 15102, 4111, 5002, 2113, 24103,
        12113, 2012, 5003, 2111, 25100, 12111, 4112),
        (5012,),
        (5103, 25101, 15103),
        (4113, 5013),
        (25102, 2112, 12112, 5110),
        (25103,),
        (5111,),
        (5112,),
        (),
        (5113,),
        (),
        (),
        (),
        (),
        (),
        (),
    ),
    (
        (30100, 40100, 20100, 10100, 31100, 41100, 21100, 11100, 33100, 43100, 23100, 13100, 0,
        101, 100, 1100, 2100, 3100, 4100, 5100, 102, 110, 30102, 40101, 20101, 10101, 1101,
        1102, 1110, 3000, 31102, 41101, 20102, 10102, 3101, 3102, 3110, 1000, 33102, 43101,
        21101, 10110, 2101, 103, 111, 1, 30103, 41000, 20103, 10103, 1103, 4101, 112, 3001,
        42100, 31103, 21102, 10111, 3103, 1001, 1111, 3002, 41001, 33103, 21103, 10112, 1002,
        5101, 113, 1010, 41010, 23101, 31000, 10113, 2102, 1112, 3003, 1011, 41011, 23102,
        31002, 11101, 1003, 1113, 2, 42101, 31010, 23103, 11102, 1012, 3111, 10, 44100, 31003,
        23000, 11103, 1013, 3112, 11, 31012, 44101, 23001, 13101, 2103, 3113, 3, 31013, 45100,
        23002, 13102, 4102, 3010, 12, 32100, 45101, 23003, 13103, 4103, 3011, 13, 32102, 2001,
        42001, 22001, 12100, 5102, 3012, 4000, 32103, 24000, 12101, 5103, 3013, 4001, 34100,
        24001, 12102, 2003, 2011, 4002, 32003, 24002, 12103, 4010, 4003, 34102),
        (24003, 14100),
        (4011, 2000, 42000, 32000),
        (22003, 14101, 4012, 5000, 34103),
        (22000, 14102),
        (4013, 5001, 35100, 2111, 42111, 2002, 22002, 12111, 2013, 5010, 32002, 22100, 14103,
        2010, 5002, 35102, 24100, 15100, 2113, 2012, 5011, 32113, 24101, 12113, 2110, 42110,
        5003, 32110, 24102, 12110, 4110, 5012, 35103, 24103, 15101, 4111, 5013, 2112, 32112,
        25100, 12112, 4112),
        (),
        (25101, 15102),
        (4113,),
        (25102, 15103, 5110),
        (25103,),
        (5111,),
        (5112,),
        (),
        (5113,),
        (),
        (),
        (),
        (),
        (),
        (),
    ),
)

SUMS = (
    (
        (),
        (),
        (),
        (),
        (),
        (),
        (),
        (4110,),
        (5100, 4113),
        (5113,),
        (),
        (2101, 4112),
        (),
        (5103, 2113),
        (4111, 5112),
        (2103, 3113),
        (5102, 2112),
        (3112,),
        (5111, 2102),
        (3111, 5101),
        (4103,),
        (3110, 5110),
        (4102,),
        (113,),
        (4101,),
        (112,),
        (),
        (2111,),
        (111,),
        (3103,),
        (4013,),
        (3102,),
        (4012,),
        (),
        (2013,),
        (4011, 103),
        (2003,),
        (4010, 102),
        (2012,),
        (3013, 101),
        (2002, 3012),
        (2100,),
        (4003, 3011),
        (),
        (2110, 4002, 5013),
        (4001,),
        (3010, 1100, 2011, 1113, 5012, 2001, 4100, 110, 3003, 1103, 5011, 3002, 1112, 13, 1102,
        5003, 5010, 1111, 5002, 1013, 3100, 3001, 1012, 1101, 5001, 12, 1110, 3101, 1011, 100,
        11, 1010, 1003, 10, 1002, 1001, 2010, 3, 4000, 2000, 5000, 2, 1, 3000, 1000, 0),
    ),
    (
        (),
        (),
        (),
        (),
        (),
        (),
        (),
        (4111,),
        (5101, 4113),
        (5113,),
        (),
        (4112,),
        (),
        (5103,),
        (4110, 5111),
        (3113,),
        (5112,),
        (3111,),
        (5102,),
        (3112, 5110),
        (),
        (3110, 5100),
        (2113,),
        (113,),
        (2103,),
        (111,),
        (),
        (2112,),
        (112,),
        (2102,),
        (4013,),
        (2101, 4103),
        (4011,),
        (),
        (2111, 4102),
        (4012, 103),
        (),
        (4010, 101),
        (),
        (2110, 3013),
        (4101, 3103, 2100, 3011),
        (),
        (3102, 4100, 3012),
        (),
        (2013, 102, 5013),
        (),
        (2003, 3010, 1101, 2012, 1113, 5011, 3101, 2002, 1103, 5012, 4003, 1111, 110, 2011,
        1112, 4002, 5010, 1102, 2001, 13, 1110, 1013, 1100, 1011, 4001, 3003, 1012, 3002, 11,
        100, 5003, 12, 5002, 1010, 10, 3001, 2010, 4000, 5001, 3100, 5000, 1003, 1002, 2000,
        3000, 3, 1001, 1000, 2, 1, 0),
    ),
    (
        (),
        (),
        (),
        (),
        (),
        (),
        (),
        (4110,),
        (4113,),
        (),
        (),
        (2101, 4112),
        (),
        (2113,),
        (4111,),
        (2103, 3113),
        (2112,),
        (3112,),
        (2102,),
        (3111,),
        (4103,),
        (3110,),
        (4102,),
        (113,),
        (4101,),
        (112,),
        (),
        (2111,),
        (111,),
        (3103,),
        (4013,),
        (5000, 3102),
        (4012, 5013),
        (),
        (2013,),
        (4011,),
        (5003, 2003),
        (4010, 5012),
        (2012,),
        (3013, 5002),
        (2002, 3012),
        (5011,),
        (4003, 3011, 5001),
        (),
        (4002, 3010, 5010),
        (4001,),
        (110, 1013, 2011, 5113, 1003, 2001, 5112, 1012, 3003, 1002, 5111, 3002, 1011, 2110,
        3001, 1001, 13, 103, 1010, 1113, 1000, 102, 4100, 5110, 101, 12, 2100, 2010, 3101, 1112,
        2000, 5103, 11, 3, 5102, 1111, 3100, 1103, 10, 4000, 1102, 1110, 5101, 2, 1101, 1, 3000,
        0, 100, 5100, 1100),
    ),
    (
        (),
        (),
        (),
        (),
        (),
        (),
        (),
        (4111,),
        (4113,),
        (),
        (),
        (4112,),
        (),
        (),
        (4110,),
        (3113,),
        (),
        (3111,),
        (),
        (3112,),
        (),
        (3110,),
        (2113,),
        (113,),
        (2103,),
        (111,),
        (),
        (2112,),
        (112,),
        (2102,),
        (4013,),
        (5001, 2101, 4103),
        (4011, 5013),
        (),
        (2111, 4102),
        (4012,),
        (5003,),
        (4010, 5011),
        (),
        (3013, 5012),
        (4101, 3103, 3011),
        (5002,),
        (3102, 3012, 5010),
        (),
        (2013, 3010, 5000),
        (),
        (2003, 110, 1013, 2012, 2110, 1003, 3101, 2002, 5113, 1011, 4003, 1012, 4100, 5111,
        2011, 4002, 1001, 5112, 2100, 2001, 1002, 5110, 1010, 1113, 1000, 13, 2010, 4001, 3003,
        1111, 4000, 3002, 1112, 2000, 11, 103, 1110, 12, 102, 3001, 10, 3000, 3, 5103, 101,
        5102, 1, 1103, 100, 2, 1102, 0, 3100, 5101, 1101, 5100, 1100),
    ),
)

ORDERS = {
    (0, 0): "zxy",
    (0, 1): "zxy",
    (1, 0): "zyx",
    (1, 1): "zyx",
    (2, 0): "yxz",
    (2, 1): "yxz",
    (3, 0): "xzy",
    (3, 1): "xzy",
    (4, 0): "xzy",
    (4, 1): "xzy",
    (5, 0): "zyx",
    (5, 1): "zyx",
}


def gather(blocks):
    return [
        lax.all_gather(lax.all_gather(block, "dp", axis=0, tiled=True), "section", axis=0)
        for block in blocks
    ]


def scatter(partials):
    results = []
    for pair in partials:
        both = lax.psum_scatter(jnp.stack(pair), "section", scatter_dimension=0, tiled=False)
        results.append(
            lax.psum_scatter(both.astype(F32), "dp", scatter_dimension=0, tiled=True)
        )
    return results


def norm_back(grad, unit, scale, gain):
    scaled = grad * gain
    inner = scaled - jnp.mean(scaled, axis=-1, keepdims=True)
    inner = inner - unit * jnp.mean(scaled * unit, axis=-1, keepdims=True)
    return jnp.sum(grad * unit, axis=0), jnp.sum(grad, axis=0), scale * inner


def by_head(rows):
    return rows.reshape(rows.shape[0], -1, HD)


def forward(hidden, weights, shared, allowed):
    query_key, value, out, up, down, first, norms = weights
    unit_one, scale_one = normalized(hidden)
    normed = (unit_one * norms[0] + norms[1]).astype(BF)
    qk = product(normed, query_key).astype(BF)
    fresh = product(normed, value).astype(BF)
    if shared is None:
        shared = product(normed, first).astype(BF)
    features = hidden.shape[1]
    queries, keys = by_head(qk[:, :features]), by_head(qk[:, features:])
    values = by_head(jnp.concatenate([fresh, shared], axis=1))
    scores = jnp.einsum("qhd,khd->hqk", queries, keys, preferred_element_type=F32) * HD**-0.5
    scores = jnp.where(allowed, scores, -1e30)
    raised = jnp.exp(scores - jnp.max(scores, axis=-1, keepdims=True))
    soft = raised / jnp.sum(raised, axis=-1, keepdims=True)
    probs = soft.astype(BF)
    attended = jnp.einsum("hqk,khd->qhd", probs, values, preferred_element_type=F32)
    attended = attended.reshape(hidden.shape).astype(BF)
    middle = hidden + product(attended, out)
    unit_two, scale_two = normalized(middle)
    mixed = (unit_two * norms[2] + norms[3]).astype(BF)
    upper = product(mixed, up)
    active = jax.nn.gelu(upper, approximate=True).astype(BF)
    output = middle + product(active, down)
    kept = (normed, queries, keys, values, soft, attended, unit_one, scale_one)
    return output, shared, kept + (unit_two, scale_two, mixed, upper, active)


def backward(grad, weights, kept, grad_shared_next):
    query_key, value, out, up, down, first, norms = weights
    normed, queries, keys, values, soft, attended, unit_one, scale_one = kept[:8]
    unit_two, scale_two, mixed, upper, active = kept[8:]
    positions, features = grad.shape
    half = value.shape[1]
    grad_low = grad.astype(BF)
    down_grad = transposed_times(active, grad_low)
    _, gelu_pull = jax.vjp(lambda u: jax.nn.gelu(u, approximate=True), upper)
    grad_upper = gelu_pull(times_transposed(grad_low, down))[0].astype(BF)
    up_grad = transposed_times(mixed, grad_upper)
    grad_mixed = times_transposed(grad_upper, up)
    two_gain, two_bias, through = norm_back(grad_mixed, unit_two, scale_two, norms[2])
    grad_middle = grad + through
    grad_attn = grad_middle.astype(BF)
    out_grad = transposed_times(attended, grad_attn)
    grad_attended = by_head(times_transposed(grad_attn, out).astype(BF))
    grad_soft = jnp.einsum("qhd,khd->hqk", grad_attended, values, preferred_element_type=F32)
    grad_values = jnp.einsum(
        "hqk,qhd->khd", soft.astype(BF), grad_attended, preferred_element_type=F32
    ).reshape(positions, features)
    grad_scores = soft * (grad_soft - jnp.sum(soft * grad_soft, axis=-1, keepdims=True))
    grad_scores = grad_scores.astype(BF)
    grad_queries = jnp.einsum("hqk,khd->qhd", grad_scores, keys, preferred_element_type=F32)
    grad_keys = jnp.einsum("hqk,qhd->khd", grad_scores, queries, preferred_element_type=F32)
    grad_qk = jnp.concatenate(
        [grad_queries.reshape(positions, features), grad_keys.reshape(positions, features)], axis=1
    )
    grad_qk = (grad_qk * HD**-0.5).astype(BF)
    grad_fresh = grad_values[:, :half].astype(BF)
    grad_shared = grad_values[:, half:]
    grad_normed = times_transposed(grad_qk, query_key) + times_transposed(grad_fresh, value)
    if grad_shared_next is not None:
        grad_shared = (grad_shared + grad_shared_next.astype(F32)).astype(BF)
        first_grad = transposed_times(normed, grad_shared)
        grad_normed = grad_normed + times_transposed(grad_shared, first)
    else:
        grad_shared = grad_shared.astype(BF)
        first_grad = None
    one_gain, one_bias, through = norm_back(grad_normed, unit_one, scale_one, norms[0])
    grad_input = (grad_middle + through).astype(BF)
    query_key_grad = transposed_times(normed, grad_qk)
    value_grad = transposed_times(normed, grad_fresh)
    gains = jnp.stack([one_gain, one_bias, two_gain, two_bias], axis=1)
    return grad_input, grad_shared, (
        query_key_grad, value_grad, out_grad, up_grad, down_grad, first_grad, gains
    )


def swapped(block):
    return lax.ppermute(block, "section", [(0, 1), (1, 0)])


def on_any_mesh(
    inputs,
    cotangent,
    lengths,
    norm_one_gain,
    norm_one_bias,
    query_key_weight,
    value_weight,
    out_weight,
    norm_two_gain,
    norm_two_bias,
    up_weight,
    down_weight,
    first_value_weight,
):
    section = lax.axis_index("section")
    first_half = section == 0
    half = value_weight.shape[2]
    features = out_weight.shape[2]
    quarter = first_value_weight.shape[1]
    own_rows = query_key_weight.shape[1]
    norms = jnp.stack([norm_one_gain[0], norm_one_bias[0], norm_two_gain[0], norm_two_bias[0]], axis=1)
    padding = -(half + features + quarter + 4) % 128
    attention = jnp.concatenate(
        [
            value_weight[0],
            out_weight[0],
            first_value_weight,
            norms,
            jnp.zeros((own_rows, padding), BF),
        ],
        axis=1,
    )
    whole = gather([query_key_weight[0], attention, up_weight[0], down_weight[0]])
    after = half + features
    first_matrix = jnp.concatenate(
        [whole[1][0, :, after : after + quarter], whole[1][1, :, after : after + quarter]], axis=1
    )

    def layer_weights(layer):
        packed = whole[1][layer]
        gains = packed[:, after + quarter : after + quarter + 4].astype(F32).T
        return (
            whole[0][layer],
            packed[:, :half],
            packed[:, half:after],
            whole[2][layer],
            whole[3][layer],
            first_matrix,
            gains,
        )

    weights = [layer_weights(0), layer_weights(1)]
    batch_sequences, positions = inputs.shape[1:3]
    hidden = lax.dynamic_index_in_dim(inputs, section, 0, keepdims=False)[0]
    grad = lax.dynamic_index_in_dim(cotangent, section, 0, keepdims=False)[0]
    length = lax.dynamic_index_in_dim(lengths, section, 0, keepdims=False)[0]
    places = jnp.arange(positions)
    live = places < length
    allowed = (places[None, :] <= places[:, None]) & live[None, :]
    output_one, shared, kept_one = forward(hidden.astype(F32), weights[0], None, allowed)
    low_one = output_one.astype(BF)
    output_two, _, kept_two = forward(low_one.astype(F32), weights[1], shared, allowed)
    low_two = output_two.astype(BF)
    outputs_there = swapped(jnp.where(first_half, low_two, low_one))
    outputs_here = jnp.where(first_half, low_one, low_two)
    grad = jnp.where(live[:, None], grad.astype(F32), 0.0)
    grad_one, grad_shared, sums_two = backward(grad, weights[1], kept_two, None)
    grad_zero, _, sums_one = backward(grad_one.astype(F32), weights[0], kept_one, grad_shared)
    grads_there = swapped(jnp.where(first_half, grad_one, grad_zero))
    grads_here = jnp.where(first_half, grad_zero, grad_one)
    first_grad = sums_one[5]

    def packed_sums(sums, first_part):
        return jnp.concatenate(
            [
                sums[1],
                sums[2],
                first_part,
                sums[6],
                jnp.zeros((first_part.shape[0], padding), F32),
            ],
            axis=1,
        ).astype(BF)

    partials = [
        (sums_one[0].astype(BF), sums_two[0].astype(BF)),
        (
            packed_sums(sums_one, first_grad[:, :quarter]),
            packed_sums(sums_two, first_grad[:, quarter:]),
        ),
        (sums_one[3].astype(BF), sums_two[3].astype(BF)),
        (sums_one[4].astype(BF), sums_two[4].astype(BF)),
    ]
    query_key_grad, packed_grad, up_grad, down_grad = scatter(partials)
    gains = packed_grad[:, after + quarter : after + quarter + 4].T

    def both(here, there):
        return jnp.stack(
            [jnp.where(first_half, here, there), jnp.where(first_half, there, here)]
        )[None, :, None]

    return (
        both(outputs_here, outputs_there),
        both(grads_here, grads_there),
        gains[0][None],
        gains[1][None],
        query_key_grad[None],
        packed_grad[:, :half][None],
        packed_grad[:, half:after][None],
        gains[2][None],
        gains[3][None],
        up_grad[None],
        down_grad[None],
        packed_grad[:, after : after + quarter],
    )


def on_device(
    tables,
    inputs,
    cotangent,
    lengths,
    norm_one_gain,
    norm_one_bias,
    query_key_weight,
    value_weight,
    out_weight,
    norm_two_gain,
    norm_two_bias,
    up_weight,
    down_weight,
    first_value_weight,
):
    gather_schedule, sum_schedule, sum_orders = tables
    first_half = lax.axis_index("section") == 0
    norms = jnp.stack([norm_one_gain[0], norm_one_bias[0], norm_two_gain[0], norm_two_bias[0]], axis=1)
    filler = jnp.zeros((norms.shape[0], PACK - NORMS - 4), BF)
    pack = jnp.concatenate(
        [value_weight[0], out_weight[0], first_value_weight, norms, filler], axis=1
    )
    own = (query_key_weight, pack[None], up_weight, down_weight)
    done = forward_call(gather_schedule, own, inputs, lengths)
    weights, kept, turned = done[:4], done[4:10], done[10:14]
    back = backward_call(
        sum_schedule, sum_orders, weights, kept, turned, inputs, cotangent, lengths
    )
    query_key_grad, pack_grad, up_grad, down_grad, grads, low_there, grad_there = back

    def both(mine, there):
        here = jnp.where(first_half, mine[0], mine[1])
        return jnp.stack(
            [jnp.where(first_half, here, there), jnp.where(first_half, there, here)]
        )[None, :, None]

    vectors = pack_grad[:, NORMS : NORMS + 4].T
    return (
        both(kept[5], low_there),
        both(grads, grad_there),
        vectors[0][None],
        vectors[1][None],
        query_key_grad[None],
        pack_grad[:, :HALF][None],
        pack_grad[:, HALF:FIRST][None],
        vectors[2][None],
        vectors[3][None],
        up_grad[None],
        down_grad[None],
        pack_grad[:, FIRST:NORMS],
    )


def solution(mesh):
    placed = (
        P(None, "dp", None, None),
        P(None, "dp", None, None),
        P(None, "dp"),
        P("section", "dp"),
        P("section", "dp"),
        P("section", "dp", None),
        P("section", "dp", None),
        P("section", "dp", None),
        P("section", "dp"),
        P("section", "dp"),
        P("section", "dp", None),
        P("section", "dp", None),
        P("dp", "section"),
    )
    if mesh.shape["dp"] == 16 and mesh.shape["section"] == 2:
        sums = [[[item[1:] for item in items] for items in k] for k in schedule_of(SUMS)]
        body = functools.partial(on_device, (schedule_of(GATHER), sums, ORDERS))
    else:
        body = on_any_mesh
    return jax.shard_map(
        body,
        mesh=mesh,
        in_specs=placed,
        out_specs=(
            P("section", None, "dp", None, None),
            P("section", None, "dp", None, None),
            P("section", "dp"),
            P("section", "dp"),
            P("section", "dp", None),
            P("section", "dp", None),
            P("section", "dp", None),
            P("section", "dp"),
            P("section", "dp"),
            P("section", "dp", None),
            P("section", "dp", None),
            P("dp", "section"),
        ),
        check_vma=False,
    )
```

```python
import functools

import jax
import jax.numpy as jnp
from jax import lax
from jax.experimental import pallas as pl
from jax.experimental.pallas import tpu as pltpu
from jax.sharding import PartitionSpec as P

HEADS = 12
HD = 64
EPSILON = 1e-05
BF = jnp.bfloat16
F32 = jnp.float32
MESH = pl.DeviceIdType.MESH
LEN = 256
FEATURES = 768
HALF = 384
HIDDEN = 3072
PACK = 1408
FIRST = HALF + FEATURES
NORMS = FIRST + 192
LINKS = ("x", "y", "near", "far")


class Place:
    def __init__(self):
        self.s = lax.axis_index("section")
        dp = lax.axis_index("dp")
        self.z = dp // 4
        self.y = (dp // 2) % 2
        self.c = dp % 2
        self.mid = (self.z == 1) | (self.z == 2)

    def device(self, s, z, y, c):
        return (s, z * 4 + y * 2 + c)

    def neighbour(self, link):
        s, z, y, c = self.s, self.z, self.y, self.c
        if link == "x":
            return self.device(1 - s, z, y, c)
        if link == "y":
            return self.device(s, z, 1 - y, c)
        if link == "near":
            return self.device(s, z + 1 - 2 * (z % 2), y, c)
        if link == "far":
            return self.device(s, 3 - z, y, c)
        return self.device(s, z, y, 1 - c)

    def along_z(self, j):
        z = self.z
        return (z, z + 1 - 2 * (z % 2), 2 - z // 2, 3 - 3 * (z // 2))[j]

    def block(self, ry, j):
        y = self.y if ry == 0 else 1 - self.y
        return self.along_z(j) * 2 + y

    def is_class(self, k):
        middle = self.mid if k % 2 else jnp.logical_not(self.mid)
        return (self.s == k // 2) & middle


def greet(place):
    barrier = pltpu.get_barrier_semaphore()
    for link in ("x", "y", "near", "core"):
        pl.semaphore_signal(barrier, 1, device_id=place.neighbour(link), device_id_type=MESH)

    @pl.when(place.mid)
    def _():
        pl.semaphore_signal(barrier, 1, device_id=place.neighbour("far"), device_id_type=MESH)


def meet(place):
    barrier = pltpu.get_barrier_semaphore()

    @pl.when(place.mid)
    def _():
        pl.semaphore_wait(barrier, 5)

    @pl.when(jnp.logical_not(place.mid))
    def _():
        pl.semaphore_wait(barrier, 4)


def remote(source, target, send_sem, recv_sem, device):
    return pltpu.make_async_remote_copy(
        src_ref=source,
        dst_ref=target,
        send_sem=send_sem,
        recv_sem=recv_sem,
        device_id=device,
        device_id_type=MESH,
    )


def product(left, right):
    return jnp.dot(left, right, preferred_element_type=F32)


def times_transposed(left, right):
    return lax.dot_general(left, right, (((1,), (1,)), ((), ())), preferred_element_type=F32)


def transposed_times(left, right):
    return lax.dot_general(left, right, (((0,), (0,)), ((), ())), preferred_element_type=F32)


def normalized(rows):
    average = jnp.mean(rows, axis=-1, keepdims=True)
    centred = rows - average
    scale = lax.rsqrt(jnp.mean(centred * centred, axis=-1, keepdims=True) + EPSILON)
    return centred * scale, scale


def lane_index(shape):
    return lax.broadcasted_iota(jnp.int32, shape, 1)


def flat(block):
    return block.reshape(-1, block.shape[-1])


ARRAY_OF = (0, 1, 2, 2, 3, 3)
ROWS = (48, 48, 48, 192)
WIDTH = (2 * FEATURES, PACK, HIDDEN, FEATURES)


def piece_of(ref, g):
    lead = (slice(None),) * (len(ref.shape) - 2)
    if g in (2, 3):
        return ref.at[lead + (slice(None), pl.ds((g - 2) * (HIDDEN // 2), HIDDEN // 2))]
    if g in (4, 5):
        return ref.at[lead + (pl.ds((g - 4) * 96, 96), slice(None))]
    return ref


def forward_kernel(
    schedule,
    own_qk, own_value, own_out, own_up, own_down, first, vector_0, vector_1, vector_2, vector_3,
    inputs, length,
    out_qk, out_pack, out_up, out_down,
    kept_qk, kept_values, kept_probs, kept_slope, kept_middle, kept_low,
    turned_normed, turned_attended, turned_mixed, turned_active, swapped_one,
    w_qk, w_pack, w_up, w_down, own_pack,
    x_ref, normed, qk, values, probs, attended, middle, mixed, active, slope, low,
    t_normed, t_attended, t_mixed, t_active,
    recv_sem, send_sem, core_send, core_recv, local_sem, keep_sem, turn_send, turn_recv, fetch_sem, swap_sem,
):
    place = Place()
    s, c = place.s, place.c
    own = (own_qk.at[0], own_pack, own_up.at[0], own_down.at[0])
    whole = (w_qk, w_pack, w_up, w_down)
    whole_out = (out_qk, out_pack, out_up, out_down)

    greet(place)
    fetch = pltpu.make_async_copy(inputs.at[s, 0], x_ref, fetch_sem.at[0])
    fetch.start()
    packing = [
        pltpu.make_async_copy(own_value.at[0], own_pack.at[:, 0:HALF], fetch_sem.at[1]),
        pltpu.make_async_copy(own_out.at[0], own_pack.at[:, HALF:FIRST], fetch_sem.at[2]),
    ]
    for one in packing:
        one.start()
    tall = jnp.concatenate(
        [jnp.zeros((64, 48), F32)]
        + [vector[...].astype(F32) for vector in (vector_0, vector_1, vector_2, vector_3)]
        + [jnp.zeros((60, 48), F32)],
        axis=0,
    )
    own_pack[:, FIRST : FIRST + 128] = first[:, :128]
    own_pack[:, FIRST + 128 :] = tall.T.astype(BF)
    own_pack[:, FIRST + 128 : NORMS] = first[:, 128:]

    def spot(g, layer, ry, j):
        return piece_of(whole[ARRAY_OF[g]].at[layer, place.block(ry, j), c], g)

    mine = [
        pltpu.make_async_copy(
            piece_of(own[ARRAY_OF[g]], g), spot(g, s, 0, 0), local_sem.at[g]
        )
        for g in range(6)
    ]
    for g, one in enumerate(mine):
        if g != 1:
            one.start()
    meet(place)

    def weight_copy(k, item):
        link, g, layer, ry, j = item
        target = spot(g, layer, ry, j)
        source = target
        if (ry, j) == (0, 0) and layer == k // 2:
            source = piece_of(own[ARRAY_OF[g]], g)
        return remote(
            source,
            target,
            send_sem.at[LINKS.index(link), g, layer, ry * 4 + j],
            recv_sem.at[g, layer, place.block(ry, j)],
            place.neighbour(link),
        )

    def hand_over(g, layer):
        part = piece_of(whole[ARRAY_OF[g]].at[layer, :, c], g)
        return remote(
            part, part, core_send.at[g, layer], core_recv.at[g, layer], place.neighbour("core")
        )

    def from_core(g, layer):
        part = piece_of(whole[ARRAY_OF[g]].at[layer, :, 1 - c], g)
        return remote(
            part, part, core_send.at[g, layer], core_recv.at[g, layer], place.neighbour("core")
        )

    missing = [{(g, l): 8 for g in range(6) for l in range(2)} for k in range(4)]
    begun = [set() for k in range(4)]

    packed = [False] * 4

    def run_items(k, items):
        for item in items:
            link, g, layer, ry, j = item
            if (g, layer, ry, j) == (1, k // 2, 0, 0) and not packed[k]:
                packed[k] = True
                for one in packing:
                    one.wait()
                mine[1].start()
            if link is not None:
                weight_copy(k, item).start()
                continue
            if (ry, j) == (0, 0) and layer == k // 2:
                mine[g].wait()
            else:
                remote(
                    spot(g, layer, ry, j),
                    spot(g, layer, ry, j),
                    send_sem.at[0, 0, 0, 0],
                    recv_sem.at[g, layer, place.block(ry, j)],
                    place.neighbour("x"),
                ).wait_recv()
            missing[k][g, layer] -= 1
            if missing[k][g, layer] == 0:
                hand_over(g, layer).start()

    swap = remote(low.at[0], swapped_one, swap_sem.at[0], swap_sem.at[1], place.neighbour("x"))
    kept = []

    def keep(source, target):
        copy = pltpu.make_async_copy(source, target, keep_sem.at[len(kept)])
        kept.append(copy)
        copy.start()

    turned = []

    def turn_over(number, layer, source, target):
        copy = pltpu.make_async_copy(source.at[:, c], target.at[layer, 0], keep_sem.at[len(kept)])
        kept.append(copy)
        copy.start()
        other = remote(
            source.at[:, 1 - c],
            target.at[layer, 1],
            turn_send.at[number, layer],
            turn_recv.at[number, layer],
            place.neighbour("core"),
        )
        other.start()
        turned.append(other)

    def norm_vectors(layer):
        window = flat(w_pack[layer, :, :, :, NORMS - 64 : NORMS + 64]).astype(F32)
        rows = window.T
        return [rows[64 + i : 65 + i, :] for i in range(4)]

    def residual(layer):
        return (x_ref if layer == 0 else low.at[0])[...].astype(F32)

    def front(layer):
        for g, l in ((0, 0), (1, 0), (1, 1)) if layer == 0 else ((0, 1),):
            from_core(g, l).wait_recv()
            keep(whole[g].at[l], whole_out[g].at[l])
        if layer == 0:
            fetch.wait()
        vectors = norm_vectors(layer)
        unit, _ = normalized(residual(layer))
        rows = (unit * vectors[0] + vectors[1]).astype(BF)
        normed[...] = rows
        for i in range(3):
            at = slice(i * 512, (i + 1) * 512)
            qk[layer, :, at] = product(rows, flat(w_qk[layer, :, :, :, at])).astype(BF)
        keep(qk.at[layer], kept_qk.at[layer])
        values[layer, :, :HALF] = product(rows, flat(w_pack[layer, :, :, :, :HALF])).astype(BF)
        if layer == 0:
            window = slice(FIRST, FIRST + 256)
            part = [product(rows, flat(w_pack[l, :, :, :, window])) for l in range(2)]
            moved = pltpu.roll(part[1], 64, 1)
            between = jnp.where(lane_index((LEN, 128)) < 64, part[0][:, 128:], moved[:, :128])
            values[0, :, HALF : HALF + 128] = part[0][:, :128].astype(BF)
            values[0, :, HALF + 128 : HALF + 256] = between.astype(BF)
            values[0, :, HALF + 256 :] = moved[:, 128:].astype(BF)
        else:
            values[1, :, HALF:] = values[0, :, HALF:]
        keep(values.at[layer], kept_values.at[layer])
        t_normed[layer] = rows.T.reshape(8, 2, 48, LEN)
        turn_over(0, layer, t_normed.at[layer], turned_normed)

    def attend(layer, pairs):
        count = length[s]
        key = lax.broadcasted_iota(jnp.int32, (LEN, LEN), 0)
        query = lax.broadcasted_iota(jnp.int32, (LEN, LEN), 1)
        allowed = (key <= query) & (key < count)
        left = lane_index((LEN, 128)) < 64
        for pair in pairs:
            at = slice(pair * 128, (pair + 1) * 128)
            queries = qk[layer, :, at] * jnp.asarray(HD**-0.5, BF)
            keys = qk[layer, :, FEATURES + pair * 128 : FEATURES + (pair + 1) * 128]
            head_values = values[layer, :, at]
            parts = []
            for head in range(2):
                chosen = left if head == 0 else jnp.logical_not(left)
                scores = times_transposed(jnp.where(chosen, keys, jnp.zeros_like(keys)), queries)
                scores = jnp.where(allowed, scores, -1e30)
                raised = jnp.exp(scores - jnp.max(scores, axis=0, keepdims=True))
                soft = (raised / jnp.sum(raised, axis=0, keepdims=True)).astype(BF)
                probs[layer, 2 * pair + head] = soft
                parts.append(transposed_times(soft, head_values))
            attended[:, at] = jnp.where(left, parts[0], parts[1]).astype(BF)

    def project_out(layer):
        keep(probs.at[layer], kept_probs.at[layer])
        rows = attended[...]
        total = residual(layer) + product(
            rows, flat(w_pack[layer, :, :, :, HALF : HALF + FEATURES])
        )
        middle[layer] = total
        keep(middle.at[layer], kept_middle.at[layer])
        vectors = norm_vectors(layer)
        unit, _ = normalized(total)
        after = (unit * vectors[2] + vectors[3]).astype(BF)
        mixed[...] = after
        t_attended[layer] = rows.T.reshape(8, 2, 48, LEN)
        turn_over(1, layer, t_attended.at[layer], turned_attended)
        t_mixed[layer] = after.T.reshape(8, 2, 48, LEN)
        turn_over(2, layer, t_mixed.at[layer], turned_mixed)

    def widen(layer, i):
        if i % 2 == 0:
            from_core(2 + i // 2, layer).wait_recv()
        at = slice(i * 768, (i + 1) * 768)
        upper = product(mixed[...], flat(w_up[layer, :, :, :, at]))
        inner = upper * (0.7978845608028654 + 0.03567740813636141 * (upper * upper))
        bent = jnp.tanh(inner)
        half = 0.5 * (1.0 + bent)
        grown = (upper * half).astype(BF)
        active[:, at] = grown
        steep = 0.7978845608028654 + 0.10703222440908423 * (upper * upper)
        slope[layer, :, at] = (half + 0.5 * upper * (1.0 - bent * bent) * steep).astype(BF)
        t_active[layer, 2 * i : 2 * i + 2] = grown.T.reshape(2, 2, 192, LEN)

    def narrow(layer):
        keep(slope.at[layer], kept_slope.at[layer])
        turn_over(3, layer, t_active.at[layer], turned_active)
        keep(w_up.at[layer], out_up.at[layer])
        from_core(4, layer).wait_recv()
        from_core(5, layer).wait_recv()
        keep(w_down.at[layer], out_down.at[layer])
        total = middle[layer] + product(active[...], flat(w_down[layer]))
        low[layer] = total.astype(BF)
        keep(low.at[layer], kept_low.at[layer])
        if layer == 0:
            pl.when(s == 1)(swap.start)

    steps = []
    for layer in range(2):
        steps.append(functools.partial(front, layer))
        for i in range(3):
            steps.append(functools.partial(attend, layer, (2 * i, 2 * i + 1)))
        steps.append(functools.partial(project_out, layer))
        for i in range(4):
            steps.append(functools.partial(widen, layer, i))
        steps.append(functools.partial(narrow, layer))

    for number in range(len(steps) + 1):
        for k in range(4):
            if schedule[k][number]:
                pl.when(place.is_class(k))(
                    functools.partial(run_items, k, schedule[k][number])
                )
        if number < len(steps):
            steps[number]()

    for k in range(4):

        def finish(k=k):
            for items in schedule[k]:
                for item in items:
                    if item[0] is not None:
                        weight_copy(k, item).wait_send()

        pl.when(place.is_class(k))(finish)
    for g in range(6):
        for layer in range(2):
            hand_over(g, layer).wait_send()
    for copy in kept:
        copy.wait()
    for copy in turned:
        copy.wait()
    pl.when(s == 0)(swap.wait_recv)
    pl.when(s == 1)(swap.wait_send)


def forward_call(schedule, own, small, inputs, length):
    def hbm(shape, dtype=BF):
        return jax.ShapeDtypeStruct(shape, dtype)

    def turn(rows):
        return (2, 2, 8, rows, LEN)

    weights = [(2, 8, 2, ROWS[a], WIDTH[a]) for a in range(4)]
    kept = [
        hbm((2, LEN, 2 * FEATURES)),
        hbm((2, LEN, FEATURES)),
        hbm((2, HEADS, LEN, LEN)),
        hbm((2, LEN, HIDDEN)),
        hbm((2, LEN, FEATURES), F32),
        hbm((2, LEN, FEATURES)),
    ]
    outs = [hbm(shape) for shape in weights] + kept
    outs += [hbm(turn(48)), hbm(turn(48)), hbm(turn(48)), hbm(turn(192)), hbm((LEN, FEATURES))]
    scratch = [pltpu.VMEM(shape, BF) for shape in weights]
    scratch += [
        pltpu.VMEM((48, PACK), BF),
        pltpu.VMEM((LEN, FEATURES), BF),
        pltpu.VMEM((LEN, FEATURES), BF),
        pltpu.VMEM((2, LEN, 2 * FEATURES), BF),
        pltpu.VMEM((2, LEN, FEATURES), BF),
        pltpu.VMEM((2, HEADS, LEN, LEN), BF),
        pltpu.VMEM((LEN, FEATURES), BF),
        pltpu.VMEM((2, LEN, FEATURES), F32),
        pltpu.VMEM((LEN, FEATURES), BF),
        pltpu.VMEM((LEN, HIDDEN), BF),
        pltpu.VMEM((2, LEN, HIDDEN), BF),
        pltpu.VMEM((2, LEN, FEATURES), BF),
        pltpu.VMEM((2, 8, 2, 48, LEN), BF),
        pltpu.VMEM((2, 8, 2, 48, LEN), BF),
        pltpu.VMEM((2, 8, 2, 48, LEN), BF),
        pltpu.VMEM((2, 8, 2, 192, LEN), BF),
        pltpu.SemaphoreType.DMA((6, 2, 8)),
        pltpu.SemaphoreType.DMA((4, 6, 2, 8)),
        pltpu.SemaphoreType.DMA((6, 2)),
        pltpu.SemaphoreType.DMA((6, 2)),
        pltpu.SemaphoreType.DMA((6,)),
        pltpu.SemaphoreType.DMA((32,)),
        pltpu.SemaphoreType.DMA((4, 2)),
        pltpu.SemaphoreType.DMA((4, 2)),
        pltpu.SemaphoreType.DMA((3,)),
        pltpu.SemaphoreType.DMA((2,)),
    ]
    anywhere = pl.BlockSpec(memory_space=pl.ANY)
    return pl.pallas_call(
        functools.partial(forward_kernel, schedule),
        out_shape=outs,
        in_specs=[anywhere] * 5
        + [pl.BlockSpec(memory_space=pltpu.VMEM)] * 5
        + [anywhere, pl.BlockSpec(memory_space=pltpu.SMEM)],
        out_specs=[anywhere] * len(outs),
        scratch_shapes=scratch,
        compiler_params=pltpu.CompilerParams(
            collective_id=0, has_side_effects=True, vmem_limit_bytes=62 * 2**20
        ),
    )(*own, *small, inputs, length)


def schedule_of(codes):
    result = []
    for per_class in codes:
        result.append([])
        for numbers in per_class:
            items = []
            for n in numbers:
                link = None if n < 10000 else LINKS[n // 10000 - 1]
                items.append((link, n // 1000 % 10, n // 100 % 10, n // 10 % 10, n % 10))
            result[-1].append(items)
    return result


def branches(order, rx, ry, j):
    apart = {"x": rx != 0, "y": ry != 0, "z": j != 0}
    last = max([i for i, axis in enumerate(order) if apart[axis]], default=-1)
    links = []
    for i, axis in enumerate(order):
        if i < last:
            continue
        if axis != "z":
            if i > last:
                links.append((axis, False))
        elif i > last:
            links += [("near", False), ("far", True)]
        else:
            links.append(("far" if j == 1 else "near", True))
    return links


def slot_table(orders):
    table, counts = {}, []
    for g in range(6):
        number = 0
        for rx in range(2):
            for ry in range(2):
                for j in range(4):
                    links = []
                    for layer in range(2):
                        for link, _ in branches(orders[g, layer], rx, ry, j):
                            if link not in links:
                                links.append(link)
                    for link in links:
                        table[g, rx, ry, j, link] = number
                        number += 1
        counts.append(number)
    return table, counts


def towards_owner(order, k, rx, ry, j):
    apart = {"x": rx != 0, "y": ry != 0, "z": j != 0}
    axis = [axis for axis in order if apart[axis]][-1]
    if axis == "x":
        return "x", (0, ry, j)
    if axis == "y":
        return "y", (rx, 0, j)
    if j == 1:
        return "near", (rx, ry, 0)
    if k % 2:
        return "far", (rx, ry, 0 if j == 2 else 1)
    return "near", (rx, ry, j)


def backward_kernel(
    schedule, order_of_steps, orders, slots,
    w_qk, w_pack, w_up, w_down,
    kept_qk, kept_values, kept_probs, kept_slope, kept_middle, kept_low,
    turned_normed, turned_attended, turned_mixed, turned_active,
    inputs, cotangent, length,
    out_qk, out_pack, out_up, out_down, out_grads, swapped_low, swapped_grad,
    m_qk, m_pack, m_wide,
    qk, values, probs, slope, middle, entering, t_normed, t_attended, t_mixed, t_active,
    cot,
    dy, du, da, dqk, dv,
    far_dy, far_du, far_da, far_dqk, far_dv,
    total, d_mixed, d_attended, shared_two, grads, vectors, far_vectors, columns,
    h_qk, h_pack, h_up, h_down,
    arrived_0, arrived_1, arrived_2, arrived_3, arrived_4, arrived_5,
    r_qk, r_pack, r_up, r_down,
    load_sem, pair_send, pair_recv, credit, swap_send, swap_recv, sum_send, sum_recv, out_sem,
):
    place = Place()
    s, c = place.s, place.c
    held = (h_qk, h_pack, h_up, h_down)
    arrived = (arrived_0, arrived_1, arrived_2, arrived_3, arrived_4, arrived_5)
    result = (r_qk, r_pack, r_up, r_down)
    outs = (out_qk, out_pack, out_up, out_down)

    sources = {
        "qk_matrix": (m_qk, lambda l: w_qk.at[l]),
        "pack0": (m_pack.at[0], lambda l: w_pack.at[0]),
        "pack1": (m_pack.at[1], lambda l: w_pack.at[1]),
        "down0": (m_wide.at[0:16], lambda l: w_down.at[l, pl.ds(0, 16)]),
        "down1": (m_wide.at[16:32], lambda l: w_down.at[l, pl.ds(16, 16)]),
        "down2": (m_wide.at[32:48], lambda l: w_down.at[l, pl.ds(32, 16)]),
        "down3": (m_wide.at[48:64], lambda l: w_down.at[l, pl.ds(48, 16)]),
        "up0": (m_wide.at[0:16], lambda l: w_up.at[l, :, :, pl.ds(0, 768)]),
        "up1": (m_wide.at[16:32], lambda l: w_up.at[l, :, :, pl.ds(768, 768)]),
        "up2": (m_wide.at[32:48], lambda l: w_up.at[l, :, :, pl.ds(1536, 768)]),
        "up3": (m_wide.at[48:64], lambda l: w_up.at[l, :, :, pl.ds(2304, 768)]),
        "qk": (qk, lambda l: kept_qk.at[l]),
        "values": (values, lambda l: kept_values.at[l]),
        "probs": (probs, lambda l: kept_probs.at[l]),
        "slope": (slope, lambda l: kept_slope.at[l]),
        "middle": (middle, lambda l: kept_middle.at[l]),
        "entering": (entering, lambda l: inputs.at[s, 0] if l == 0 else kept_low.at[0]),
        "normed": (t_normed, lambda l: turned_normed.at[l]),
        "attended": (t_attended, lambda l: turned_attended.at[l]),
        "mixed": (t_mixed, lambda l: turned_mixed.at[l]),
        "active": (t_active, lambda l: turned_active.at[l]),
        "cotangent": (cot, lambda l: cotangent.at[s, 0]),
    }
    names = list(sources)

    def loading(name, layer):
        target, source = sources[name]
        return pltpu.make_async_copy(
            source(layer), target, load_sem.at[names.index(name), layer]
        )

    def load(*which, layer):
        for name in which:
            loading(name, layer).start()

    def loaded(*which, layer):
        for name in which:
            loading(name, layer).wait()

    load("cotangent", "down0", "slope", "down1", "down2", "down3", layer=1)
    greet(place)

    across = place.neighbour("x")
    low_swap = remote(kept_low.at[1], swapped_low, swap_send.at[0], swap_recv.at[0], across)
    grad_swap = remote(grads.at[1 - s], swapped_grad, swap_send.at[1], swap_recv.at[1], across)

    shared = {
        "dy": (dy, far_dy),
        "du0": (du.at[:, 0:1536], far_du.at[:, 0:1536]),
        "du1": (du.at[:, 1536:3072], far_du.at[:, 1536:3072]),
        "da": (da, far_da),
        "dqk": (dqk, far_dqk),
        "dv": (dv, far_dv),
        "vectors": (vectors, far_vectors),
    }
    shared_names = list(shared)

    def exchange(name, layer):
        n = shared_names.index(name)
        return remote(
            *shared[name], pair_send.at[n, layer], pair_recv.at[n, layer], place.neighbour("core")
        )

    def hand(name, layer):
        if layer == 0:
            pl.semaphore_wait(credit.at[shared_names.index(name)], 1)
        exchange(name, layer).start()

    def done_with(name, layer):
        if layer == 1:
            pl.semaphore_signal(
                credit.at[shared_names.index(name)],
                1,
                device_id=place.neighbour("core"),
                device_id_type=MESH,
            )

    def free_to_write(name, layer):
        if layer == 0:
            exchange(name, 1).wait_send()

    def summed(left, right, far_right):
        return product(flat3(left[0]), right) + product(flat3(left[1]), far_right)

    def flat3(block):
        return block.reshape(-1, block.shape[-1])

    def norm_rows(layer):
        window = flat(m_pack[layer, :, :, :, NORMS - 64 : NORMS + 64]).astype(F32)
        rows = window.T
        return [rows[64 + i : 65 + i, :] for i in range(4)]

    def norm_back(grad, rows, gain):
        unit, scale = normalized(rows)
        scaled = grad * gain
        inner = scaled - jnp.mean(scaled, axis=-1, keepdims=True)
        inner = inner - unit * jnp.mean(scaled * unit, axis=-1, keepdims=True)
        return (
            jnp.sum(grad * unit, axis=0, keepdims=True),
            jnp.sum(grad, axis=0, keepdims=True),
            scale * inner,
        )

    def begin(layer):
        if layer == 1:
            vectors[...] = jnp.zeros_like(vectors)
            loaded("cotangent", layer=1)
            position = lax.broadcasted_iota(jnp.int32, (LEN, FEATURES), 0)
            grad = jnp.where(position < length[s], cot[...].astype(F32), 0.0)
        else:
            grad = grads[1].astype(F32)
        free_to_write("dy", layer)
        total[...] = grad
        dy[...] = grad.astype(BF)
        if layer == 0:
            hand("dy", layer)

    def through_active(layer, i):
        if i == 0:
            loaded("slope", layer=layer)
            if layer == 1:
                load("active", "mixed", "middle", "pack1", "qk", "values", layer=1)
                load("probs", "attended", "entering", "qk_matrix", "normed", layer=1)
                load("pack0", layer=0)
        if i % 2 == 0:
            free_to_write("du%d" % (i // 2), layer)
        loaded("down%d" % i, layer=layer)
        at = slice(i * 768, (i + 1) * 768)
        grad = times_transposed(dy[...], flat3(m_wide[16 * i : 16 * i + 16]))
        du[:, at] = (grad * slope[:, at].astype(F32)).astype(BF)
        if i == 0 and layer == 1:
            meet(place)
            hand("dy", layer)
            pl.when(s == 0)(low_swap.start)
        if i % 2 == 1:
            hand("du%d" % (i // 2), layer)
        if i == 3:
            load("up0", "up1", "up2", "up3", layer=layer)
            if layer == 1:
                load("slope", layer=0)

    def sum_down(layer, half):
        if half == 0:
            loaded("active", layer=layer)
            exchange("dy", layer).wait_recv()
        rows = slice(half * 96, half * 96 + 96)
        sums = summed(t_active[:, :, rows, :], dy[...], far_dy[...])
        h_down[layer, :, rows, :] = sums.astype(BF).reshape(8, 96, FEATURES)
        if half == 1:
            done_with("dy", layer)
            if layer == 1:
                load("active", layer=0)

    def to_mixed(layer):
        for q in range(4):
            loaded("up%d" % q, layer=layer)
            part = times_transposed(
                du[:, q * 768 : (q + 1) * 768], flat3(m_wide[16 * q : 16 * q + 16])
            )
            d_mixed[...] = part if q == 0 else d_mixed[...] + part
        if layer == 1:
            load("down0", "down1", "down2", "down3", layer=0)

    def sum_up(layer, q):
        if q == 0:
            loaded("mixed", layer=layer)
        if q % 2 == 0:
            exchange("du%d" % (q // 2), layer).wait_recv()
        at = slice(q * 768, (q + 1) * 768)
        sums = summed(t_mixed[...], du[:, at], far_du[:, at])
        h_up[layer, :, :, at] = sums.astype(BF).reshape(8, 48, 768)
        if q % 2 == 1:
            done_with("du%d" % (q // 2), layer)
        if q == 3 and layer == 1:
            load("mixed", layer=0)

    def second_norm(layer):
        loaded("middle", "pack%d" % layer, layer=layer)
        free_to_write("vectors", layer)
        free_to_write("da", layer)
        gain, bias, through = norm_back(d_mixed[...], middle[...], norm_rows(layer)[2])
        vectors[2:3, :] = gain
        vectors[3:4, :] = bias
        grad = total[...] + through
        total[...] = grad
        da[...] = grad.astype(BF)
        hand("da", layer)
        matrix = flat(m_pack[layer, :, :, :, HALF:FIRST])
        d_attended[...] = times_transposed(da[...], matrix).astype(BF)
        if layer == 1:
            load("middle", layer=0)

    def through_attention(layer, pair):
        if pair == 0:
            loaded("qk", "values", "probs", layer=layer)
            free_to_write("dqk", layer)
            free_to_write("dv", layer)
        left = lane_index((LEN, 128)) < 64
        at = slice(pair * 128, (pair + 1) * 128)
        key_at = slice(FEATURES + pair * 128, FEATURES + (pair + 1) * 128)
        queries, keys, head_values = qk[:, at], qk[:, key_at], values[:, at]
        grad = d_attended[:, at]
        parts = []
        for head in range(2):
            chosen = left if head == 0 else jnp.logical_not(left)
            soft = probs[2 * pair + head]
            to_soft = times_transposed(
                jnp.where(chosen, head_values, jnp.zeros_like(head_values)), grad
            )
            exact = soft.astype(F32)
            inner = jnp.sum(exact * to_soft, axis=0, keepdims=True)
            to_scores = (exact * (to_soft - inner)).astype(BF)
            parts.append(
                (
                    transposed_times(to_scores, keys),
                    product(to_scores, queries),
                    product(soft, grad),
                )
            )
        of_queries, of_keys, of_values = [
            jnp.where(left, one, other) for one, other in zip(*parts)
        ]
        dqk[:, at] = (of_queries * HD**-0.5).astype(BF)
        dqk[:, key_at] = (of_keys * HD**-0.5).astype(BF)
        if pair < 3:
            dv[:, at] = of_values.astype(BF)
        else:
            there = slice((pair - 3) * 128, (pair - 2) * 128)
            if layer == 1:
                shared_two[:, there] = of_values.astype(BF)
            else:
                dv[:, at] = (of_values + shared_two[:, there].astype(F32)).astype(BF)
        if pair == 5:
            hand("dqk", layer)
            hand("dv", layer)
            if layer == 1:
                load("qk", "values", "probs", layer=0)

    def first_window(part):
        if part == 0:
            window = lambda ref: ref[:, HALF : HALF + 256]
        else:
            window = lambda ref: pltpu.roll(
                ref[:, HALF + 128 :].astype(F32), 192, 1
            ).astype(BF)
        inside = lane_index((LEN, 256)) < 192
        return [
            jnp.where(inside, window(ref), jnp.zeros((LEN, 256), BF)) for ref in (dv, far_dv)
        ]

    def first_norm(layer):
        loaded("qk_matrix", "entering", layer=layer)
        grad = times_transposed(dqk[...], flat(m_qk[...]))
        grad = grad + times_transposed(dv[:, :HALF], flat(m_pack[layer, :, :, :, :HALF]))
        if layer == 0:
            for part in range(2):
                grad = grad + times_transposed(
                    first_window(part)[0], flat(m_pack[part, :, :, :, FIRST : FIRST + 256])
                )
        rows = entering[...].astype(F32)
        gain, bias, through = norm_back(grad, rows, norm_rows(layer)[0])
        vectors[0:1, :] = gain
        vectors[1:2, :] = bias
        hand("vectors", layer)
        grads[layer] = (total[...] + through).astype(BF)
        own_grads(layer).start()
        if layer == 1:
            load("qk_matrix", "entering", layer=0)
        pl.when(s == 1 - layer)(grad_swap.start)

    def sum_out(layer):
        loaded("attended", layer=layer)
        exchange("da", layer).wait_recv()
        sums = summed(t_attended[...], da[...], far_da[...])
        h_pack[layer, :, :, HALF:FIRST] = sums.astype(BF).reshape(8, 48, FEATURES)
        done_with("da", layer)
        if layer == 1:
            load("attended", layer=0)

    def sum_qk(layer):
        loaded("normed", layer=layer)
        exchange("dqk", layer).wait_recv()
        for q in range(2):
            at = slice(q * FEATURES, (q + 1) * FEATURES)
            sums = summed(t_normed[...], dqk[:, at], far_dqk[:, at])
            h_qk[layer, :, :, at] = sums.astype(BF).reshape(8, 48, FEATURES)
        done_with("dqk", layer)

    def sum_pack(layer):
        exchange("dv", layer).wait_recv()
        exchange("vectors", layer).wait_recv()
        sums = summed(t_normed[...], dv[:, :HALF], far_dv[:, :HALF])
        h_pack[layer, :, :, :HALF] = sums.astype(BF).reshape(8, 48, HALF)
        both = vectors[...] + far_vectors[...]
        nothing = jnp.zeros((64, FEATURES), F32)
        tall = jnp.concatenate([nothing, both, nothing[:56]], axis=0)
        columns[layer] = tall.T.astype(BF).reshape(8, 2, 48, 128)
        if layer == 0:
            for part in range(2):
                sums = summed(t_normed[...], *first_window(part)).reshape(8, 48, 256)
                h_pack[part, :, :, FIRST : FIRST + 128] = sums[:, :, :128].astype(BF)
                h_pack[part, :, :, FIRST + 128 :] = (
                    sums[:, :, 128:] + columns[part, :, c].astype(F32)
                ).astype(BF)
        done_with("dv", layer)
        done_with("vectors", layer)
        if layer == 1:
            load("normed", layer=0)

    def own_grads(layer):
        return pltpu.make_async_copy(grads.at[layer], out_grads.at[layer], out_sem.at[6 + layer])

    steps = []

    def step(action, *arguments):
        steps.append(functools.partial(action, *arguments))

    for layer in (1, 0):
        step(begin, layer)
        for i in range(4):
            step(through_active, layer, i)
        for half in range(2):
            step(sum_down, layer, half)
        step(to_mixed, layer)
        for q in range(4):
            step(sum_up, layer, q)
        step(second_norm, layer)
        for pair in range(6):
            step(through_attention, layer, pair)
        step(sum_out, layer)
        step(first_norm, layer)
        step(sum_qk, layer)
        step(sum_pack, layer)

    steps = [steps[number] for number in order_of_steps]

    def sum_copy(k, item):
        g, layer, ry, j = item
        rx = int(k // 2 != layer)
        link, there = towards_owner(orders[g, layer], k, rx, ry, j)
        return remote(
            piece_of(held[ARRAY_OF[g]].at[layer, place.block(ry, j)], g),
            arrived[g].at[slots[(g,) + there + (link,)]],
            sum_send.at[g, layer, ry * 4 + j],
            sum_recv.at[g, slots[(g,) + there + (link,)]],
            place.neighbour(link),
        )

    def run_items(k, items):
        for item in items:
            g, layer, ry, j = item
            rx = int(k // 2 != layer)
            mine = piece_of(held[ARRAY_OF[g]].at[layer, place.block(ry, j)], g)
            terms = []
            for link, middle_only in branches(orders[g, layer], rx, ry, j):
                if middle_only and not k % 2:
                    continue
                slot = slots[g, rx, ry, j, link]
                remote(
                    mine,
                    arrived[g].at[slot],
                    sum_send.at[g, layer, ry * 4 + j],
                    sum_recv.at[g, slot],
                    place.neighbour(link),
                ).wait_recv()
                terms.append(arrived[g].at[slot])
            final = (rx, ry, j) == (0, 0, 0)
            target = piece_of(result[ARRAY_OF[g]], g) if final else mine
            if terms or final:
                add_up(target, [mine] + terms)
            if not final:
                sum_copy(k, item).start()
                continue
            out = piece_of(outs[ARRAY_OF[g]], g)
            pltpu.make_async_copy(target, out, out_sem.at[g]).start()

    def add_up(target, terms):
        @pl.loop(0, target.shape[0] // 16)
        def _(i):
            at = pl.ds(pl.multiple_of(i * 16, 16), 16)
            sums = terms[0][at, :].astype(F32)
            for term in terms[1:]:
                sums = sums + term[at, :].astype(F32)
            target[at, :] = sums.astype(target.dtype)

    for number in range(len(steps) + 1):
        for k in range(4):
            if schedule[k][number]:
                pl.when(place.is_class(k))(
                    functools.partial(run_items, k, schedule[k][number])
                )
        if number < len(steps):
            steps[number]()

    for k in range(4):

        def finish(k=k):
            for items in schedule[k]:
                for item in items:
                    g, layer, ry, j = item
                    if (k // 2 != layer, ry, j) == (False, 0, 0):
                        pltpu.make_async_copy(
                            piece_of(result[ARRAY_OF[g]], g),
                            piece_of(outs[ARRAY_OF[g]], g),
                            out_sem.at[g],
                        ).wait()
                    else:
                        sum_copy(k, item).wait_send()

        pl.when(place.is_class(k))(finish)
    for name in shared_names:
        exchange(name, 0).wait_send()
    pl.when(s == 0)(low_swap.wait_send)
    pl.when(s == 1)(low_swap.wait_recv)
    grad_swap.wait()
    for layer in range(2):
        own_grads(layer).wait()


def backward_call(schedule, order_of_steps, orders, weights, kept, turned, inputs, cotangent, lengths):
    slots, counts = slot_table(orders)
    blocks = [(48, 2 * FEATURES), (48, PACK), (48, HIDDEN), (192, FEATURES)]
    pieces = [(48, 1536), (48, PACK), (48, 1536), (48, 1536), (96, FEATURES), (96, FEATURES)]
    rows = (LEN, FEATURES)
    outs = [jax.ShapeDtypeStruct(block, F32) for block in blocks]
    outs += [jax.ShapeDtypeStruct((2,) + rows, BF)] + [jax.ShapeDtypeStruct(rows, BF)] * 2
    pair = [rows, (LEN, HIDDEN), rows, (LEN, 2 * FEATURES), rows]
    scratch = [
        pltpu.VMEM((8, 2, 48, 2 * FEATURES), BF),
        pltpu.VMEM((2, 8, 2, 48, PACK), BF),
        pltpu.VMEM((64, 48, FEATURES), BF),
        pltpu.VMEM((LEN, 2 * FEATURES), BF),
        pltpu.VMEM(rows, BF),
        pltpu.VMEM((HEADS, LEN, LEN), BF),
        pltpu.VMEM((LEN, HIDDEN), BF),
        pltpu.VMEM(rows, F32),
        pltpu.VMEM(rows, BF),
        pltpu.VMEM((2, 8, 48, LEN), BF),
        pltpu.VMEM((2, 8, 48, LEN), BF),
        pltpu.VMEM((2, 8, 48, LEN), BF),
        pltpu.VMEM((2, 8, 192, LEN), BF),
        pltpu.VMEM(rows, BF),
    ]
    scratch += [pltpu.VMEM(shape, BF) for shape in pair + pair]
    scratch += [
        pltpu.VMEM(rows, F32),
        pltpu.VMEM(rows, F32),
        pltpu.VMEM(rows, BF),
        pltpu.VMEM((LEN, HALF), BF),
        pltpu.VMEM((2,) + rows, BF),
        pltpu.VMEM((8, FEATURES), F32),
        pltpu.VMEM((8, FEATURES), F32),
        pltpu.VMEM((2, 8, 2, 48, 128), BF),
    ]
    scratch += [pltpu.VMEM((2, 8) + block, BF) for block in blocks]
    scratch += [pltpu.VMEM((count,) + piece, BF) for count, piece in zip(counts, pieces)]
    scratch += [pltpu.VMEM(block, F32) for block in blocks]
    scratch += [
        pltpu.SemaphoreType.DMA((22, 2)),
        pltpu.SemaphoreType.DMA((7, 2)),
        pltpu.SemaphoreType.DMA((7, 2)),
        pltpu.SemaphoreType.REGULAR((7,)),
        pltpu.SemaphoreType.DMA((2,)),
        pltpu.SemaphoreType.DMA((2,)),
        pltpu.SemaphoreType.DMA((6, 2, 8)),
        pltpu.SemaphoreType.DMA((6, max(counts))),
        pltpu.SemaphoreType.DMA((8,)),
    ]
    anywhere = pl.BlockSpec(memory_space=pl.ANY)
    operands = [
        weights[0],
        weights[1],
        weights[2].reshape(2, 16, 48, HIDDEN),
        weights[3].reshape(2, 64, 48, FEATURES),
    ]
    operands += list(kept) + list(turned) + [inputs, cotangent]
    return pl.pallas_call(
        functools.partial(backward_kernel, schedule, order_of_steps, orders, slots),
        out_shape=outs,
        in_specs=[anywhere] * len(operands) + [pl.BlockSpec(memory_space=pltpu.SMEM)],
        out_specs=[anywhere] * len(outs),
        scratch_shapes=scratch,
        compiler_params=pltpu.CompilerParams(
            collective_id=1, has_side_effects=True, vmem_limit_bytes=63 * 2**20
        ),
    )(*operands, lengths)


GATHER = (
    (
        (10000, 20000, 30000, 13000, 23000, 33000, 31000, 1, 10, 100, 20001, 10010, 32000,
        10001, 0, 1000, 2000, 3000, 4000, 5000, 1100, 3001, 3010, 23001, 34000, 110, 2, 11,
        20002, 10011, 35000, 10002, 1101, 3002, 3011, 23002, 101, 3, 12, 20003, 10012, 10003,
        111, 3003, 3012, 23003, 21000, 1102, 1001, 13, 10013, 21001, 11000, 102, 1002, 3013,
        21002, 12000, 1103, 1003, 1010, 21003, 2100, 2001, 12001, 1011, 21100, 103, 1012, 2002,
        12002, 21101, 1013, 2101, 2003, 12003, 21102, 14000, 1110, 112, 4001, 21103, 15000,
        1111, 2102, 4002, 22000, 1112, 113, 4003, 24000, 1113, 2103, 5001, 15001, 25000, 2010,
        12010, 32010, 3100, 5002, 22100, 4010, 14010, 34010, 3101, 5003, 22101, 15002, 5010,
        35010),
        (3102, 2011, 22102),
        (12011, 2110),
        (4100, 4011, 22103),
        (15003, 2111),
        (5100, 35100, 2012, 23100, 12012, 2112, 3103, 4012, 23101, 15010, 2113, 2013, 23102,
        12013, 4101, 3110, 4013, 23103, 4102, 3111, 5011, 15011, 25100, 4103, 3112, 5012, 15012,
        4110, 3113),
        (5013, 15013),
        (),
        (4111, 5110),
        (5103, 25103, 4112, 5101, 25101, 4113, 5113),
        (5102, 25102),
        (),
        (5111,),
        (),
        (5112,),
        (),
        (),
        (),
        (),
        (),
        (),
    ),
    (
        (10000, 20000, 30000, 40000, 13000, 23000, 33000, 43000, 1, 2, 10, 100, 10001, 20001, 0,
        1000, 2000, 3000, 4000, 5000, 40001, 30002, 10002, 20002, 1100, 3001, 3002, 3010, 43001,
        33002, 10010, 41000, 101, 1001, 3, 11, 20003, 30003, 41001, 10003, 23001, 1101, 2001,
        12, 3003, 33003, 42000, 10011, 31000, 23002, 1102, 1002, 4001, 13, 42001, 31002, 10012,
        23003, 102, 1003, 5001, 3011, 31003, 44000, 10013, 21000, 1103, 2002, 3012, 32000,
        44001, 21001, 11000, 110, 2003, 3013, 32002, 21002, 45000, 12000, 103, 4002, 1010,
        21003, 32003, 45001, 12001, 111, 1011, 4003, 21100, 34000, 12002, 2100, 1012, 5002,
        21101, 34002, 12003, 1013, 2101, 5003, 21102, 34003, 14000, 1110, 112, 21103, 35000,
        15000, 1111, 2102, 22000, 35002, 1112, 15001, 113, 24000, 35003, 1113, 15002, 2103,
        25000, 2010, 32010, 42010, 12010, 3100, 22100, 4010, 34010, 44010, 3101, 22101, 2011,
        2012, 12011, 42011, 32012, 5010),
        (12012, 3102, 22102),
        (4011, 4012, 44011, 34012, 2110),
        (45010, 3103, 22103),
        (2013, 5011, 12013, 32013, 2111),
        (14010, 45011, 4100, 23100, 4013, 34013, 2112, 15003, 4101, 23101, 5012, 35010, 2113,
        5101, 45101, 15010, 4102, 23102, 5013, 35012, 3110, 15011, 4103, 23103, 5103, 35013,
        3111, 15012, 5100, 45100, 25101, 35103, 3112, 15013, 25103, 4110, 35100, 3113, 5102),
        (),
        (25100, 4111),
        (35102, 5111),
        (25102, 4112, 5113, 4113, 5110),
        (),
        (5112,),
        (),
        (),
        (),
        (),
        (),
        (),
        (),
        (),
        (),
    ),
    (
        (10100, 20100, 30100, 11100, 21100, 31100, 32100, 0, 101, 110, 20101, 10110, 1101, 1110,
        100, 1100, 2100, 3100, 4100, 5100, 11101, 3000, 23000, 33000, 10101, 21101, 33100, 102,
        111, 10, 10111, 34100, 3001, 3010, 23001, 1, 35100, 1102, 1111, 11102, 21102, 11, 10102,
        3002, 3011, 23002, 2, 1103, 1112, 11103, 21103, 12, 12100, 3003, 3012, 23003, 3, 20102,
        1113, 103, 10103, 13, 3013, 2101, 12101, 1000, 21000, 31000, 20103, 112, 10112, 2102,
        2000, 12102, 1010, 1001, 21001, 2001, 22100, 113, 10113, 2103, 2002, 12103, 1011, 1002,
        21002, 2003, 22101, 13100, 2110, 3101, 4000, 34000, 13101, 1012, 1003, 21003, 22102,
        5000, 2111, 3102, 13102, 22103, 14100, 1013, 5001, 4001, 23100, 15100, 2112),
        (2010, 4002, 23101),
        (2113,),
        (4010, 34010, 3103, 13103, 23102),
        (3110,),
        (5002, 4003, 23103, 3111, 2011, 4101, 14101, 24100, 3112, 5003, 4102, 14102, 24101,
        3113, 2012, 4103, 14103, 24102, 4110, 14110, 5010, 5101, 24103, 4111, 14111, 2013, 4013,
        25100, 4112, 14112, 5011),
        (4011,),
        (25101,),
        (4113, 14113, 5012, 4012),
        (5110, 5013, 5102, 25102, 5111),
        (5103, 25103),
        (5112,),
        (),
        (),
        (5113,),
        (),
        (),
        (),
        (),
        (),
        (),
    ),
    (
        (10100, 20100, 30100, 40100, 11100, 21100, 31100, 41100, 0, 101, 102, 110, 10101, 20101,
        100, 1100, 2100, 3100, 4100, 5100, 40101, 30102, 1101, 1102, 1110, 11101, 3000, 23000,
        33000, 43000, 11102, 21101, 41101, 31102, 103, 111, 2101, 1, 10102, 3001, 3002, 3010,
        23001, 43001, 33002, 2, 42100, 23002, 1103, 1111, 11103, 31103, 3101, 10, 10110, 42101,
        3003, 3011, 23003, 33003, 4101, 3, 10103, 30103, 21102, 43100, 2102, 3012, 5101, 11,
        10111, 21103, 32100, 43101, 2103, 3013, 12, 12100, 20102, 32102, 44100, 1112, 3102, 13,
        12101, 1113, 3103, 1000, 21000, 31000, 41000, 20103, 32103, 44101, 112, 10112, 4102,
        2000, 12102, 1001, 21001, 41001, 1010, 1002, 31002, 2001, 21002, 33100, 45100, 113,
        10113, 4103, 2002, 12103, 45101, 1011, 1003, 21003, 31003, 22100, 2003, 33102, 13100,
        1012, 5102, 22101, 4000, 44000, 34000, 13101, 1013, 5103, 22102, 5000, 13102, 2110,
        4001, 44001, 4002, 34002, 22103, 5001, 33103, 13103, 2111, 23100, 5002, 14100, 2112,
        4003, 34003),
        (23101, 2010),
        (34100, 14101, 2113),
        (23102,),
        (2011, 34102, 14102, 3110),
        (23103, 2012, 34103, 4011, 44011, 14103, 3111, 24100, 2013, 35100, 15100, 3112, 24101,
        4013, 4010, 44010, 34013, 3113, 24102, 5003, 34010, 4110, 14110, 4012, 24103, 5010,
        34012, 4111, 14111, 25100, 5011, 35102, 4112, 14112),
        (),
        (25101, 5012, 35103),
        (4113, 14113),
        (25102, 5013, 5110, 25103, 5111),
        (),
        (5112,),
        (),
        (),
        (5113,),
        (),
        (),
        (),
        (),
        (),
        (),
    ),
)

SUMS = (
    (
        (),
        (),
        (),
        (),
        (),
        (),
        (),
        (5112,),
        (),
        (2112, 5111, 4113, 2111),
        (),
        (),
        (),
        (5102, 2113, 5103),
        (5101,),
        (3112,),
        (),
        (),
        (),
        (2110,),
        (3113,),
        (),
        (111,),
        (),
        (2103, 113),
        (5113, 4102),
        (),
        (),
        (),
        (112, 3103),
        (),
        (),
        (5013,),
        (2102, 4012),
        (5011,),
        (),
        (103, 2013),
        (2012, 5003),
        (),
        (3100, 3013),
        (2101, 3110, 4100, 5012, 5001, 4112),
        (),
        (),
        (3011, 4013, 102, 4110),
        (),
        (4111, 3101),
        (3012, 5002, 1112, 3102, 2011, 2003, 1013, 110, 4003, 1113, 3003, 13, 2002, 100, 1102,
        1003, 1011, 4103, 3, 4101, 1111, 1010, 3111, 2001, 4002, 3010, 12, 1103, 2010, 1012,
        101, 3002, 11, 2100, 5110, 2, 1101, 4010, 1110, 4011, 1002, 10, 1001, 5010, 3001, 5100,
        1, 4001, 1100, 2000, 4000, 0, 1000, 3000, 5000),
    ),
    (
        (),
        (),
        (),
        (),
        (),
        (),
        (),
        (),
        (),
        (2112, 2113, 2111),
        (),
        (),
        (),
        (),
        (4112,),
        (4103, 4113),
        (),
        (),
        (3103,),
        (2110,),
        (),
        (),
        (),
        (),
        (110, 113),
        (),
        (111,),
        (4111, 112),
        (),
        (4102,),
        (3113,),
        (5102, 3102, 3110, 3100),
        (2103, 5103),
        (),
        (2011,),
        (),
        (),
        (5013,),
        (5112,),
        (3010, 3012, 2013, 4013, 102, 5003, 2102, 3111),
        (2010, 3013, 3112),
        (),
        (5113, 5012, 2100, 4012),
        (),
        (5001, 101, 5100),
        (4011, 3011, 103, 5110, 2101),
        (1013, 3003, 2012, 1011, 5011, 1110, 5111, 1113, 4003, 5101, 5002, 4001, 1010, 2003,
        4100, 3001, 1111, 2002, 3101, 1112, 13, 1003, 12, 4002, 11, 4110, 1103, 3002, 1102,
        1012, 1101, 100, 1001, 5010, 3, 2001, 4101, 10, 2000, 1100, 2, 1, 4010, 1002, 0, 3000,
        5000, 1000, 4000),
    ),
    (
        (),
        (),
        (),
        (),
        (),
        (),
        (),
        (5101,),
        (),
        (2112, 5103),
        (2113,),
        (),
        (5102,),
        (),
        (),
        (2111,),
        (5113,),
        (),
        (),
        (),
        (4113, 5111),
        (),
        (),
        (110, 5112),
        (),
        (),
        (113,),
        (3113, 4012, 4000),
        (),
        (3112,),
        (2103,),
        (5013, 4011),
        (),
        (),
        (),
        (),
        (2012, 2010, 5012, 4013, 2102, 4010, 5003),
        (),
        (),
        (3013,),
        (),
        (),
        (),
        (3103,),
        (),
        (2002, 2013, 5002, 4003, 3003),
        (1013, 10, 5001, 1112, 13, 3, 5011, 112, 2003, 4112, 3012, 2101, 1003, 103, 3011, 1012,
        11, 4102, 4002, 0, 12, 1113, 3002, 1011, 1103, 1010, 4111, 3001, 2, 4103, 3010, 102,
        1002, 1102, 2011, 5010, 1110, 111, 5000, 1, 3111, 2000, 2001, 1001, 1111, 3102, 5110,
        4001, 4101, 1000, 3000, 1101, 3110, 2110, 4110, 100, 101, 3101, 5100, 3100, 2100, 1100,
        4100),
    ),
    (
        (),
        (),
        (),
        (),
        (),
        (),
        (),
        (),
        (),
        (2112,),
        (),
        (2113,),
        (),
        (2111,),
        (),
        (),
        (),
        (),
        (),
        (5103,),
        (2110,),
        (),
        (),
        (),
        (110,),
        (),
        (),
        (4112,),
        (4013,),
        (4002, 4011),
        (112,),
        (),
        (),
        (),
        (2013,),
        (3013,),
        (113, 4001),
        (),
        (2011, 3011),
        (),
        (2012, 3012, 2103),
        (5102,),
        (4012, 3010),
        (111, 4113),
        (2102,),
        (3113, 4003, 5003),
        (3003, 12, 4010, 1012, 2010, 5113, 1113, 10, 5013, 3001, 5012, 3002, 3111, 2003, 1013,
        4000, 2002, 13, 1, 1011, 11, 5001, 4111, 5002, 5011, 5112, 5000, 103, 2100, 5111, 3112,
        3, 5010, 2001, 4102, 1112, 2101, 1111, 1003, 3103, 4103, 5101, 1001, 102, 1103, 2, 1010,
        1002, 4110, 101, 5110, 2000, 0, 1110, 1102, 3000, 3101, 3102, 1101, 3110, 4100, 4101,
        1000, 100, 1100, 5100, 3100),
    ),
)

STEPS = (
    0, 1, 2, 3, 5, 4, 6, 8, 9, 10, 7, 11, 12, 13, 14, 15, 16, 17, 18, 19, 20, 21, 23, 22, 24,
    28, 25, 26, 27, 29, 30, 31, 32, 33, 34, 35, 36, 37, 38, 39, 40, 41, 42, 43, 44, 45,
)

ORDERS = {
    (0, 0): "zyx",
    (0, 1): "zxy",
    (1, 0): "xzy",
    (1, 1): "xzy",
    (2, 0): "xzy",
    (2, 1): "xzy",
    (3, 0): "zxy",
    (3, 1): "zyx",
    (4, 0): "zyx",
    (4, 1): "zyx",
    (5, 0): "yxz",
    (5, 1): "yxz",
}


def gather(blocks):
    return [
        lax.all_gather(lax.all_gather(block, "dp", axis=0, tiled=True), "section", axis=0)
        for block in blocks
    ]


def scatter(partials):
    results = []
    for pair in partials:
        both = lax.psum_scatter(jnp.stack(pair), "section", scatter_dimension=0, tiled=False)
        results.append(
            lax.psum_scatter(both.astype(F32), "dp", scatter_dimension=0, tiled=True)
        )
    return results


def norm_back(grad, unit, scale, gain):
    scaled = grad * gain
    inner = scaled - jnp.mean(scaled, axis=-1, keepdims=True)
    inner = inner - unit * jnp.mean(scaled * unit, axis=-1, keepdims=True)
    return jnp.sum(grad * unit, axis=0), jnp.sum(grad, axis=0), scale * inner


def by_head(rows):
    return rows.reshape(rows.shape[0], -1, HD)


def forward(hidden, weights, shared, allowed):
    query_key, value, out, up, down, first, norms = weights
    unit_one, scale_one = normalized(hidden)
    normed = (unit_one * norms[0] + norms[1]).astype(BF)
    qk = product(normed, query_key).astype(BF)
    fresh = product(normed, value).astype(BF)
    if shared is None:
        shared = product(normed, first).astype(BF)
    features = hidden.shape[1]
    queries, keys = by_head(qk[:, :features]), by_head(qk[:, features:])
    values = by_head(jnp.concatenate([fresh, shared], axis=1))
    scores = jnp.einsum("qhd,khd->hqk", queries, keys, preferred_element_type=F32) * HD**-0.5
    scores = jnp.where(allowed, scores, -1e30)
    raised = jnp.exp(scores - jnp.max(scores, axis=-1, keepdims=True))
    soft = raised / jnp.sum(raised, axis=-1, keepdims=True)
    probs = soft.astype(BF)
    attended = jnp.einsum("hqk,khd->qhd", probs, values, preferred_element_type=F32)
    attended = attended.reshape(hidden.shape).astype(BF)
    middle = hidden + product(attended, out)
    unit_two, scale_two = normalized(middle)
    mixed = (unit_two * norms[2] + norms[3]).astype(BF)
    upper = product(mixed, up)
    active = jax.nn.gelu(upper, approximate=True).astype(BF)
    output = middle + product(active, down)
    kept = (normed, queries, keys, values, soft, attended, unit_one, scale_one)
    return output, shared, kept + (unit_two, scale_two, mixed, upper, active)


def backward(grad, weights, kept, grad_shared_next):
    query_key, value, out, up, down, first, norms = weights
    normed, queries, keys, values, soft, attended, unit_one, scale_one = kept[:8]
    unit_two, scale_two, mixed, upper, active = kept[8:]
    positions, features = grad.shape
    half = value.shape[1]
    grad_low = grad.astype(BF)
    down_grad = transposed_times(active, grad_low)
    _, gelu_pull = jax.vjp(lambda u: jax.nn.gelu(u, approximate=True), upper)
    grad_upper = gelu_pull(times_transposed(grad_low, down))[0].astype(BF)
    up_grad = transposed_times(mixed, grad_upper)
    grad_mixed = times_transposed(grad_upper, up)
    two_gain, two_bias, through = norm_back(grad_mixed, unit_two, scale_two, norms[2])
    grad_middle = grad + through
    grad_attn = grad_middle.astype(BF)
    out_grad = transposed_times(attended, grad_attn)
    grad_attended = by_head(times_transposed(grad_attn, out).astype(BF))
    grad_soft = jnp.einsum("qhd,khd->hqk", grad_attended, values, preferred_element_type=F32)
    grad_values = jnp.einsum(
        "hqk,qhd->khd", soft.astype(BF), grad_attended, preferred_element_type=F32
    ).reshape(positions, features)
    grad_scores = soft * (grad_soft - jnp.sum(soft * grad_soft, axis=-1, keepdims=True))
    grad_scores = grad_scores.astype(BF)
    grad_queries = jnp.einsum("hqk,khd->qhd", grad_scores, keys, preferred_element_type=F32)
    grad_keys = jnp.einsum("hqk,qhd->khd", grad_scores, queries, preferred_element_type=F32)
    grad_qk = jnp.concatenate(
        [grad_queries.reshape(positions, features), grad_keys.reshape(positions, features)], axis=1
    )
    grad_qk = (grad_qk * HD**-0.5).astype(BF)
    grad_fresh = grad_values[:, :half].astype(BF)
    grad_shared = grad_values[:, half:]
    grad_normed = times_transposed(grad_qk, query_key) + times_transposed(grad_fresh, value)
    if grad_shared_next is not None:
        grad_shared = (grad_shared + grad_shared_next.astype(F32)).astype(BF)
        first_grad = transposed_times(normed, grad_shared)
        grad_normed = grad_normed + times_transposed(grad_shared, first)
    else:
        grad_shared = grad_shared.astype(BF)
        first_grad = None
    one_gain, one_bias, through = norm_back(grad_normed, unit_one, scale_one, norms[0])
    grad_input = (grad_middle + through).astype(BF)
    query_key_grad = transposed_times(normed, grad_qk)
    value_grad = transposed_times(normed, grad_fresh)
    gains = jnp.stack([one_gain, one_bias, two_gain, two_bias], axis=1)
    return grad_input, grad_shared, (
        query_key_grad, value_grad, out_grad, up_grad, down_grad, first_grad, gains
    )


def swapped(block):
    return lax.ppermute(block, "section", [(0, 1), (1, 0)])


def on_any_mesh(
    inputs,
    cotangent,
    lengths,
    norm_one_gain,
    norm_one_bias,
    query_key_weight,
    value_weight,
    out_weight,
    norm_two_gain,
    norm_two_bias,
    up_weight,
    down_weight,
    first_value_weight,
):
    section = lax.axis_index("section")
    first_half = section == 0
    half = value_weight.shape[2]
    features = out_weight.shape[2]
    quarter = first_value_weight.shape[1]
    own_rows = query_key_weight.shape[1]
    norms = jnp.stack([norm_one_gain[0], norm_one_bias[0], norm_two_gain[0], norm_two_bias[0]], axis=1)
    padding = -(half + features + quarter + 4) % 128
    attention = jnp.concatenate(
        [
            value_weight[0],
            out_weight[0],
            first_value_weight,
            norms,
            jnp.zeros((own_rows, padding), BF),
        ],
        axis=1,
    )
    whole = gather([query_key_weight[0], attention, up_weight[0], down_weight[0]])
    after = half + features
    first_matrix = jnp.concatenate(
        [whole[1][0, :, after : after + quarter], whole[1][1, :, after : after + quarter]], axis=1
    )

    def layer_weights(layer):
        packed = whole[1][layer]
        gains = packed[:, after + quarter : after + quarter + 4].astype(F32).T
        return (
            whole[0][layer],
            packed[:, :half],
            packed[:, half:after],
            whole[2][layer],
            whole[3][layer],
            first_matrix,
            gains,
        )

    weights = [layer_weights(0), layer_weights(1)]
    batch_sequences, positions = inputs.shape[1:3]
    hidden = lax.dynamic_index_in_dim(inputs, section, 0, keepdims=False)[0]
    grad = lax.dynamic_index_in_dim(cotangent, section, 0, keepdims=False)[0]
    length = lax.dynamic_index_in_dim(lengths, section, 0, keepdims=False)[0]
    places = jnp.arange(positions)
    live = places < length
    allowed = (places[None, :] <= places[:, None]) & live[None, :]
    output_one, shared, kept_one = forward(hidden.astype(F32), weights[0], None, allowed)
    low_one = output_one.astype(BF)
    output_two, _, kept_two = forward(low_one.astype(F32), weights[1], shared, allowed)
    low_two = output_two.astype(BF)
    outputs_there = swapped(jnp.where(first_half, low_two, low_one))
    outputs_here = jnp.where(first_half, low_one, low_two)
    grad = jnp.where(live[:, None], grad.astype(F32), 0.0)
    grad_one, grad_shared, sums_two = backward(grad, weights[1], kept_two, None)
    grad_zero, _, sums_one = backward(grad_one.astype(F32), weights[0], kept_one, grad_shared)
    grads_there = swapped(jnp.where(first_half, grad_one, grad_zero))
    grads_here = jnp.where(first_half, grad_zero, grad_one)
    first_grad = sums_one[5]

    def packed_sums(sums, first_part):
        return jnp.concatenate(
            [
                sums[1],
                sums[2],
                first_part,
                sums[6],
                jnp.zeros((first_part.shape[0], padding), F32),
            ],
            axis=1,
        ).astype(BF)

    partials = [
        (sums_one[0].astype(BF), sums_two[0].astype(BF)),
        (
            packed_sums(sums_one, first_grad[:, :quarter]),
            packed_sums(sums_two, first_grad[:, quarter:]),
        ),
        (sums_one[3].astype(BF), sums_two[3].astype(BF)),
        (sums_one[4].astype(BF), sums_two[4].astype(BF)),
    ]
    query_key_grad, packed_grad, up_grad, down_grad = scatter(partials)
    gains = packed_grad[:, after + quarter : after + quarter + 4].T

    def both(here, there):
        return jnp.stack(
            [jnp.where(first_half, here, there), jnp.where(first_half, there, here)]
        )[None, :, None]

    return (
        both(outputs_here, outputs_there),
        both(grads_here, grads_there),
        gains[0][None],
        gains[1][None],
        query_key_grad[None],
        packed_grad[:, :half][None],
        packed_grad[:, half:after][None],
        gains[2][None],
        gains[3][None],
        up_grad[None],
        down_grad[None],
        packed_grad[:, after : after + quarter],
    )


def on_device(
    tables,
    inputs,
    cotangent,
    lengths,
    norm_one_gain,
    norm_one_bias,
    query_key_weight,
    value_weight,
    out_weight,
    norm_two_gain,
    norm_two_bias,
    up_weight,
    down_weight,
    first_value_weight,
):
    gather_schedule, sum_schedule, steps, sum_orders = tables
    own = (query_key_weight, value_weight, out_weight, up_weight, down_weight)
    small = (first_value_weight, norm_one_gain, norm_one_bias, norm_two_gain, norm_two_bias)
    lengths = lengths.reshape(-1)
    done = forward_call(gather_schedule, own, small, inputs, lengths)
    weights, kept, turned, one_there = done[:4], done[4:10], done[10:14], done[14]
    back = backward_call(
        sum_schedule, steps, sum_orders, weights, kept, turned, inputs, cotangent, lengths
    )
    return last_call(back, kept[5], one_there)


def last_kernel(
    pack, query_key, up, down, grads, low, one_there, two_there, grad_there,
    out_low, out_grads, out_vector_0, out_vector_1, out_query_key, out_value, out_out,
    out_vector_2, out_vector_3, out_up, out_down, out_first,
    v_query_key, v_up, v_down, v_rows,
    in_sems, out_sems,
):
    s = lax.axis_index("section")
    copies = [
        (query_key, v_query_key, out_query_key.at[0]),
        (up, v_up, out_up.at[0]),
        (down, v_down, out_down.at[0]),
        (low.at[s], v_rows.at[0], out_low.at[0, s, 0]),
        (one_there, v_rows.at[1], out_low.at[0, 1 - s, 0]),
        (grads.at[s], v_rows.at[2], out_grads.at[0, s, 0]),
        (grad_there, v_rows.at[3], out_grads.at[0, 1 - s, 0]),
    ]
    reads = [
        pltpu.make_async_copy(source, held, in_sems.at[i])
        for i, (source, held, _) in enumerate(copies)
    ]
    writes = [
        pltpu.make_async_copy(held, target, out_sems.at[i])
        for i, (_, held, target) in enumerate(copies)
    ]
    for i, read in enumerate(reads):
        if i != 4:
            read.start()
    pl.when(s == 0)(reads[4].start)
    pl.when(s == 1)(pltpu.make_async_copy(two_there, v_rows.at[1], in_sems.at[4]).start)
    out_value[0] = pack[:, :HALF]
    out_out[0] = pack[:, HALF:FIRST]
    out_first[...] = pack[:, FIRST:NORMS]
    rows = pack[:, NORMS - 64 :].T
    for i, out in enumerate((out_vector_0, out_vector_1, out_vector_2, out_vector_3)):
        out[...] = rows[64 + i : 65 + i, :]
    for read, write in zip(reads, writes):
        read.wait()
        write.start()
    for write in writes:
        write.wait()


def last_call(back, low, one_there):
    query_key, pack, up, down, grads, two_there, grad_there = back
    anywhere = pl.BlockSpec(memory_space=pl.ANY)
    vmem = pl.BlockSpec(memory_space=pltpu.VMEM)
    vector = jax.ShapeDtypeStruct((1, 48), F32)
    rows = jax.ShapeDtypeStruct((1, 2, 1, LEN, FEATURES), BF)

    def block(*shape):
        return jax.ShapeDtypeStruct(shape, F32)

    return pl.pallas_call(
        last_kernel,
        out_shape=[
            rows, rows, vector, vector, block(1, 48, 2 * FEATURES), block(1, 48, HALF),
            block(1, 48, FEATURES), vector, vector, block(1, 48, HIDDEN),
            block(1, 192, FEATURES), block(48, 192),
        ],
        in_specs=[vmem] + [anywhere] * 8,
        out_specs=[
            anywhere, anywhere, vmem, vmem, anywhere, vmem, vmem, vmem, vmem, anywhere, anywhere,
            vmem,
        ],
        scratch_shapes=[
            pltpu.VMEM((48, 2 * FEATURES), F32),
            pltpu.VMEM((48, HIDDEN), F32),
            pltpu.VMEM((192, FEATURES), F32),
            pltpu.VMEM((4, LEN, FEATURES), BF),
            pltpu.SemaphoreType.DMA((7,)),
            pltpu.SemaphoreType.DMA((7,)),
        ],
    )(pack, query_key, up, down, grads, low, one_there, two_there, grad_there)


def solution(mesh):
    placed = (
        P(None, "dp", None, None),
        P(None, "dp", None, None),
        P(None, "dp"),
        P("section", "dp"),
        P("section", "dp"),
        P("section", "dp", None),
        P("section", "dp", None),
        P("section", "dp", None),
        P("section", "dp"),
        P("section", "dp"),
        P("section", "dp", None),
        P("section", "dp", None),
        P("dp", "section"),
    )
    if mesh.shape["dp"] == 16 and mesh.shape["section"] == 2:
        sums = [[[item[1:] for item in items] for items in k] for k in schedule_of(SUMS)]
        body = functools.partial(on_device, (schedule_of(GATHER), sums, STEPS, ORDERS))
    else:
        body = on_any_mesh
    return jax.shard_map(
        body,
        mesh=mesh,
        in_specs=placed,
        out_specs=(
            P("section", None, "dp", None, None),
            P("section", None, "dp", None, None),
            P("section", "dp"),
            P("section", "dp"),
            P("section", "dp", None),
            P("section", "dp", None),
            P("section", "dp", None),
            P("section", "dp"),
            P("section", "dp"),
            P("section", "dp", None),
            P("section", "dp", None),
            P("dp", "section"),
        ),
        check_vma=False,
    )
```

```python
import functools

import jax
import jax.numpy as jnp
from jax import lax
from jax.experimental import pallas as pl
from jax.experimental.pallas import tpu as pltpu
from jax.sharding import PartitionSpec as P

HEADS = 12
HD = 64
EPSILON = 1e-05
BF = jnp.bfloat16
F32 = jnp.float32
MESH = pl.DeviceIdType.MESH
LEN = 256
FEATURES = 768
HALF = 384
HIDDEN = 3072
PACK = 1408
FIRST = HALF + FEATURES
NORMS = FIRST + 192
LINKS = ("x", "y", "near", "far")


class Place:
    def __init__(self):
        self.s = lax.axis_index("section")
        dp = lax.axis_index("dp")
        self.z = dp // 4
        self.y = (dp // 2) % 2
        self.c = dp % 2
        self.mid = (self.z == 1) | (self.z == 2)

    def device(self, s, z, y, c):
        return (s, z * 4 + y * 2 + c)

    def neighbour(self, link):
        s, z, y, c = self.s, self.z, self.y, self.c
        if link == "x":
            return self.device(1 - s, z, y, c)
        if link == "y":
            return self.device(s, z, 1 - y, c)
        if link == "near":
            return self.device(s, z + 1 - 2 * (z % 2), y, c)
        if link == "far":
            return self.device(s, 3 - z, y, c)
        return self.device(s, z, y, 1 - c)

    def along_z(self, j):
        z = self.z
        return (z, z + 1 - 2 * (z % 2), 2 - z // 2, 3 - 3 * (z // 2))[j]

    def block(self, ry, j):
        y = self.y if ry == 0 else 1 - self.y
        return self.along_z(j) * 2 + y

    def is_class(self, k):
        middle = self.mid if k % 2 else jnp.logical_not(self.mid)
        return (self.s == k // 2) & middle


def greet(place):
    barrier = pltpu.get_barrier_semaphore()
    for link in ("x", "y", "near", "core"):
        pl.semaphore_signal(barrier, 1, device_id=place.neighbour(link), device_id_type=MESH)

    @pl.when(place.mid)
    def _():
        pl.semaphore_signal(barrier, 1, device_id=place.neighbour("far"), device_id_type=MESH)


def meet(place):
    barrier = pltpu.get_barrier_semaphore()

    @pl.when(place.mid)
    def _():
        pl.semaphore_wait(barrier, 5)

    @pl.when(jnp.logical_not(place.mid))
    def _():
        pl.semaphore_wait(barrier, 4)


def remote(source, target, send_sem, recv_sem, device):
    return pltpu.make_async_remote_copy(
        src_ref=source,
        dst_ref=target,
        send_sem=send_sem,
        recv_sem=recv_sem,
        device_id=device,
        device_id_type=MESH,
    )


def product(left, right):
    return jnp.dot(left, right, preferred_element_type=F32)


def times_transposed(left, right):
    return lax.dot_general(left, right, (((1,), (1,)), ((), ())), preferred_element_type=F32)


def transposed_times(left, right):
    return lax.dot_general(left, right, (((0,), (0,)), ((), ())), preferred_element_type=F32)


def normalized(rows):
    average = jnp.mean(rows, axis=-1, keepdims=True)
    centred = rows - average
    scale = lax.rsqrt(jnp.mean(centred * centred, axis=-1, keepdims=True) + EPSILON)
    return centred * scale, scale


def lane_index(shape):
    return lax.broadcasted_iota(jnp.int32, shape, 1)


def flat(block):
    return block.reshape(-1, block.shape[-1])


ARRAY_OF = (0, 1, 2, 2, 3, 3)
ROWS = (48, 48, 48, 192)
WIDTH = (2 * FEATURES, PACK, HIDDEN, FEATURES)


def piece_of(ref, g):
    lead = (slice(None),) * (len(ref.shape) - 2)
    if g in (2, 3):
        return ref.at[lead + (slice(None), pl.ds((g - 2) * (HIDDEN // 2), HIDDEN // 2))]
    if g in (4, 5):
        return ref.at[lead + (pl.ds((g - 4) * 96, 96), slice(None))]
    return ref


def forward_kernel(
    schedule,
    own_qk, own_value, own_out, own_up, own_down, first, vector_0, vector_1, vector_2, vector_3,
    inputs, lengths,
    out_qk, out_pack, out_up, out_down,
    kept_qk, kept_values, kept_probs, kept_slope, kept_middle, kept_low,
    turned_normed, turned_attended, turned_mixed, turned_active, swapped_one,
    w_qk, w_pack, w_up, w_down, own_pack, v_first, v_vectors, length,
    x_ref, normed, qk, values, probs, attended, middle, mixed, active, slope, low,
    t_normed, t_attended, t_mixed, t_active,
    recv_sem, send_sem, core_send, core_recv, local_sem, keep_sem, turn_send, turn_recv, fetch_sem, swap_sem,
):
    place = Place()
    s, c = place.s, place.c
    own = (own_qk.at[0], own_pack, own_up.at[0], own_down.at[0])
    whole = (w_qk, w_pack, w_up, w_down)
    whole_out = (out_qk, out_pack, out_up, out_down)

    greet(place)
    fetch = pltpu.make_async_copy(inputs.at[s, 0], x_ref, fetch_sem.at[0])
    fetch.start()
    packing = [
        pltpu.make_async_copy(own_value.at[0], own_pack.at[:, 0:HALF], fetch_sem.at[1]),
        pltpu.make_async_copy(own_out.at[0], own_pack.at[:, HALF:FIRST], fetch_sem.at[2]),
    ]
    small = [pltpu.make_async_copy(first, v_first, fetch_sem.at[3])]
    small += [
        pltpu.make_async_copy(vector, v_vectors.at[i], fetch_sem.at[4 + i])
        for i, vector in enumerate((vector_0, vector_1, vector_2, vector_3))
    ]
    small_length = pltpu.make_async_copy(lengths, length, fetch_sem.at[8])
    for one in packing + small + [small_length]:
        one.start()

    def pack_small():
        for one in small + packing:
            one.wait()
        tall = jnp.concatenate(
            [jnp.zeros((64, 48), F32)]
            + [v_vectors[i].astype(F32) for i in range(4)]
            + [jnp.zeros((60, 48), F32)],
            axis=0,
        )
        own_pack[:, FIRST : FIRST + 128] = v_first[:, :128]
        own_pack[:, FIRST + 128 :] = tall.T.astype(BF)
        own_pack[:, FIRST + 128 : NORMS] = v_first[:, 128:]
        mine[1].start()


    def spot(g, layer, ry, j):
        return piece_of(whole[ARRAY_OF[g]].at[layer, place.block(ry, j), c], g)

    mine = [
        pltpu.make_async_copy(
            piece_of(own[ARRAY_OF[g]], g), spot(g, s, 0, 0), local_sem.at[g]
        )
        for g in range(6)
    ]
    for g, one in enumerate(mine):
        if g != 1:
            one.start()
    meet(place)

    def weight_copy(k, item):
        link, g, layer, ry, j = item
        target = spot(g, layer, ry, j)
        source = target
        if (ry, j) == (0, 0) and layer == k // 2:
            source = piece_of(own[ARRAY_OF[g]], g)
        return remote(
            source,
            target,
            send_sem.at[LINKS.index(link), g, layer],
            recv_sem.at[g, layer, place.block(ry, j)],
            place.neighbour(link),
        )

    def hand_over(g, layer):
        part = piece_of(whole[ARRAY_OF[g]].at[layer, :, c], g)
        return remote(
            part, part, core_send.at[g, layer], core_recv.at[g, layer], place.neighbour("core")
        )

    def from_core(g, layer):
        part = piece_of(whole[ARRAY_OF[g]].at[layer, :, 1 - c], g)
        return remote(
            part, part, core_send.at[g, layer], core_recv.at[g, layer], place.neighbour("core")
        )

    missing = [{(g, l): 8 for g in range(6) for l in range(2)} for k in range(4)]
    begun = [set() for k in range(4)]

    packed = [False] * 4

    def run_items(k, items):
        for item in items:
            link, g, layer, ry, j = item
            if (g, layer, ry, j) == (1, k // 2, 0, 0) and not packed[k]:
                packed[k] = True
                pack_small()
            if link is not None:
                weight_copy(k, item).start()
                continue
            if (ry, j) == (0, 0) and layer == k // 2:
                mine[g].wait()
            else:
                remote(
                    spot(g, layer, ry, j),
                    spot(g, layer, ry, j),
                    send_sem.at[0, g, layer],
                    recv_sem.at[g, layer, place.block(ry, j)],
                    place.neighbour("x"),
                ).wait_recv()
            missing[k][g, layer] -= 1
            if missing[k][g, layer] == 0:
                hand_over(g, layer).start()

    swap = remote(low.at[0], swapped_one, swap_sem.at[0], swap_sem.at[1], place.neighbour("x"))
    kept = []

    def keep(source, target):
        copy = pltpu.make_async_copy(source, target, keep_sem.at[len(kept)])
        kept.append(copy)
        copy.start()

    turned = []

    def turn_over(number, layer, source, target):
        copy = pltpu.make_async_copy(source.at[:, c], target.at[layer, 0], keep_sem.at[len(kept)])
        kept.append(copy)
        copy.start()
        other = remote(
            source.at[:, 1 - c],
            target.at[layer, 1],
            turn_send.at[number, layer],
            turn_recv.at[number, layer],
            place.neighbour("core"),
        )
        other.start()
        turned.append(other)

    def norm_vectors(layer):
        window = flat(w_pack[layer, :, :, :, NORMS - 64 : NORMS + 64]).astype(F32)
        rows = window.T
        return [rows[64 + i : 65 + i, :] for i in range(4)]

    def residual(layer):
        return (x_ref if layer == 0 else low.at[0])[...].astype(F32)

    def front(layer):
        for g, l in ((0, 0), (1, 0), (1, 1)) if layer == 0 else ((0, 1),):
            from_core(g, l).wait_recv()
            keep(whole[g].at[l], whole_out[g].at[l])
        if layer == 0:
            fetch.wait()
            small_length.wait()
        vectors = norm_vectors(layer)
        unit, _ = normalized(residual(layer))
        rows = (unit * vectors[0] + vectors[1]).astype(BF)
        normed[...] = rows
        for i in range(3):
            at = slice(i * 512, (i + 1) * 512)
            qk[layer, :, at] = product(rows, flat(w_qk[layer, :, :, :, at])).astype(BF)
        keep(qk.at[layer], kept_qk.at[layer])
        values[layer, :, :HALF] = product(rows, flat(w_pack[layer, :, :, :, :HALF])).astype(BF)
        if layer == 0:
            window = slice(FIRST, FIRST + 256)
            part = [product(rows, flat(w_pack[l, :, :, :, window])) for l in range(2)]
            moved = pltpu.roll(part[1], 64, 1)
            between = jnp.where(lane_index((LEN, 128)) < 64, part[0][:, 128:], moved[:, :128])
            values[0, :, HALF : HALF + 128] = part[0][:, :128].astype(BF)
            values[0, :, HALF + 128 : HALF + 256] = between.astype(BF)
            values[0, :, HALF + 256 :] = moved[:, 128:].astype(BF)
        else:
            values[1, :, HALF:] = values[0, :, HALF:]
        keep(values.at[layer], kept_values.at[layer])
        t_normed[layer] = rows.T.reshape(8, 2, 48, LEN)
        turn_over(0, layer, t_normed.at[layer], turned_normed)

    def attend(layer, pairs):
        count = length[s]
        key = lax.broadcasted_iota(jnp.int32, (LEN, LEN), 0)
        query = lax.broadcasted_iota(jnp.int32, (LEN, LEN), 1)
        allowed = (key <= query) & (key < count)
        left = lane_index((LEN, 128)) < 64
        for pair in pairs:
            at = slice(pair * 128, (pair + 1) * 128)
            queries = qk[layer, :, at] * jnp.asarray(HD**-0.5, BF)
            keys = qk[layer, :, FEATURES + pair * 128 : FEATURES + (pair + 1) * 128]
            head_values = values[layer, :, at]
            parts = []
            for head in range(2):
                chosen = left if head == 0 else jnp.logical_not(left)
                scores = times_transposed(jnp.where(chosen, keys, jnp.zeros_like(keys)), queries)
                scores = jnp.where(allowed, scores, -1e30)
                raised = jnp.exp(scores - jnp.max(scores, axis=0, keepdims=True))
                soft = (raised / jnp.sum(raised, axis=0, keepdims=True)).astype(BF)
                probs[layer, 2 * pair + head] = soft
                parts.append(transposed_times(soft, head_values))
            attended[:, at] = jnp.where(left, parts[0], parts[1]).astype(BF)

    def project_out(layer):
        keep(probs.at[layer], kept_probs.at[layer])
        rows = attended[...]
        total = residual(layer) + product(
            rows, flat(w_pack[layer, :, :, :, HALF : HALF + FEATURES])
        )
        middle[layer] = total
        keep(middle.at[layer], kept_middle.at[layer])
        vectors = norm_vectors(layer)
        unit, _ = normalized(total)
        after = (unit * vectors[2] + vectors[3]).astype(BF)
        mixed[...] = after
        t_attended[layer] = rows.T.reshape(8, 2, 48, LEN)
        turn_over(1, layer, t_attended.at[layer], turned_attended)
        t_mixed[layer] = after.T.reshape(8, 2, 48, LEN)
        turn_over(2, layer, t_mixed.at[layer], turned_mixed)

    def widen(layer, i):
        if i % 2 == 0:
            from_core(2 + i // 2, layer).wait_recv()
        at = slice(i * 768, (i + 1) * 768)
        upper = product(mixed[...], flat(w_up[layer, :, :, :, at]))
        inner = upper * (0.7978845608028654 + 0.03567740813636141 * (upper * upper))
        bent = jnp.tanh(inner)
        half = 0.5 * (1.0 + bent)
        grown = (upper * half).astype(BF)
        active[:, at] = grown
        steep = 0.7978845608028654 + 0.10703222440908423 * (upper * upper)
        slope[layer, :, at] = (half + 0.5 * upper * (1.0 - bent * bent) * steep).astype(BF)
        t_active[layer, 2 * i : 2 * i + 2] = grown.T.reshape(2, 2, 192, LEN)

    def narrow(layer):
        keep(slope.at[layer], kept_slope.at[layer])
        turn_over(3, layer, t_active.at[layer], turned_active)
        keep(w_up.at[layer], out_up.at[layer])
        from_core(4, layer).wait_recv()
        from_core(5, layer).wait_recv()
        keep(w_down.at[layer], out_down.at[layer])
        total = middle[layer] + product(active[...], flat(w_down[layer]))
        low[layer] = total.astype(BF)
        keep(low.at[layer], kept_low.at[layer])
        if layer == 0:
            pl.when(s == 1)(swap.start)

    steps = []
    for layer in range(2):
        steps.append(functools.partial(front, layer))
        for i in range(3):
            steps.append(functools.partial(attend, layer, (2 * i, 2 * i + 1)))
        steps.append(functools.partial(project_out, layer))
        for i in range(4):
            steps.append(functools.partial(widen, layer, i))
        steps.append(functools.partial(narrow, layer))

    for number in range(len(steps) + 1):
        for k in range(4):
            if schedule[k][number]:
                pl.when(place.is_class(k))(
                    functools.partial(run_items, k, schedule[k][number])
                )
        if number < len(steps):
            steps[number]()

    for k in range(4):

        def finish(k=k):
            sent = [item[:3] for items in schedule[k] for item in items if item[0] is not None]
            for link, g, layer in sorted(set(sent)):
                blocks = whole[ARRAY_OF[g]].at[layer, 0 : sent.count((link, g, layer)), 0]
                part = piece_of(blocks, g)
                sem = send_sem.at[LINKS.index(link), g, layer]
                remote(part, part, sem, recv_sem.at[g, layer, 0], place.neighbour("x")).wait_send()

        pl.when(place.is_class(k))(finish)
    for g in range(6):
        for layer in range(2):
            hand_over(g, layer).wait_send()
    for copy in kept:
        copy.wait()
    for copy in turned:
        copy.wait()
    pl.when(s == 0)(swap.wait_recv)
    pl.when(s == 1)(swap.wait_send)


def forward_call(schedule, own, small, inputs, length):
    def hbm(shape, dtype=BF):
        return jax.ShapeDtypeStruct(shape, dtype)

    def turn(rows):
        return (2, 2, 8, rows, LEN)

    weights = [(2, 8, 2, ROWS[a], WIDTH[a]) for a in range(4)]
    kept = [
        hbm((2, LEN, 2 * FEATURES)),
        hbm((2, LEN, FEATURES)),
        hbm((2, HEADS, LEN, LEN)),
        hbm((2, LEN, HIDDEN)),
        hbm((2, LEN, FEATURES), F32),
        hbm((2, LEN, FEATURES)),
    ]
    outs = [hbm(shape) for shape in weights] + kept
    outs += [hbm(turn(48)), hbm(turn(48)), hbm(turn(48)), hbm(turn(192)), hbm((LEN, FEATURES))]
    scratch = [pltpu.VMEM(shape, BF) for shape in weights]
    scratch += [
        pltpu.VMEM((48, PACK), BF),
        pltpu.VMEM((48, 192), BF),
        pltpu.VMEM((4, 1, 48), BF),
        pltpu.SMEM((2,), jnp.int32),
        pltpu.VMEM((LEN, FEATURES), BF),
        pltpu.VMEM((LEN, FEATURES), BF),
        pltpu.VMEM((2, LEN, 2 * FEATURES), BF),
        pltpu.VMEM((2, LEN, FEATURES), BF),
        pltpu.VMEM((2, HEADS, LEN, LEN), BF),
        pltpu.VMEM((LEN, FEATURES), BF),
        pltpu.VMEM((2, LEN, FEATURES), F32),
        pltpu.VMEM((LEN, FEATURES), BF),
        pltpu.VMEM((LEN, HIDDEN), BF),
        pltpu.VMEM((2, LEN, HIDDEN), BF),
        pltpu.VMEM((2, LEN, FEATURES), BF),
        pltpu.VMEM((2, 8, 2, 48, LEN), BF),
        pltpu.VMEM((2, 8, 2, 48, LEN), BF),
        pltpu.VMEM((2, 8, 2, 48, LEN), BF),
        pltpu.VMEM((2, 8, 2, 192, LEN), BF),
        pltpu.SemaphoreType.DMA((6, 2, 8)),
        pltpu.SemaphoreType.DMA((4, 6, 2)),
        pltpu.SemaphoreType.DMA((6, 2)),
        pltpu.SemaphoreType.DMA((6, 2)),
        pltpu.SemaphoreType.DMA((6,)),
        pltpu.SemaphoreType.DMA((28,)),
        pltpu.SemaphoreType.DMA((4, 2)),
        pltpu.SemaphoreType.DMA((4, 2)),
        pltpu.SemaphoreType.DMA((9,)),
        pltpu.SemaphoreType.DMA((2,)),
    ]
    anywhere = pl.BlockSpec(memory_space=pl.ANY)
    return pl.pallas_call(
        functools.partial(forward_kernel, schedule),
        out_shape=outs,
        in_specs=[anywhere] * 12,
        out_specs=[anywhere] * len(outs),
        scratch_shapes=scratch,
        compiler_params=pltpu.CompilerParams(
            collective_id=0, has_side_effects=True, vmem_limit_bytes=62 * 2**20
        ),
    )(*own, *small, inputs, length)


def schedule_of(codes):
    result = []
    for per_class in codes:
        result.append([])
        for numbers in per_class:
            items = []
            for n in numbers:
                link = None if n < 10000 else LINKS[n // 10000 - 1]
                items.append((link, n // 1000 % 10, n // 100 % 10, n // 10 % 10, n % 10))
            result[-1].append(items)
    return result


def branches(order, rx, ry, j):
    apart = {"x": rx != 0, "y": ry != 0, "z": j != 0}
    last = max([i for i, axis in enumerate(order) if apart[axis]], default=-1)
    links = []
    for i, axis in enumerate(order):
        if i < last:
            continue
        if axis != "z":
            if i > last:
                links.append((axis, False))
        elif i > last:
            links += [("near", False), ("far", True)]
        else:
            links.append(("far" if j == 1 else "near", True))
    return links


def slot_table(orders):
    table, counts = {}, []
    for g in range(6):
        number = 0
        for rx in range(2):
            for ry in range(2):
                for j in range(4):
                    links = []
                    for layer in range(2):
                        for link, _ in branches(orders[g, layer], rx, ry, j):
                            if link not in links:
                                links.append(link)
                    for link in links:
                        table[g, rx, ry, j, link] = number
                        number += 1
        counts.append(number)
    return table, counts


def towards_owner(order, k, rx, ry, j):
    apart = {"x": rx != 0, "y": ry != 0, "z": j != 0}
    axis = [axis for axis in order if apart[axis]][-1]
    if axis == "x":
        return "x", (0, ry, j)
    if axis == "y":
        return "y", (rx, 0, j)
    if j == 1:
        return "near", (rx, ry, 0)
    if k % 2:
        return "far", (rx, ry, 0 if j == 2 else 1)
    return "near", (rx, ry, j)


def backward_kernel(
    schedule, order_of_steps, orders, slots,
    w_qk, w_pack, w_up, w_down,
    kept_qk, kept_values, kept_probs, kept_slope, kept_middle, kept_low,
    turned_normed, turned_attended, turned_mixed, turned_active,
    inputs, cotangent, lengths,
    out_qk, out_pack, out_up, out_down, out_grads, swapped_low, swapped_grad,
    m_qk, m_pack, m_wide,
    qk, values, probs, slope, middle, entering, t_normed, t_attended, t_mixed, t_active,
    cot, length,
    dy, du, da, dqk, dv,
    far_dy, far_du, far_da, far_dqk, far_dv,
    total, d_mixed, d_attended, shared_two, grads, vectors, far_vectors, columns,
    h_qk, h_pack, h_up, h_down,
    arrived_0, arrived_1, arrived_2, arrived_3, arrived_4, arrived_5,
    r_qk, r_pack, r_up, r_down,
    load_sem, pair_send, pair_recv, credit, swap_send, swap_recv, sum_send, sum_recv, out_sem,
):
    place = Place()
    s, c = place.s, place.c
    held = (h_qk, h_pack, h_up, h_down)
    arrived = (arrived_0, arrived_1, arrived_2, arrived_3, arrived_4, arrived_5)
    result = (r_qk, r_pack, r_up, r_down)
    outs = (out_qk, out_pack, out_up, out_down)

    sources = {
        "qk_matrix": (m_qk, lambda l: w_qk.at[l]),
        "pack0": (m_pack.at[0], lambda l: w_pack.at[0]),
        "pack1": (m_pack.at[1], lambda l: w_pack.at[1]),
        "down0": (m_wide.at[0:16], lambda l: w_down.at[l, pl.ds(0, 16)]),
        "down1": (m_wide.at[16:32], lambda l: w_down.at[l, pl.ds(16, 16)]),
        "down2": (m_wide.at[32:48], lambda l: w_down.at[l, pl.ds(32, 16)]),
        "down3": (m_wide.at[48:64], lambda l: w_down.at[l, pl.ds(48, 16)]),
        "up0": (m_wide.at[0:16], lambda l: w_up.at[l, :, :, pl.ds(0, 768)]),
        "up1": (m_wide.at[16:32], lambda l: w_up.at[l, :, :, pl.ds(768, 768)]),
        "up2": (m_wide.at[32:48], lambda l: w_up.at[l, :, :, pl.ds(1536, 768)]),
        "up3": (m_wide.at[48:64], lambda l: w_up.at[l, :, :, pl.ds(2304, 768)]),
        "qk": (qk, lambda l: kept_qk.at[l]),
        "values": (values, lambda l: kept_values.at[l]),
        "probs": (probs, lambda l: kept_probs.at[l]),
        "slope": (slope, lambda l: kept_slope.at[l]),
        "middle": (middle, lambda l: kept_middle.at[l]),
        "entering": (entering, lambda l: inputs.at[s, 0] if l == 0 else kept_low.at[0]),
        "normed": (t_normed, lambda l: turned_normed.at[l]),
        "attended": (t_attended, lambda l: turned_attended.at[l]),
        "mixed": (t_mixed, lambda l: turned_mixed.at[l]),
        "active": (t_active, lambda l: turned_active.at[l]),
        "cotangent": (cot, lambda l: cotangent.at[s, 0]),
    }
    names = list(sources)

    def loading(name, layer):
        target, source = sources[name]
        return pltpu.make_async_copy(
            source(layer), target, load_sem.at[names.index(name)]
        )

    def load(*which, layer):
        for name in which:
            loading(name, layer).start()

    def loaded(*which, layer):
        for name in which:
            loading(name, layer).wait()

    fetch_length = pltpu.make_async_copy(lengths, length, out_sem.at[8])
    fetch_length.start()
    load("cotangent", "down0", "slope", "down1", "down2", "down3", layer=1)
    greet(place)

    across = place.neighbour("x")
    low_swap = remote(kept_low.at[1], swapped_low, swap_send.at[0], swap_recv.at[0], across)
    grad_swap = remote(grads.at[1 - s], swapped_grad, swap_send.at[1], swap_recv.at[1], across)

    shared = {
        "dy": (dy, far_dy),
        "du0": (du.at[:, 0:1536], far_du.at[:, 0:1536]),
        "du1": (du.at[:, 1536:3072], far_du.at[:, 1536:3072]),
        "da": (da, far_da),
        "dqk": (dqk, far_dqk),
        "dv": (dv, far_dv),
        "vectors": (vectors, far_vectors),
    }
    shared_names = list(shared)

    def exchange(name, layer):
        n = shared_names.index(name)
        return remote(
            *shared[name], pair_send.at[n], pair_recv.at[n], place.neighbour("core")
        )

    def hand(name, layer):
        if layer == 0:
            pl.semaphore_wait(credit.at[shared_names.index(name)], 1)
        exchange(name, layer).start()

    def done_with(name, layer):
        if layer == 1:
            pl.semaphore_signal(
                credit.at[shared_names.index(name)],
                1,
                device_id=place.neighbour("core"),
                device_id_type=MESH,
            )

    def free_to_write(name, layer):
        if layer == 0:
            exchange(name, 1).wait_send()

    def summed(left, right, far_right):
        return product(flat3(left[0]), right) + product(flat3(left[1]), far_right)

    def flat3(block):
        return block.reshape(-1, block.shape[-1])

    def norm_rows(layer):
        window = flat(m_pack[layer, :, :, :, NORMS - 64 : NORMS + 64]).astype(F32)
        rows = window.T
        return [rows[64 + i : 65 + i, :] for i in range(4)]

    def norm_back(grad, rows, gain):
        unit, scale = normalized(rows)
        scaled = grad * gain
        inner = scaled - jnp.mean(scaled, axis=-1, keepdims=True)
        inner = inner - unit * jnp.mean(scaled * unit, axis=-1, keepdims=True)
        return (
            jnp.sum(grad * unit, axis=0, keepdims=True),
            jnp.sum(grad, axis=0, keepdims=True),
            scale * inner,
        )

    def begin(layer):
        if layer == 1:
            vectors[...] = jnp.zeros_like(vectors)
            loaded("cotangent", layer=1)
            fetch_length.wait()
            position = lax.broadcasted_iota(jnp.int32, (LEN, FEATURES), 0)
            grad = jnp.where(position < length[s], cot[...].astype(F32), 0.0)
        else:
            grad = grads[1].astype(F32)
        free_to_write("dy", layer)
        total[...] = grad
        dy[...] = grad.astype(BF)
        if layer == 0:
            hand("dy", layer)

    def through_active(layer, i):
        if i == 0:
            loaded("slope", layer=layer)
            if layer == 1:
                load("active", "mixed", "middle", "pack1", "qk", "values", layer=1)
                load("probs", "attended", "entering", "qk_matrix", "normed", layer=1)
                load("pack0", layer=0)
        if i % 2 == 0:
            free_to_write("du%d" % (i // 2), layer)
        loaded("down%d" % i, layer=layer)
        at = slice(i * 768, (i + 1) * 768)
        grad = times_transposed(dy[...], flat3(m_wide[16 * i : 16 * i + 16]))
        du[:, at] = (grad * slope[:, at].astype(F32)).astype(BF)
        if i == 0 and layer == 1:
            meet(place)
            hand("dy", layer)
            pl.when(s == 0)(low_swap.start)
        if i % 2 == 1:
            hand("du%d" % (i // 2), layer)
        if i == 3:
            load("up0", "up1", "up2", "up3", layer=layer)
            if layer == 1:
                load("slope", layer=0)

    def sum_down(layer, half):
        if half == 0:
            loaded("active", layer=layer)
            exchange("dy", layer).wait_recv()
        rows = slice(half * 96, half * 96 + 96)
        sums = summed(t_active[:, :, rows, :], dy[...], far_dy[...])
        h_down[layer, :, rows, :] = sums.astype(BF).reshape(8, 96, FEATURES)
        if half == 1:
            done_with("dy", layer)
            if layer == 1:
                load("active", layer=0)

    def to_mixed(layer):
        for q in range(4):
            loaded("up%d" % q, layer=layer)
            part = times_transposed(
                du[:, q * 768 : (q + 1) * 768], flat3(m_wide[16 * q : 16 * q + 16])
            )
            d_mixed[...] = part if q == 0 else d_mixed[...] + part
        if layer == 1:
            load("down0", "down1", "down2", "down3", layer=0)

    def sum_up(layer, q):
        if q == 0:
            loaded("mixed", layer=layer)
        if q % 2 == 0:
            exchange("du%d" % (q // 2), layer).wait_recv()
        at = slice(q * 768, (q + 1) * 768)
        sums = summed(t_mixed[...], du[:, at], far_du[:, at])
        h_up[layer, :, :, at] = sums.astype(BF).reshape(8, 48, 768)
        if q % 2 == 1:
            done_with("du%d" % (q // 2), layer)
        if q == 3 and layer == 1:
            load("mixed", layer=0)

    def second_norm(layer):
        loaded("middle", "pack%d" % layer, layer=layer)
        free_to_write("vectors", layer)
        free_to_write("da", layer)
        gain, bias, through = norm_back(d_mixed[...], middle[...], norm_rows(layer)[2])
        vectors[2:3, :] = gain
        vectors[3:4, :] = bias
        grad = total[...] + through
        total[...] = grad
        da[...] = grad.astype(BF)
        hand("da", layer)
        matrix = flat(m_pack[layer, :, :, :, HALF:FIRST])
        d_attended[...] = times_transposed(da[...], matrix).astype(BF)
        if layer == 1:
            load("middle", layer=0)

    def through_attention(layer, pair):
        if pair == 0:
            loaded("qk", "values", "probs", layer=layer)
            free_to_write("dqk", layer)
            free_to_write("dv", layer)
        left = lane_index((LEN, 128)) < 64
        at = slice(pair * 128, (pair + 1) * 128)
        key_at = slice(FEATURES + pair * 128, FEATURES + (pair + 1) * 128)
        queries, keys, head_values = qk[:, at], qk[:, key_at], values[:, at]
        grad = d_attended[:, at]
        parts = []
        for head in range(2):
            chosen = left if head == 0 else jnp.logical_not(left)
            soft = probs[2 * pair + head]
            to_soft = times_transposed(
                jnp.where(chosen, head_values, jnp.zeros_like(head_values)), grad
            )
            exact = soft.astype(F32)
            inner = jnp.sum(exact * to_soft, axis=0, keepdims=True)
            to_scores = (exact * (to_soft - inner)).astype(BF)
            parts.append(
                (
                    transposed_times(to_scores, keys),
                    product(to_scores, queries),
                    product(soft, grad),
                )
            )
        of_queries, of_keys, of_values = [
            jnp.where(left, one, other) for one, other in zip(*parts)
        ]
        dqk[:, at] = (of_queries * HD**-0.5).astype(BF)
        dqk[:, key_at] = (of_keys * HD**-0.5).astype(BF)
        if pair < 3:
            dv[:, at] = of_values.astype(BF)
        else:
            there = slice((pair - 3) * 128, (pair - 2) * 128)
            if layer == 1:
                shared_two[:, there] = of_values.astype(BF)
            else:
                dv[:, at] = (of_values + shared_two[:, there].astype(F32)).astype(BF)
        if pair == 5:
            hand("dqk", layer)
            hand("dv", layer)
            if layer == 1:
                load("qk", "values", "probs", layer=0)

    def first_window(part):
        if part == 0:
            window = lambda ref: ref[:, HALF : HALF + 256]
        else:
            window = lambda ref: pltpu.roll(
                ref[:, HALF + 128 :].astype(F32), 192, 1
            ).astype(BF)
        inside = lane_index((LEN, 256)) < 192
        return [
            jnp.where(inside, window(ref), jnp.zeros((LEN, 256), BF)) for ref in (dv, far_dv)
        ]

    def first_norm(layer):
        loaded("qk_matrix", "entering", layer=layer)
        grad = times_transposed(dqk[...], flat(m_qk[...]))
        grad = grad + times_transposed(dv[:, :HALF], flat(m_pack[layer, :, :, :, :HALF]))
        if layer == 0:
            for part in range(2):
                grad = grad + times_transposed(
                    first_window(part)[0], flat(m_pack[part, :, :, :, FIRST : FIRST + 256])
                )
        rows = entering[...].astype(F32)
        gain, bias, through = norm_back(grad, rows, norm_rows(layer)[0])
        vectors[0:1, :] = gain
        vectors[1:2, :] = bias
        hand("vectors", layer)
        grads[layer] = (total[...] + through).astype(BF)
        own_grads(layer).start()
        if layer == 1:
            load("qk_matrix", "entering", layer=0)
        pl.when(s == 1 - layer)(grad_swap.start)

    def sum_out(layer):
        loaded("attended", layer=layer)
        exchange("da", layer).wait_recv()
        sums = summed(t_attended[...], da[...], far_da[...])
        h_pack[layer, :, :, HALF:FIRST] = sums.astype(BF).reshape(8, 48, FEATURES)
        done_with("da", layer)
        if layer == 1:
            load("attended", layer=0)

    def sum_qk(layer):
        loaded("normed", layer=layer)
        exchange("dqk", layer).wait_recv()
        for q in range(2):
            at = slice(q * FEATURES, (q + 1) * FEATURES)
            sums = summed(t_normed[...], dqk[:, at], far_dqk[:, at])
            h_qk[layer, :, :, at] = sums.astype(BF).reshape(8, 48, FEATURES)
        done_with("dqk", layer)

    def sum_pack(layer):
        exchange("dv", layer).wait_recv()
        exchange("vectors", layer).wait_recv()
        sums = summed(t_normed[...], dv[:, :HALF], far_dv[:, :HALF])
        h_pack[layer, :, :, :HALF] = sums.astype(BF).reshape(8, 48, HALF)
        both = vectors[...] + far_vectors[...]
        nothing = jnp.zeros((64, FEATURES), F32)
        tall = jnp.concatenate([nothing, both, nothing[:56]], axis=0)
        columns[layer] = tall.T.astype(BF).reshape(8, 2, 48, 128)
        if layer == 0:
            for part in range(2):
                sums = summed(t_normed[...], *first_window(part)).reshape(8, 48, 256)
                h_pack[part, :, :, FIRST : FIRST + 128] = sums[:, :, :128].astype(BF)
                h_pack[part, :, :, FIRST + 128 :] = (
                    sums[:, :, 128:] + columns[part, :, c].astype(F32)
                ).astype(BF)
        done_with("dv", layer)
        done_with("vectors", layer)
        if layer == 1:
            load("normed", layer=0)

    def own_grads(layer):
        return pltpu.make_async_copy(grads.at[layer], out_grads.at[layer], out_sem.at[6 + layer])

    steps = []

    def step(action, *arguments):
        steps.append(functools.partial(action, *arguments))

    for layer in (1, 0):
        step(begin, layer)
        for i in range(4):
            step(through_active, layer, i)
        for half in range(2):
            step(sum_down, layer, half)
        step(to_mixed, layer)
        for q in range(4):
            step(sum_up, layer, q)
        step(second_norm, layer)
        for pair in range(6):
            step(through_attention, layer, pair)
        step(sum_out, layer)
        step(first_norm, layer)
        step(sum_qk, layer)
        step(sum_pack, layer)

    steps = [steps[number] for number in order_of_steps]

    first_slot = [sum(ref.shape[0] for ref in arrived[:g]) for g in range(6)]

    def sum_copy(k, item):
        g, layer, ry, j = item
        rx = int(k // 2 != layer)
        link, there = towards_owner(orders[g, layer], k, rx, ry, j)
        return remote(
            piece_of(held[ARRAY_OF[g]].at[layer, place.block(ry, j)], g),
            arrived[g].at[slots[(g,) + there + (link,)]],
            sum_send.at[g, layer],
            sum_recv.at[first_slot[g] + slots[(g,) + there + (link,)]],
            place.neighbour(link),
        )

    def run_items(k, items):
        for item in items:
            g, layer, ry, j = item
            rx = int(k // 2 != layer)
            mine = piece_of(held[ARRAY_OF[g]].at[layer, place.block(ry, j)], g)
            terms = []
            for link, middle_only in branches(orders[g, layer], rx, ry, j):
                if middle_only and not k % 2:
                    continue
                slot = slots[g, rx, ry, j, link]
                remote(
                    mine,
                    arrived[g].at[slot],
                    sum_send.at[g, layer],
                    sum_recv.at[first_slot[g] + slot],
                    place.neighbour(link),
                ).wait_recv()
                terms.append(arrived[g].at[slot])
            final = (rx, ry, j) == (0, 0, 0)
            target = piece_of(result[ARRAY_OF[g]], g) if final else mine
            if terms or final:
                add_up(target, [mine] + terms)
            if not final:
                sum_copy(k, item).start()
                continue
            out = piece_of(outs[ARRAY_OF[g]], g)
            pltpu.make_async_copy(target, out, out_sem.at[g]).start()

    def add_up(target, terms):
        @pl.loop(0, target.shape[0] // 16)
        def _(i):
            at = pl.ds(pl.multiple_of(i * 16, 16), 16)
            sums = terms[0][at, :].astype(F32)
            for term in terms[1:]:
                sums = sums + term[at, :].astype(F32)
            target[at, :] = sums.astype(target.dtype)

    for number in range(len(steps) + 1):
        for k in range(4):
            if schedule[k][number]:
                pl.when(place.is_class(k))(
                    functools.partial(run_items, k, schedule[k][number])
                )
        if number < len(steps):
            steps[number]()

    for k in range(4):

        def finish(k=k):
            for g in range(6):
                for layer in range(2):
                    own = k // 2 == layer
                    if own:
                        pltpu.make_async_copy(
                            piece_of(result[ARRAY_OF[g]], g),
                            piece_of(outs[ARRAY_OF[g]], g),
                            out_sem.at[g],
                        ).wait()
                    part = piece_of(held[ARRAY_OF[g]].at[layer, 0 : 7 if own else 8], g)
                    remote(
                        part, part, sum_send.at[g, layer], sum_recv.at[0], place.neighbour("x")
                    ).wait_send()

        pl.when(place.is_class(k))(finish)
    for name in shared_names:
        exchange(name, 0).wait_send()
    pl.when(s == 0)(low_swap.wait_send)
    pl.when(s == 1)(low_swap.wait_recv)
    grad_swap.wait()
    for layer in range(2):
        own_grads(layer).wait()


def backward_call(schedule, order_of_steps, orders, weights, kept, turned, inputs, cotangent, lengths):
    slots, counts = slot_table(orders)
    blocks = [(48, 2 * FEATURES), (48, PACK), (48, HIDDEN), (192, FEATURES)]
    pieces = [(48, 1536), (48, PACK), (48, 1536), (48, 1536), (96, FEATURES), (96, FEATURES)]
    rows = (LEN, FEATURES)
    outs = [jax.ShapeDtypeStruct(block, F32) for block in blocks]
    outs += [jax.ShapeDtypeStruct((2,) + rows, BF)] + [jax.ShapeDtypeStruct(rows, BF)] * 2
    pair = [rows, (LEN, HIDDEN), rows, (LEN, 2 * FEATURES), rows]
    scratch = [
        pltpu.VMEM((8, 2, 48, 2 * FEATURES), BF),
        pltpu.VMEM((2, 8, 2, 48, PACK), BF),
        pltpu.VMEM((64, 48, FEATURES), BF),
        pltpu.VMEM((LEN, 2 * FEATURES), BF),
        pltpu.VMEM(rows, BF),
        pltpu.VMEM((HEADS, LEN, LEN), BF),
        pltpu.VMEM((LEN, HIDDEN), BF),
        pltpu.VMEM(rows, F32),
        pltpu.VMEM(rows, BF),
        pltpu.VMEM((2, 8, 48, LEN), BF),
        pltpu.VMEM((2, 8, 48, LEN), BF),
        pltpu.VMEM((2, 8, 48, LEN), BF),
        pltpu.VMEM((2, 8, 192, LEN), BF),
        pltpu.VMEM(rows, BF),
        pltpu.SMEM((2,), jnp.int32),
    ]
    scratch += [pltpu.VMEM(shape, BF) for shape in pair + pair]
    scratch += [
        pltpu.VMEM(rows, F32),
        pltpu.VMEM(rows, F32),
        pltpu.VMEM(rows, BF),
        pltpu.VMEM((LEN, HALF), BF),
        pltpu.VMEM((2,) + rows, BF),
        pltpu.VMEM((8, FEATURES), F32),
        pltpu.VMEM((8, FEATURES), F32),
        pltpu.VMEM((2, 8, 2, 48, 128), BF),
    ]
    scratch += [pltpu.VMEM((2, 8) + block, BF) for block in blocks]
    scratch += [pltpu.VMEM((count,) + piece, BF) for count, piece in zip(counts, pieces)]
    scratch += [pltpu.VMEM(block, F32) for block in blocks]
    scratch += [
        pltpu.SemaphoreType.DMA((22,)),
        pltpu.SemaphoreType.DMA((7,)),
        pltpu.SemaphoreType.DMA((7,)),
        pltpu.SemaphoreType.REGULAR((7,)),
        pltpu.SemaphoreType.DMA((2,)),
        pltpu.SemaphoreType.DMA((2,)),
        pltpu.SemaphoreType.DMA((6, 2)),
        pltpu.SemaphoreType.DMA((sum(counts),)),
        pltpu.SemaphoreType.DMA((9,)),
    ]
    anywhere = pl.BlockSpec(memory_space=pl.ANY)
    operands = [
        weights[0],
        weights[1],
        weights[2].reshape(2, 16, 48, HIDDEN),
        weights[3].reshape(2, 64, 48, FEATURES),
    ]
    operands += list(kept) + list(turned) + [inputs, cotangent]
    return pl.pallas_call(
        functools.partial(backward_kernel, schedule, order_of_steps, orders, slots),
        out_shape=outs,
        in_specs=[anywhere] * (len(operands) + 1),
        out_specs=[anywhere] * len(outs),
        scratch_shapes=scratch,
        compiler_params=pltpu.CompilerParams(
            collective_id=1, has_side_effects=True, vmem_limit_bytes=63 * 2**20
        ),
    )(*operands, lengths)


GATHER = (
    (
        (13000, 11000, 15000, 30000, 31000, 14000, 33000, 25000, 12000, 34000, 21000, 24000,
        5010, 22000, 0, 1000, 2000, 3000, 4000, 5000, 10000, 5100, 2100, 35000, 20000, 4010,
        2010, 23000, 12010, 1001, 1, 32010, 20001, 3100, 2, 10001, 2101, 20002, 10002, 22101,
        1100, 2001, 23100, 32000, 21100, 22100, 3, 34010, 10, 14010, 3010, 15010, 11, 5011,
        3001, 12001, 5001, 35100, 2002, 1110, 100, 10010, 35010, 10003, 20003, 12002, 23001, 12,
        1002, 3002, 23002, 1003, 25100, 15011, 13, 1102, 21001, 101, 1103, 1101, 3011, 21002,
        10011, 4102, 21101, 10013, 2011, 10012, 21103, 1011, 12011, 1012, 3102, 2003, 2013,
        1111, 12003, 2102, 22102, 5012, 5002, 1113, 1010, 12013, 3101, 21102, 3103, 3003, 5003,
        15012, 21003, 2012, 5013, 15013, 23003, 15002, 5110, 23101, 1013, 23102, 12012, 1112,
        15003),
        (2103, 4101, 4001),
        (),
        (110, 22103),
        (23103, 15001, 112, 4110, 3013),
        (4002, 4013, 5102, 102, 111, 3012, 2113, 2111, 3111, 25102, 4012, 103, 4011, 2112),
        (113, 3112, 4003),
        (),
        (3113, 2110),
        (3110, 4103, 5101, 25101, 4100),
        (4112,),
        (5112, 5103, 25103, 4113),
        (),
        (),
        (4111,),
        (5111, 5113),
        (),
        (),
        (),
        (),
        (),
    ),
    (
        (13000, 32000, 35000, 20000, 10000, 45000, 14000, 40000, 24000, 21000, 33000, 1, 30000,
        22000, 0, 1000, 2000, 3000, 4000, 5000, 42000, 15000, 40001, 31000, 1001, 5002, 11000,
        2002, 2, 41001, 20001, 10001, 2010, 3001, 42010, 30002, 20002, 43001, 10, 4001, 15002,
        43000, 12010, 41000, 3, 25000, 1100, 11, 30003, 44000, 10003, 34000, 21001, 1101, 32002,
        21100, 1102, 21101, 5010, 1003, 3002, 15010, 45010, 35010, 1002, 21003, 2001, 5001,
        12000, 31003, 21102, 23002, 23000, 1111, 23001, 4010, 2011, 31002, 5100, 2102, 4002,
        45001, 10011, 12, 2012, 33002, 12002, 12001, 42011, 3100, 1011, 32012, 32010, 1103,
        42001, 44010, 5101, 21103, 3003, 10010, 45100, 10012, 5012, 35002, 5003, 2013, 2003,
        4102, 23003, 14010, 21002, 4012, 15001, 20003, 45101, 113, 32003, 4011, 1113, 5102, 101,
        1110, 32013, 3103, 12013, 10002, 35012, 44011, 3010, 23103, 1012, 5103, 1010, 5011,
        1112, 3011, 1013, 12003, 33003, 12011, 45011, 22102, 4013, 3102, 13, 23102, 35003,
        10013),
        (5013, 35013, 35102),
        (2103, 2100, 22103, 34010, 25100, 12012, 44001, 4003, 15012, 2113, 34012, 23100),
        (34013, 3101, 34002),
        (),
        (15011, 3013, 15013, 22100, 25102),
        (2112, 2101, 111, 34003, 103, 3012),
        (102, 2110, 15003, 22101, 5110, 3112, 112, 110, 25103, 100, 35100, 4112, 3113),
        (),
        (4110,),
        (23101, 2111, 5112, 35103),
        (4101, 4113, 25101),
        (5113,),
        (),
        (4111,),
        (3111, 3110, 4100),
        (4103,),
        (5111,),
        (),
        (),
        (),
    ),
    (
        (12100, 22100, 34100, 24100, 11100, 23100, 31100, 30100, 15100, 13100, 4110, 21100,
        2101, 1101, 100, 1100, 2100, 3100, 4100, 5100, 3000, 14100, 12101, 4101, 1000, 23000,
        32100, 10100, 31000, 101, 11101, 24101, 21000, 20101, 33100, 3101, 5000, 25100, 4000,
        21101, 20100, 34000, 14110, 4102, 23101, 3010, 1010, 35100, 14102, 0, 14101, 1103,
        13101, 4010, 1102, 22101, 33000, 34010, 3001, 11102, 21102, 23001, 3110, 10101, 11103,
        1001, 2102, 3102, 2110, 21103, 110, 4111, 13102, 24102, 102, 1002, 21001, 12102, 1110,
        103, 10110, 20102, 3103, 13, 1113, 14111, 5011, 21002, 2111, 10, 3, 2, 4112, 1003, 111,
        21003, 23103, 13103, 2103, 5110, 2002, 1011, 3002, 1111, 112, 4103, 14112, 1013, 1112,
        10103, 2010, 1012, 20103, 12, 3003, 1, 5010, 11, 3113, 24103, 12103, 2001, 22102, 3011),
        (10112, 113, 23003, 2003, 2000, 4012, 2011, 2013),
        (5013, 23002, 10102),
        (4113, 22103, 23102, 10111, 2112, 2012, 10113, 3013),
        (4001, 5012, 4013, 5002, 14103, 14113),
        (3012, 4002, 5003),
        (),
        (5101, 25101, 4003, 4011, 5001),
        (),
        (3112, 5103, 2113, 25103),
        (3111,),
        (5111, 5102, 25102),
        (),
        (),
        (),
        (5113, 5112),
        (),
        (),
        (),
        (),
        (),
    ),
    (
        (42100, 20100, 32100, 31100, 34100, 25100, 10100, 11100, 44100, 30100, 13100, 2102,
        41100, 21100, 100, 1100, 2100, 3100, 4100, 5100, 12100, 12102, 4101, 3000, 40100, 4102,
        32102, 1101, 43000, 24102, 22102, 33100, 1102, 24100, 102, 33000, 11101, 1110, 101,
        21101, 40101, 34102, 1000, 2101, 41101, 4110, 11102, 10101, 15100, 31102, 5110, 44101,
        103, 20103, 1103, 43100, 22100, 5002, 3101, 31103, 113, 41000, 1001, 11103, 41001,
        23000, 3102, 21000, 5000, 0, 4000, 30103, 1111, 43101, 31000, 10103, 20102, 1002, 4001,
        33102, 14102, 20101, 42101, 13102, 10113, 112, 1003, 44000, 1, 3103, 14101, 21003,
        13103, 30102, 3001, 12101, 2000, 24101, 4103, 111, 4011, 31002, 44001, 43001, 31003,
        33103, 11, 1013, 21002, 4002, 44011, 3002, 2103, 23001, 45100, 4112, 12103, 4003, 2110,
        23002, 34103, 4010, 14110, 21001, 33002, 5101, 13101, 3012, 21102, 32103, 3003, 10102,
        33003, 44010, 34000, 2010, 2112, 12, 14103, 3, 23100, 2001, 24103, 4012, 3110, 10111,
        34012, 1112, 1012, 21103, 45101, 110, 1011, 34010, 4013, 1010, 23003, 5102, 10112,
        23103, 5103, 2, 4113, 2002, 34002, 13, 10, 10110, 35100, 23101, 22103, 25101, 1113,
        14112, 34013, 14113, 3011),
        (),
        (2013, 2011, 34003, 2012, 5011, 2003, 5010, 14100, 3013, 35103, 23102, 5012, 3111,
        22101, 3010),
        (),
        (2113, 4111, 14111, 5013),
        (35102, 5001),
        (25103, 5003),
        (),
        (25102,),
        (),
        (3113,),
        (5111, 2111),
        (),
        (3112,),
        (5113,),
        (5112,),
        (),
        (),
        (),
        (),
        (),
    ),
)

SUMS = (
    (
        (),
        (),
        (),
        (),
        (),
        (),
        (),
        (5112,),
        (),
        (2112, 5111, 4113, 2111),
        (),
        (),
        (),
        (5102, 2113, 5103),
        (5101,),
        (3112,),
        (),
        (),
        (),
        (2110,),
        (3113,),
        (),
        (111,),
        (),
        (2103, 113),
        (5113, 4102),
        (),
        (),
        (),
        (112, 3103),
        (),
        (),
        (5013,),
        (2102, 4012),
        (5011,),
        (),
        (103, 2013),
        (2012, 5003),
        (),
        (3100, 3013),
        (2101, 3110, 4100, 5012, 5001, 4112),
        (),
        (),
        (3011, 4013, 102, 4110),
        (),
        (4111, 3101),
        (3012, 5002, 1112, 3102, 2011, 2003, 1013, 110, 4003, 1113, 3003, 13, 2002, 100, 1102,
        1003, 1011, 4103, 3, 4101, 1111, 1010, 3111, 2001, 4002, 3010, 12, 1103, 2010, 1012,
        101, 3002, 11, 2100, 5110, 2, 1101, 4010, 1110, 4011, 1002, 10, 1001, 5010, 3001, 5100,
        1, 4001, 1100, 2000, 4000, 0, 1000, 3000, 5000),
    ),
    (
        (),
        (),
        (),
        (),
        (),
        (),
        (),
        (),
        (),
        (2112, 2113, 2111),
        (),
        (),
        (),
        (),
        (4112,),
        (4103, 4113),
        (),
        (),
        (3103,),
        (2110,),
        (),
        (),
        (),
        (),
        (110, 113),
        (),
        (111,),
        (4111, 112),
        (),
        (4102,),
        (3113,),
        (5102, 3102, 3110, 3100),
        (2103, 5103),
        (),
        (2011,),
        (),
        (),
        (5013,),
        (5112,),
        (3010, 3012, 2013, 4013, 102, 5003, 2102, 3111),
        (2010, 3013, 3112),
        (),
        (5113, 5012, 2100, 4012),
        (),
        (5001, 101, 5100),
        (4011, 3011, 103, 5110, 2101),
        (1013, 3003, 2012, 1011, 5011, 1110, 5111, 1113, 4003, 5101, 5002, 4001, 1010, 2003,
        4100, 3001, 1111, 2002, 3101, 1112, 13, 1003, 12, 4002, 11, 4110, 1103, 3002, 1102,
        1012, 1101, 100, 1001, 5010, 3, 2001, 4101, 10, 2000, 1100, 2, 1, 4010, 1002, 0, 3000,
        5000, 1000, 4000),
    ),
    (
        (),
        (),
        (),
        (),
        (),
        (),
        (),
        (5101,),
        (),
        (2112, 5103),
        (2113,),
        (),
        (5102,),
        (),
        (),
        (2111,),
        (5113,),
        (),
        (),
        (),
        (4113, 5111),
        (),
        (),
        (110, 5112),
        (),
        (),
        (113,),
        (3113, 4012, 4000),
        (),
        (3112,),
        (2103,),
        (5013, 4011),
        (),
        (),
        (),
        (),
        (2012, 2010, 5012, 4013, 2102, 4010, 5003),
        (),
        (),
        (3013,),
        (),
        (),
        (),
        (3103,),
        (),
        (2002, 2013, 5002, 4003, 3003),
        (1013, 10, 5001, 1112, 13, 3, 5011, 112, 2003, 4112, 3012, 2101, 1003, 103, 3011, 1012,
        11, 4102, 4002, 0, 12, 1113, 3002, 1011, 1103, 1010, 4111, 3001, 2, 4103, 3010, 102,
        1002, 1102, 2011, 5010, 1110, 111, 5000, 1, 3111, 2000, 2001, 1001, 1111, 3102, 5110,
        4001, 4101, 1000, 3000, 1101, 3110, 2110, 4110, 100, 101, 3101, 5100, 3100, 2100, 1100,
        4100),
    ),
    (
        (),
        (),
        (),
        (),
        (),
        (),
        (),
        (),
        (),
        (2112,),
        (),
        (2113,),
        (),
        (2111,),
        (),
        (),
        (),
        (),
        (),
        (5103,),
        (2110,),
        (),
        (),
        (),
        (110,),
        (),
        (),
        (4112,),
        (4013,),
        (4002, 4011),
        (112,),
        (),
        (),
        (),
        (2013,),
        (3013,),
        (113, 4001),
        (),
        (2011, 3011),
        (),
        (2012, 3012, 2103),
        (5102,),
        (4012, 3010),
        (111, 4113),
        (2102,),
        (3113, 4003, 5003),
        (3003, 12, 4010, 1012, 2010, 5113, 1113, 10, 5013, 3001, 5012, 3002, 3111, 2003, 1013,
        4000, 2002, 13, 1, 1011, 11, 5001, 4111, 5002, 5011, 5112, 5000, 103, 2100, 5111, 3112,
        3, 5010, 2001, 4102, 1112, 2101, 1111, 1003, 3103, 4103, 5101, 1001, 102, 1103, 2, 1010,
        1002, 4110, 101, 5110, 2000, 0, 1110, 1102, 3000, 3101, 3102, 1101, 3110, 4100, 4101,
        1000, 100, 1100, 5100, 3100),
    ),
)

STEPS = (
    0, 1, 2, 3, 5, 4, 6, 8, 9, 10, 7, 11, 12, 13, 14, 15, 16, 17, 18, 19, 20, 21, 23, 22, 24,
    28, 25, 26, 27, 29, 30, 31, 32, 33, 34, 35, 36, 37, 38, 39, 40, 41, 42, 43, 44, 45,
)

ORDERS = {
    (0, 0): "zyx",
    (0, 1): "zxy",
    (1, 0): "xzy",
    (1, 1): "xzy",
    (2, 0): "xzy",
    (2, 1): "xzy",
    (3, 0): "zxy",
    (3, 1): "zyx",
    (4, 0): "zyx",
    (4, 1): "zyx",
    (5, 0): "yxz",
    (5, 1): "yxz",
}


def gather(blocks):
    return [
        lax.all_gather(lax.all_gather(block, "dp", axis=0, tiled=True), "section", axis=0)
        for block in blocks
    ]


def scatter(partials):
    results = []
    for pair in partials:
        both = lax.psum_scatter(jnp.stack(pair), "section", scatter_dimension=0, tiled=False)
        results.append(
            lax.psum_scatter(both.astype(F32), "dp", scatter_dimension=0, tiled=True)
        )
    return results


def norm_back(grad, unit, scale, gain):
    scaled = grad * gain
    inner = scaled - jnp.mean(scaled, axis=-1, keepdims=True)
    inner = inner - unit * jnp.mean(scaled * unit, axis=-1, keepdims=True)
    return jnp.sum(grad * unit, axis=0), jnp.sum(grad, axis=0), scale * inner


def by_head(rows):
    return rows.reshape(rows.shape[0], -1, HD)


def forward(hidden, weights, shared, allowed):
    query_key, value, out, up, down, first, norms = weights
    unit_one, scale_one = normalized(hidden)
    normed = (unit_one * norms[0] + norms[1]).astype(BF)
    qk = product(normed, query_key).astype(BF)
    fresh = product(normed, value).astype(BF)
    if shared is None:
        shared = product(normed, first).astype(BF)
    features = hidden.shape[1]
    queries, keys = by_head(qk[:, :features]), by_head(qk[:, features:])
    values = by_head(jnp.concatenate([fresh, shared], axis=1))
    scores = jnp.einsum("qhd,khd->hqk", queries, keys, preferred_element_type=F32) * HD**-0.5
    scores = jnp.where(allowed, scores, -1e30)
    raised = jnp.exp(scores - jnp.max(scores, axis=-1, keepdims=True))
    soft = raised / jnp.sum(raised, axis=-1, keepdims=True)
    probs = soft.astype(BF)
    attended = jnp.einsum("hqk,khd->qhd", probs, values, preferred_element_type=F32)
    attended = attended.reshape(hidden.shape).astype(BF)
    middle = hidden + product(attended, out)
    unit_two, scale_two = normalized(middle)
    mixed = (unit_two * norms[2] + norms[3]).astype(BF)
    upper = product(mixed, up)
    active = jax.nn.gelu(upper, approximate=True).astype(BF)
    output = middle + product(active, down)
    kept = (normed, queries, keys, values, soft, attended, unit_one, scale_one)
    return output, shared, kept + (unit_two, scale_two, mixed, upper, active)


def backward(grad, weights, kept, grad_shared_next):
    query_key, value, out, up, down, first, norms = weights
    normed, queries, keys, values, soft, attended, unit_one, scale_one = kept[:8]
    unit_two, scale_two, mixed, upper, active = kept[8:]
    positions, features = grad.shape
    half = value.shape[1]
    grad_low = grad.astype(BF)
    down_grad = transposed_times(active, grad_low)
    _, gelu_pull = jax.vjp(lambda u: jax.nn.gelu(u, approximate=True), upper)
    grad_upper = gelu_pull(times_transposed(grad_low, down))[0].astype(BF)
    up_grad = transposed_times(mixed, grad_upper)
    grad_mixed = times_transposed(grad_upper, up)
    two_gain, two_bias, through = norm_back(grad_mixed, unit_two, scale_two, norms[2])
    grad_middle = grad + through
    grad_attn = grad_middle.astype(BF)
    out_grad = transposed_times(attended, grad_attn)
    grad_attended = by_head(times_transposed(grad_attn, out).astype(BF))
    grad_soft = jnp.einsum("qhd,khd->hqk", grad_attended, values, preferred_element_type=F32)
    grad_values = jnp.einsum(
        "hqk,qhd->khd", soft.astype(BF), grad_attended, preferred_element_type=F32
    ).reshape(positions, features)
    grad_scores = soft * (grad_soft - jnp.sum(soft * grad_soft, axis=-1, keepdims=True))
    grad_scores = grad_scores.astype(BF)
    grad_queries = jnp.einsum("hqk,khd->qhd", grad_scores, keys, preferred_element_type=F32)
    grad_keys = jnp.einsum("hqk,qhd->khd", grad_scores, queries, preferred_element_type=F32)
    grad_qk = jnp.concatenate(
        [grad_queries.reshape(positions, features), grad_keys.reshape(positions, features)], axis=1
    )
    grad_qk = (grad_qk * HD**-0.5).astype(BF)
    grad_fresh = grad_values[:, :half].astype(BF)
    grad_shared = grad_values[:, half:]
    grad_normed = times_transposed(grad_qk, query_key) + times_transposed(grad_fresh, value)
    if grad_shared_next is not None:
        grad_shared = (grad_shared + grad_shared_next.astype(F32)).astype(BF)
        first_grad = transposed_times(normed, grad_shared)
        grad_normed = grad_normed + times_transposed(grad_shared, first)
    else:
        grad_shared = grad_shared.astype(BF)
        first_grad = None
    one_gain, one_bias, through = norm_back(grad_normed, unit_one, scale_one, norms[0])
    grad_input = (grad_middle + through).astype(BF)
    query_key_grad = transposed_times(normed, grad_qk)
    value_grad = transposed_times(normed, grad_fresh)
    gains = jnp.stack([one_gain, one_bias, two_gain, two_bias], axis=1)
    return grad_input, grad_shared, (
        query_key_grad, value_grad, out_grad, up_grad, down_grad, first_grad, gains
    )


def swapped(block):
    return lax.ppermute(block, "section", [(0, 1), (1, 0)])


def on_any_mesh(
    inputs,
    cotangent,
    lengths,
    norm_one_gain,
    norm_one_bias,
    query_key_weight,
    value_weight,
    out_weight,
    norm_two_gain,
    norm_two_bias,
    up_weight,
    down_weight,
    first_value_weight,
):
    section = lax.axis_index("section")
    first_half = section == 0
    half = value_weight.shape[2]
    features = out_weight.shape[2]
    quarter = first_value_weight.shape[1]
    own_rows = query_key_weight.shape[1]
    norms = jnp.stack([norm_one_gain[0], norm_one_bias[0], norm_two_gain[0], norm_two_bias[0]], axis=1)
    padding = -(half + features + quarter + 4) % 128
    attention = jnp.concatenate(
        [
            value_weight[0],
            out_weight[0],
            first_value_weight,
            norms,
            jnp.zeros((own_rows, padding), BF),
        ],
        axis=1,
    )
    whole = gather([query_key_weight[0], attention, up_weight[0], down_weight[0]])
    after = half + features
    first_matrix = jnp.concatenate(
        [whole[1][0, :, after : after + quarter], whole[1][1, :, after : after + quarter]], axis=1
    )

    def layer_weights(layer):
        packed = whole[1][layer]
        gains = packed[:, after + quarter : after + quarter + 4].astype(F32).T
        return (
            whole[0][layer],
            packed[:, :half],
            packed[:, half:after],
            whole[2][layer],
            whole[3][layer],
            first_matrix,
            gains,
        )

    weights = [layer_weights(0), layer_weights(1)]
    batch_sequences, positions = inputs.shape[1:3]
    hidden = lax.dynamic_index_in_dim(inputs, section, 0, keepdims=False)[0]
    grad = lax.dynamic_index_in_dim(cotangent, section, 0, keepdims=False)[0]
    length = lax.dynamic_index_in_dim(lengths, section, 0, keepdims=False)[0]
    places = jnp.arange(positions)
    live = places < length
    allowed = (places[None, :] <= places[:, None]) & live[None, :]
    output_one, shared, kept_one = forward(hidden.astype(F32), weights[0], None, allowed)
    low_one = output_one.astype(BF)
    output_two, _, kept_two = forward(low_one.astype(F32), weights[1], shared, allowed)
    low_two = output_two.astype(BF)
    outputs_there = swapped(jnp.where(first_half, low_two, low_one))
    outputs_here = jnp.where(first_half, low_one, low_two)
    grad = jnp.where(live[:, None], grad.astype(F32), 0.0)
    grad_one, grad_shared, sums_two = backward(grad, weights[1], kept_two, None)
    grad_zero, _, sums_one = backward(grad_one.astype(F32), weights[0], kept_one, grad_shared)
    grads_there = swapped(jnp.where(first_half, grad_one, grad_zero))
    grads_here = jnp.where(first_half, grad_zero, grad_one)
    first_grad = sums_one[5]

    def packed_sums(sums, first_part):
        return jnp.concatenate(
            [
                sums[1],
                sums[2],
                first_part,
                sums[6],
                jnp.zeros((first_part.shape[0], padding), F32),
            ],
            axis=1,
        ).astype(BF)

    partials = [
        (sums_one[0].astype(BF), sums_two[0].astype(BF)),
        (
            packed_sums(sums_one, first_grad[:, :quarter]),
            packed_sums(sums_two, first_grad[:, quarter:]),
        ),
        (sums_one[3].astype(BF), sums_two[3].astype(BF)),
        (sums_one[4].astype(BF), sums_two[4].astype(BF)),
    ]
    query_key_grad, packed_grad, up_grad, down_grad = scatter(partials)
    gains = packed_grad[:, after + quarter : after + quarter + 4].T

    def both(here, there):
        return jnp.stack(
            [jnp.where(first_half, here, there), jnp.where(first_half, there, here)]
        )[None, :, None]

    return (
        both(outputs_here, outputs_there),
        both(grads_here, grads_there),
        gains[0][None],
        gains[1][None],
        query_key_grad[None],
        packed_grad[:, :half][None],
        packed_grad[:, half:after][None],
        gains[2][None],
        gains[3][None],
        up_grad[None],
        down_grad[None],
        packed_grad[:, after : after + quarter],
    )


def on_device(
    tables,
    inputs,
    cotangent,
    lengths,
    norm_one_gain,
    norm_one_bias,
    query_key_weight,
    value_weight,
    out_weight,
    norm_two_gain,
    norm_two_bias,
    up_weight,
    down_weight,
    first_value_weight,
):
    gather_schedule, sum_schedule, steps, sum_orders = tables
    own = (query_key_weight, value_weight, out_weight, up_weight, down_weight)
    small = (first_value_weight, norm_one_gain, norm_one_bias, norm_two_gain, norm_two_bias)
    lengths = lengths.reshape(-1)
    done = forward_call(gather_schedule, own, small, inputs, lengths)
    weights, kept, turned, one_there = done[:4], done[4:10], done[10:14], done[14]
    back = backward_call(
        sum_schedule, steps, sum_orders, weights, kept, turned, inputs, cotangent, lengths
    )
    return last_call(back, kept[5], one_there)


def last_kernel(
    pack, query_key, up, down, grads, low, one_there, two_there, grad_there,
    out_low, out_grads, out_vector_0, out_vector_1, out_query_key, out_value, out_out,
    out_vector_2, out_vector_3, out_up, out_down, out_first,
    v_query_key, v_up, v_down, v_rows,
    in_sems, out_sems,
):
    s = lax.axis_index("section")
    copies = [
        (query_key, v_query_key, out_query_key.at[0]),
        (up, v_up, out_up.at[0]),
        (down, v_down, out_down.at[0]),
        (low.at[s], v_rows.at[0], out_low.at[0, s, 0]),
        (one_there, v_rows.at[1], out_low.at[0, 1 - s, 0]),
        (grads.at[s], v_rows.at[2], out_grads.at[0, s, 0]),
        (grad_there, v_rows.at[3], out_grads.at[0, 1 - s, 0]),
    ]
    reads = [
        pltpu.make_async_copy(source, held, in_sems.at[i])
        for i, (source, held, _) in enumerate(copies)
    ]
    writes = [
        pltpu.make_async_copy(held, target, out_sems.at[i])
        for i, (_, held, target) in enumerate(copies)
    ]
    for i, read in enumerate(reads):
        if i != 4:
            read.start()
    pl.when(s == 0)(reads[4].start)
    pl.when(s == 1)(pltpu.make_async_copy(two_there, v_rows.at[1], in_sems.at[4]).start)
    out_value[0] = pack[:, :HALF]
    out_out[0] = pack[:, HALF:FIRST]
    out_first[...] = pack[:, FIRST:NORMS]
    rows = pack[:, NORMS - 64 :].T
    for i, out in enumerate((out_vector_0, out_vector_1, out_vector_2, out_vector_3)):
        out[...] = rows[64 + i : 65 + i, :]
    for read, write in zip(reads, writes):
        read.wait()
        write.start()
    for write in writes:
        write.wait()


def last_call(back, low, one_there):
    query_key, pack, up, down, grads, two_there, grad_there = back
    anywhere = pl.BlockSpec(memory_space=pl.ANY)
    vmem = pl.BlockSpec(memory_space=pltpu.VMEM)
    vector = jax.ShapeDtypeStruct((1, 48), F32)
    rows = jax.ShapeDtypeStruct((1, 2, 1, LEN, FEATURES), BF)

    def block(*shape):
        return jax.ShapeDtypeStruct(shape, F32)

    return pl.pallas_call(
        last_kernel,
        out_shape=[
            rows, rows, vector, vector, block(1, 48, 2 * FEATURES), block(1, 48, HALF),
            block(1, 48, FEATURES), vector, vector, block(1, 48, HIDDEN),
            block(1, 192, FEATURES), block(48, 192),
        ],
        in_specs=[vmem] + [anywhere] * 8,
        out_specs=[
            anywhere, anywhere, vmem, vmem, anywhere, vmem, vmem, vmem, vmem, anywhere, anywhere,
            vmem,
        ],
        scratch_shapes=[
            pltpu.VMEM((48, 2 * FEATURES), F32),
            pltpu.VMEM((48, HIDDEN), F32),
            pltpu.VMEM((192, FEATURES), F32),
            pltpu.VMEM((4, LEN, FEATURES), BF),
            pltpu.SemaphoreType.DMA((7,)),
            pltpu.SemaphoreType.DMA((7,)),
        ],
    )(pack, query_key, up, down, grads, low, one_there, two_there, grad_there)


def solution(mesh):
    placed = (
        P(None, "dp", None, None),
        P(None, "dp", None, None),
        P(None, "dp"),
        P("section", "dp"),
        P("section", "dp"),
        P("section", "dp", None),
        P("section", "dp", None),
        P("section", "dp", None),
        P("section", "dp"),
        P("section", "dp"),
        P("section", "dp", None),
        P("section", "dp", None),
        P("dp", "section"),
    )
    if mesh.shape["dp"] == 16 and mesh.shape["section"] == 2:
        sums = [[[item[1:] for item in items] for items in k] for k in schedule_of(SUMS)]
        body = functools.partial(on_device, (schedule_of(GATHER), sums, STEPS, ORDERS))
    else:
        body = on_any_mesh
    return jax.shard_map(
        body,
        mesh=mesh,
        in_specs=placed,
        out_specs=(
            P("section", None, "dp", None, None),
            P("section", None, "dp", None, None),
            P("section", "dp"),
            P("section", "dp"),
            P("section", "dp", None),
            P("section", "dp", None),
            P("section", "dp", None),
            P("section", "dp"),
            P("section", "dp"),
            P("section", "dp", None),
            P("section", "dp", None),
            P("dp", "section"),
        ),
        check_vma=False,
    )
```

```python
import functools

import jax
import jax.numpy as jnp
from jax import lax
from jax.experimental import pallas as pl
from jax.experimental.pallas import tpu as pltpu
from jax.sharding import PartitionSpec as P

HEADS = 12
HD = 64
EPSILON = 1e-05
BF = jnp.bfloat16
F32 = jnp.float32
MESH = pl.DeviceIdType.MESH
LEN = 256
FEATURES = 768
HALF = 384
HIDDEN = 3072
PACK = 1408
FIRST = HALF + FEATURES
NORMS = FIRST + 192
LINKS = ("x", "y", "near", "far")


class Place:
    def __init__(self):
        self.s = lax.axis_index("section")
        dp = lax.axis_index("dp")
        self.z = dp // 4
        self.y = (dp // 2) % 2
        self.c = dp % 2
        self.mid = (self.z == 1) | (self.z == 2)

    def device(self, s, z, y, c):
        return (s, z * 4 + y * 2 + c)

    def neighbour(self, link):
        s, z, y, c = self.s, self.z, self.y, self.c
        if link == "x":
            return self.device(1 - s, z, y, c)
        if link == "y":
            return self.device(s, z, 1 - y, c)
        if link == "near":
            return self.device(s, z + 1 - 2 * (z % 2), y, c)
        if link == "far":
            return self.device(s, 3 - z, y, c)
        return self.device(s, z, y, 1 - c)

    def along_z(self, j):
        z = self.z
        return (z, z + 1 - 2 * (z % 2), 2 - z // 2, 3 - 3 * (z // 2))[j]

    def block(self, ry, j):
        y = self.y if ry == 0 else 1 - self.y
        return self.along_z(j) * 2 + y

    def is_class(self, k):
        middle = self.mid if k % 2 else jnp.logical_not(self.mid)
        return (self.s == k // 2) & middle


def greet(place):
    barrier = pltpu.get_barrier_semaphore()
    for link in ("x", "y", "near", "core"):
        pl.semaphore_signal(barrier, 1, device_id=place.neighbour(link), device_id_type=MESH)

    @pl.when(place.mid)
    def _():
        pl.semaphore_signal(barrier, 1, device_id=place.neighbour("far"), device_id_type=MESH)


def meet(place):
    barrier = pltpu.get_barrier_semaphore()

    @pl.when(place.mid)
    def _():
        pl.semaphore_wait(barrier, 5)

    @pl.when(jnp.logical_not(place.mid))
    def _():
        pl.semaphore_wait(barrier, 4)


def remote(source, target, send_sem, recv_sem, device):
    return pltpu.make_async_remote_copy(
        src_ref=source,
        dst_ref=target,
        send_sem=send_sem,
        recv_sem=recv_sem,
        device_id=device,
        device_id_type=MESH,
    )


def product(left, right):
    return jnp.dot(left, right, preferred_element_type=F32)


def times_transposed(left, right):
    return lax.dot_general(left, right, (((1,), (1,)), ((), ())), preferred_element_type=F32)


def transposed_times(left, right):
    return lax.dot_general(left, right, (((0,), (0,)), ((), ())), preferred_element_type=F32)


def normalized(rows):
    average = jnp.mean(rows, axis=-1, keepdims=True)
    centred = rows - average
    scale = lax.rsqrt(jnp.mean(centred * centred, axis=-1, keepdims=True) + EPSILON)
    return centred * scale, scale


def lane_index(shape):
    return lax.broadcasted_iota(jnp.int32, shape, 1)


def flat(block):
    return block.reshape(-1, block.shape[-1])


ARRAY_OF = (0, 1, 2, 2, 3, 3)
ROWS = (48, 48, 48, 192)
WIDTH = (2 * FEATURES, PACK, HIDDEN, FEATURES)


def piece_of(ref, g):
    lead = (slice(None),) * (len(ref.shape) - 2)
    if g in (2, 3):
        return ref.at[lead + (slice(None), pl.ds((g - 2) * (HIDDEN // 2), HIDDEN // 2))]
    if g in (4, 5):
        return ref.at[lead + (pl.ds((g - 4) * 96, 96), slice(None))]
    return ref


def forward_kernel(
    schedule,
    own_qk, own_value, own_out, own_up, own_down, first, vector_0, vector_1, vector_2, vector_3,
    inputs, lengths,
    out_qk, out_pack, out_up, out_down,
    kept_qk, kept_values, kept_probs, kept_slope, kept_middle, kept_low,
    turned_normed, turned_attended, turned_mixed, turned_active, swapped_one,
    w_qk, w_pack, w_up, w_down, own_pack, v_first, v_vectors, length,
    x_ref, normed, qk, values, probs, attended, middle, mixed, active, slope, low,
    t_normed, t_attended, t_mixed, t_active,
    recv_sem, send_sem, core_send, core_recv, local_sem, keep_sem, turn_send, turn_recv, fetch_sem, swap_sem,
):
    place = Place()
    s, c = place.s, place.c
    own = (own_qk.at[0], own_pack, own_up.at[0], own_down.at[0])
    whole = (w_qk, w_pack, w_up, w_down)
    whole_out = (out_qk, out_pack, out_up, out_down)

    greet(place)
    fetch = pltpu.make_async_copy(inputs.at[s, 0], x_ref, fetch_sem.at[0])
    fetch.start()
    packing = [
        pltpu.make_async_copy(own_value.at[0], own_pack.at[:, 0:HALF], fetch_sem.at[1]),
        pltpu.make_async_copy(own_out.at[0], own_pack.at[:, HALF:FIRST], fetch_sem.at[2]),
    ]
    small = [pltpu.make_async_copy(first, v_first, fetch_sem.at[3])]
    small += [
        pltpu.make_async_copy(vector, v_vectors.at[i], fetch_sem.at[4 + i])
        for i, vector in enumerate((vector_0, vector_1, vector_2, vector_3))
    ]
    small_length = pltpu.make_async_copy(lengths, length, fetch_sem.at[8])
    for one in packing + small + [small_length]:
        one.start()

    def pack_small():
        for one in small + packing:
            one.wait()
        tall = jnp.concatenate(
            [jnp.zeros((64, 48), F32)]
            + [v_vectors[i].astype(F32) for i in range(4)]
            + [jnp.zeros((60, 48), F32)],
            axis=0,
        )
        own_pack[:, FIRST : FIRST + 128] = v_first[:, :128]
        own_pack[:, FIRST + 128 :] = tall.T.astype(BF)
        own_pack[:, FIRST + 128 : NORMS] = v_first[:, 128:]
        mine[1].start()


    def spot(g, layer, ry, j):
        return piece_of(whole[ARRAY_OF[g]].at[layer, place.block(ry, j), c], g)

    mine = [
        pltpu.make_async_copy(
            piece_of(own[ARRAY_OF[g]], g), spot(g, s, 0, 0), local_sem.at[g]
        )
        for g in range(6)
    ]
    for g, one in enumerate(mine):
        if g != 1:
            one.start()
    meet(place)

    def weight_copy(k, item):
        link, g, layer, ry, j = item
        target = spot(g, layer, ry, j)
        source = target
        if (ry, j) == (0, 0) and layer == k // 2:
            source = piece_of(own[ARRAY_OF[g]], g)
        return remote(
            source,
            target,
            send_sem.at[LINKS.index(link), g, layer],
            recv_sem.at[g, layer, place.block(ry, j)],
            place.neighbour(link),
        )

    def hand_over(g, layer):
        part = piece_of(whole[ARRAY_OF[g]].at[layer, :, c], g)
        return remote(
            part, part, core_send.at[g, layer], core_recv.at[g, layer], place.neighbour("core")
        )

    def from_core(g, layer):
        part = piece_of(whole[ARRAY_OF[g]].at[layer, :, 1 - c], g)
        return remote(
            part, part, core_send.at[g, layer], core_recv.at[g, layer], place.neighbour("core")
        )

    packed = [False] * 4

    def run_items(k, items):
        for item in items:
            link, g, layer, ry, j = item
            if (g, layer, ry, j) == (1, k // 2, 0, 0) and not packed[k]:
                packed[k] = True
                pack_small()
            if link is not None:
                weight_copy(k, item).start()
                continue
            if (ry, j) == (0, 0) and layer == k // 2:
                mine[g].wait()
            else:
                remote(
                    spot(g, layer, ry, j),
                    spot(g, layer, ry, j),
                    send_sem.at[0, g, layer],
                    recv_sem.at[g, layer, place.block(ry, j)],
                    place.neighbour("x"),
                ).wait_recv()
            block = spot(g, layer, ry, j)
            remote(
                block,
                block,
                core_send.at[g, layer],
                core_recv.at[g, layer],
                place.neighbour("core"),
            ).start()

    swap = remote(low.at[0], swapped_one, swap_sem.at[0], swap_sem.at[1], place.neighbour("x"))
    kept = []

    def keep(source, target):
        copy = pltpu.make_async_copy(source, target, keep_sem.at[len(kept)])
        kept.append(copy)
        copy.start()

    turned = []

    def turn_over(number, layer, source, target):
        copy = pltpu.make_async_copy(source.at[:, c], target.at[layer, 0], keep_sem.at[len(kept)])
        kept.append(copy)
        copy.start()
        other = remote(
            source.at[:, 1 - c],
            target.at[layer, 1],
            turn_send.at[number, layer],
            turn_recv.at[number, layer],
            place.neighbour("core"),
        )
        other.start()
        turned.append(other)

    def norm_vectors(layer):
        window = flat(w_pack[layer, :, :, :, NORMS - 64 : NORMS + 64]).astype(F32)
        rows = window.T
        return [rows[64 + i : 65 + i, :] for i in range(4)]

    def residual(layer):
        return (x_ref if layer == 0 else low.at[0])[...].astype(F32)

    def front(layer):
        for g, l in ((0, 0), (1, 0), (1, 1)) if layer == 0 else ((0, 1),):
            from_core(g, l).wait_recv()
            keep(whole[g].at[l], whole_out[g].at[l])
        if layer == 0:
            fetch.wait()
            small_length.wait()
        vectors = norm_vectors(layer)
        unit, _ = normalized(residual(layer))
        rows = (unit * vectors[0] + vectors[1]).astype(BF)
        normed[...] = rows
        for i in range(3):
            at = slice(i * 512, (i + 1) * 512)
            qk[layer, :, at] = product(rows, flat(w_qk[layer, :, :, :, at])).astype(BF)
        keep(qk.at[layer], kept_qk.at[layer])

    def front_values(layer):
        rows = normed[...]
        values[layer, :, :HALF] = product(rows, flat(w_pack[layer, :, :, :, :HALF])).astype(BF)
        if layer == 0:
            window = slice(FIRST, FIRST + 256)
            part = [product(rows, flat(w_pack[l, :, :, :, window])) for l in range(2)]
            moved = pltpu.roll(part[1], 64, 1)
            between = jnp.where(lane_index((LEN, 128)) < 64, part[0][:, 128:], moved[:, :128])
            values[0, :, HALF : HALF + 128] = part[0][:, :128].astype(BF)
            values[0, :, HALF + 128 : HALF + 256] = between.astype(BF)
            values[0, :, HALF + 256 :] = moved[:, 128:].astype(BF)
        else:
            values[1, :, HALF:] = values[0, :, HALF:]
        keep(values.at[layer], kept_values.at[layer])
        t_normed[layer] = rows.T.reshape(8, 2, 48, LEN)
        turn_over(0, layer, t_normed.at[layer], turned_normed)

    def attend(layer, pairs):
        count = length[s]
        key = lax.broadcasted_iota(jnp.int32, (LEN, LEN), 0)
        query = lax.broadcasted_iota(jnp.int32, (LEN, LEN), 1)
        allowed = (key <= query) & (key < count)
        left = lane_index((LEN, 128)) < 64
        for pair in pairs:
            at = slice(pair * 128, (pair + 1) * 128)
            queries = qk[layer, :, at] * jnp.asarray(HD**-0.5, BF)
            keys = qk[layer, :, FEATURES + pair * 128 : FEATURES + (pair + 1) * 128]
            head_values = values[layer, :, at]
            parts = []
            for head in range(2):
                chosen = left if head == 0 else jnp.logical_not(left)
                scores = times_transposed(jnp.where(chosen, keys, jnp.zeros_like(keys)), queries)
                scores = jnp.where(allowed, scores, -1e30)
                raised = jnp.exp(scores - jnp.max(scores, axis=0, keepdims=True))
                soft = (raised / jnp.sum(raised, axis=0, keepdims=True)).astype(BF)
                probs[layer, 2 * pair + head] = soft
                parts.append(transposed_times(soft, head_values))
            attended[:, at] = jnp.where(left, parts[0], parts[1]).astype(BF)

    def project_out(layer):
        keep(probs.at[layer], kept_probs.at[layer])
        rows = attended[...]
        total = residual(layer) + product(
            rows, flat(w_pack[layer, :, :, :, HALF : HALF + FEATURES])
        )
        middle[layer] = total
        keep(middle.at[layer], kept_middle.at[layer])
        vectors = norm_vectors(layer)
        unit, _ = normalized(total)
        after = (unit * vectors[2] + vectors[3]).astype(BF)
        mixed[...] = after
        t_attended[layer] = rows.T.reshape(8, 2, 48, LEN)
        turn_over(1, layer, t_attended.at[layer], turned_attended)
        t_mixed[layer] = after.T.reshape(8, 2, 48, LEN)
        turn_over(2, layer, t_mixed.at[layer], turned_mixed)

    def widen(layer, i):
        if i % 2 == 0:
            from_core(2 + i // 2, layer).wait_recv()
        at = slice(i * 768, (i + 1) * 768)
        upper = product(mixed[...], flat(w_up[layer, :, :, :, at]))
        inner = upper * (0.7978845608028654 + 0.03567740813636141 * (upper * upper))
        bent = jnp.tanh(inner)
        half = 0.5 * (1.0 + bent)
        grown = (upper * half).astype(BF)
        active[:, at] = grown
        steep = 0.7978845608028654 + 0.10703222440908423 * (upper * upper)
        slope[layer, :, at] = (half + 0.5 * upper * (1.0 - bent * bent) * steep).astype(BF)
        t_active[layer, 2 * i : 2 * i + 2] = grown.T.reshape(2, 2, 192, LEN)

    def narrow(layer):
        keep(slope.at[layer], kept_slope.at[layer])
        turn_over(3, layer, t_active.at[layer], turned_active)
        keep(w_up.at[layer], out_up.at[layer])
        from_core(4, layer).wait_recv()
        from_core(5, layer).wait_recv()
        keep(w_down.at[layer], out_down.at[layer])
        total = middle[layer] + product(active[...], flat(w_down[layer]))
        low[layer] = total.astype(BF)
        keep(low.at[layer], kept_low.at[layer])
        if layer == 0:
            pl.when(s == 1)(swap.start)

    steps = []
    for layer in range(2):
        steps.append(functools.partial(front, layer))
        steps.append(functools.partial(front_values, layer))
        for i in range(6):
            steps.append(functools.partial(attend, layer, (i,)))
        steps.append(functools.partial(project_out, layer))
        for i in range(4):
            steps.append(functools.partial(widen, layer, i))
        steps.append(functools.partial(narrow, layer))

    for number in range(len(steps) + 1):
        for k in range(4):
            if schedule[k][number]:
                pl.when(place.is_class(k))(
                    functools.partial(run_items, k, schedule[k][number])
                )
        if number < len(steps):
            steps[number]()

    for k in range(4):

        def finish(k=k):
            sent = [item[:3] for items in schedule[k] for item in items if item[0] is not None]
            for link, g, layer in sorted(set(sent)):
                blocks = whole[ARRAY_OF[g]].at[layer, 0 : sent.count((link, g, layer)), 0]
                part = piece_of(blocks, g)
                sem = send_sem.at[LINKS.index(link), g, layer]
                remote(part, part, sem, recv_sem.at[g, layer, 0], place.neighbour("x")).wait_send()

        pl.when(place.is_class(k))(finish)
    for g in range(6):
        for layer in range(2):
            hand_over(g, layer).wait_send()
    for copy in kept:
        copy.wait()
    for copy in turned:
        copy.wait()
    pl.when(s == 0)(swap.wait_recv)
    pl.when(s == 1)(swap.wait_send)


def forward_call(schedule, own, small, inputs, length):
    def hbm(shape, dtype=BF):
        return jax.ShapeDtypeStruct(shape, dtype)

    def turn(rows):
        return (2, 2, 8, rows, LEN)

    weights = [(2, 8, 2, ROWS[a], WIDTH[a]) for a in range(4)]
    kept = [
        hbm((2, LEN, 2 * FEATURES)),
        hbm((2, LEN, FEATURES)),
        hbm((2, HEADS, LEN, LEN)),
        hbm((2, LEN, HIDDEN)),
        hbm((2, LEN, FEATURES), F32),
        hbm((2, LEN, FEATURES)),
    ]
    outs = [hbm(shape) for shape in weights] + kept
    outs += [hbm(turn(48)), hbm(turn(48)), hbm(turn(48)), hbm(turn(192)), hbm((LEN, FEATURES))]
    scratch = [pltpu.VMEM(shape, BF) for shape in weights]
    scratch += [
        pltpu.VMEM((48, PACK), BF),
        pltpu.VMEM((48, 192), BF),
        pltpu.VMEM((4, 1, 48), BF),
        pltpu.SMEM((2,), jnp.int32),
        pltpu.VMEM((LEN, FEATURES), BF),
        pltpu.VMEM((LEN, FEATURES), BF),
        pltpu.VMEM((2, LEN, 2 * FEATURES), BF),
        pltpu.VMEM((2, LEN, FEATURES), BF),
        pltpu.VMEM((2, HEADS, LEN, LEN), BF),
        pltpu.VMEM((LEN, FEATURES), BF),
        pltpu.VMEM((2, LEN, FEATURES), F32),
        pltpu.VMEM((LEN, FEATURES), BF),
        pltpu.VMEM((LEN, HIDDEN), BF),
        pltpu.VMEM((2, LEN, HIDDEN), BF),
        pltpu.VMEM((2, LEN, FEATURES), BF),
        pltpu.VMEM((2, 8, 2, 48, LEN), BF),
        pltpu.VMEM((2, 8, 2, 48, LEN), BF),
        pltpu.VMEM((2, 8, 2, 48, LEN), BF),
        pltpu.VMEM((2, 8, 2, 192, LEN), BF),
        pltpu.SemaphoreType.DMA((6, 2, 8)),
        pltpu.SemaphoreType.DMA((4, 6, 2)),
        pltpu.SemaphoreType.DMA((6, 2)),
        pltpu.SemaphoreType.DMA((6, 2)),
        pltpu.SemaphoreType.DMA((6,)),
        pltpu.SemaphoreType.DMA((28,)),
        pltpu.SemaphoreType.DMA((4, 2)),
        pltpu.SemaphoreType.DMA((4, 2)),
        pltpu.SemaphoreType.DMA((9,)),
        pltpu.SemaphoreType.DMA((2,)),
    ]
    anywhere = pl.BlockSpec(memory_space=pl.ANY)
    return pl.pallas_call(
        functools.partial(forward_kernel, schedule),
        out_shape=outs,
        in_specs=[anywhere] * 12,
        out_specs=[anywhere] * len(outs),
        scratch_shapes=scratch,
        compiler_params=pltpu.CompilerParams(
            collective_id=0, has_side_effects=True, vmem_limit_bytes=62 * 2**20
        ),
    )(*own, *small, inputs, length)


def schedule_of(codes):
    result = []
    for per_class in codes:
        result.append([])
        for numbers in per_class:
            items = []
            for n in numbers:
                link = None if n < 10000 else LINKS[n // 10000 - 1]
                items.append((link, n // 1000 % 10, n // 100 % 10, n // 10 % 10, n % 10))
            result[-1].append(items)
    return result


def branches(order, rx, ry, j):
    apart = {"x": rx != 0, "y": ry != 0, "z": j != 0}
    last = max([i for i, axis in enumerate(order) if apart[axis]], default=-1)
    links = []
    for i, axis in enumerate(order):
        if i < last:
            continue
        if axis != "z":
            if i > last:
                links.append((axis, False))
        elif i > last:
            links += [("near", False), ("far", True)]
        else:
            links.append(("far" if j == 1 else "near", True))
    return links


def slot_table(orders):
    table, counts = {}, []
    for g in range(6):
        number = 0
        for rx in range(2):
            for ry in range(2):
                for j in range(4):
                    links = []
                    for layer in range(2):
                        for link, _ in branches(orders[g, layer], rx, ry, j):
                            if link not in links:
                                links.append(link)
                    for link in links:
                        table[g, rx, ry, j, link] = number
                        number += 1
        counts.append(number)
    return table, counts


def towards_owner(order, k, rx, ry, j):
    apart = {"x": rx != 0, "y": ry != 0, "z": j != 0}
    axis = [axis for axis in order if apart[axis]][-1]
    if axis == "x":
        return "x", (0, ry, j)
    if axis == "y":
        return "y", (rx, 0, j)
    if j == 1:
        return "near", (rx, ry, 0)
    if k % 2:
        return "far", (rx, ry, 0 if j == 2 else 1)
    return "near", (rx, ry, j)


def backward_kernel(
    schedule, order_of_steps, orders, slots,
    w_qk, w_pack, w_up, w_down,
    kept_qk, kept_values, kept_probs, kept_slope, kept_middle, kept_low,
    turned_normed, turned_attended, turned_mixed, turned_active,
    inputs, cotangent, lengths,
    out_qk, out_pack, out_up, out_down, out_grads, swapped_low, swapped_grad,
    m_qk, m_pack, m_wide,
    qk, values, probs, slope, middle, entering, t_normed, t_attended, t_mixed, t_active,
    cot, length,
    dy, du, da, dqk, dv,
    far_dy, far_du, far_da, far_dqk, far_dv,
    total, d_mixed, d_attended, shared_two, grads, vectors, far_vectors, columns,
    h_qk, h_pack, h_up, h_down,
    arrived_0, arrived_1, arrived_2, arrived_3, arrived_4, arrived_5,
    r_qk, r_pack, r_up, r_down,
    load_sem, pair_send, pair_recv, credit, swap_send, swap_recv, sum_send, sum_recv, out_sem,
):
    place = Place()
    s, c = place.s, place.c
    held = (h_qk, h_pack, h_up, h_down)
    arrived = (arrived_0, arrived_1, arrived_2, arrived_3, arrived_4, arrived_5)
    result = (r_qk, r_pack, r_up, r_down)
    outs = (out_qk, out_pack, out_up, out_down)

    sources = {
        "qk_matrix": (m_qk, lambda l: w_qk.at[l]),
        "pack0": (m_pack.at[0], lambda l: w_pack.at[0]),
        "pack1": (m_pack.at[1], lambda l: w_pack.at[1]),
        "down0": (m_wide.at[0:16], lambda l: w_down.at[l, pl.ds(0, 16)]),
        "down1": (m_wide.at[16:32], lambda l: w_down.at[l, pl.ds(16, 16)]),
        "down2": (m_wide.at[32:48], lambda l: w_down.at[l, pl.ds(32, 16)]),
        "down3": (m_wide.at[48:64], lambda l: w_down.at[l, pl.ds(48, 16)]),
        "up0": (m_wide.at[0:16], lambda l: w_up.at[l, :, :, pl.ds(0, 768)]),
        "up1": (m_wide.at[16:32], lambda l: w_up.at[l, :, :, pl.ds(768, 768)]),
        "up2": (m_wide.at[32:48], lambda l: w_up.at[l, :, :, pl.ds(1536, 768)]),
        "up3": (m_wide.at[48:64], lambda l: w_up.at[l, :, :, pl.ds(2304, 768)]),
        "qk": (qk, lambda l: kept_qk.at[l]),
        "values": (values, lambda l: kept_values.at[l]),
        "probs": (probs, lambda l: kept_probs.at[l]),
        "slope": (slope, lambda l: kept_slope.at[l]),
        "middle": (middle, lambda l: kept_middle.at[l]),
        "entering": (entering, lambda l: inputs.at[s, 0] if l == 0 else kept_low.at[0]),
        "normed": (t_normed, lambda l: turned_normed.at[l]),
        "attended": (t_attended, lambda l: turned_attended.at[l]),
        "mixed": (t_mixed, lambda l: turned_mixed.at[l]),
        "active": (t_active, lambda l: turned_active.at[l]),
        "cotangent": (cot, lambda l: cotangent.at[s, 0]),
    }
    names = list(sources)

    def loading(name, layer):
        target, source = sources[name]
        return pltpu.make_async_copy(
            source(layer), target, load_sem.at[names.index(name)]
        )

    def load(*which, layer):
        for name in which:
            loading(name, layer).start()

    def loaded(*which, layer):
        for name in which:
            loading(name, layer).wait()

    fetch_length = pltpu.make_async_copy(lengths, length, out_sem.at[8])
    fetch_length.start()
    load("cotangent", "down0", "slope", "down1", "down2", "down3", layer=1)
    greet(place)

    across = place.neighbour("x")
    low_swap = remote(kept_low.at[1], swapped_low, swap_send.at[0], swap_recv.at[0], across)
    grad_swap = remote(grads.at[1 - s], swapped_grad, swap_send.at[1], swap_recv.at[1], across)

    shared = {
        "dy": (dy, far_dy),
        "du0": (du.at[:, 0:1536], far_du.at[:, 0:1536]),
        "du1": (du.at[:, 1536:3072], far_du.at[:, 1536:3072]),
        "da": (da, far_da),
        "dqk": (dqk, far_dqk),
        "dv": (dv, far_dv),
        "vectors": (vectors, far_vectors),
    }
    shared_names = list(shared)

    def exchange(name, layer):
        n = shared_names.index(name)
        return remote(
            *shared[name], pair_send.at[n], pair_recv.at[n], place.neighbour("core")
        )

    def hand(name, layer):
        if layer == 0:
            pl.semaphore_wait(credit.at[shared_names.index(name)], 1)
        exchange(name, layer).start()

    def done_with(name, layer):
        if layer == 1:
            pl.semaphore_signal(
                credit.at[shared_names.index(name)],
                1,
                device_id=place.neighbour("core"),
                device_id_type=MESH,
            )

    def free_to_write(name, layer):
        if layer == 0:
            exchange(name, 1).wait_send()

    def summed(left, right, far_right):
        return product(flat3(left[0]), right) + product(flat3(left[1]), far_right)

    def flat3(block):
        return block.reshape(-1, block.shape[-1])

    def norm_rows(layer):
        window = flat(m_pack[layer, :, :, :, NORMS - 64 : NORMS + 64]).astype(F32)
        rows = window.T
        return [rows[64 + i : 65 + i, :] for i in range(4)]

    def norm_back(grad, rows, gain):
        unit, scale = normalized(rows)
        scaled = grad * gain
        inner = scaled - jnp.mean(scaled, axis=-1, keepdims=True)
        inner = inner - unit * jnp.mean(scaled * unit, axis=-1, keepdims=True)
        return (
            jnp.sum(grad * unit, axis=0, keepdims=True),
            jnp.sum(grad, axis=0, keepdims=True),
            scale * inner,
        )

    def begin(layer):
        if layer == 1:
            vectors[...] = jnp.zeros_like(vectors)
            loaded("cotangent", layer=1)
            fetch_length.wait()
            position = lax.broadcasted_iota(jnp.int32, (LEN, FEATURES), 0)
            grad = jnp.where(position < length[s], cot[...].astype(F32), 0.0)
        else:
            grad = grads[1].astype(F32)
        free_to_write("dy", layer)
        total[...] = grad
        dy[...] = grad.astype(BF)
        if layer == 0:
            hand("dy", layer)

    def through_active(layer, i):
        if i == 0:
            loaded("slope", layer=layer)
            if layer == 1:
                load("active", "mixed", "middle", "pack1", "qk", "values", layer=1)
                load("probs", "attended", "entering", "qk_matrix", "normed", layer=1)
                load("pack0", layer=0)
        if i % 2 == 0:
            free_to_write("du%d" % (i // 2), layer)
        loaded("down%d" % i, layer=layer)
        at = slice(i * 768, (i + 1) * 768)
        grad = times_transposed(dy[...], flat3(m_wide[16 * i : 16 * i + 16]))
        du[:, at] = (grad * slope[:, at].astype(F32)).astype(BF)
        if i == 0 and layer == 1:
            meet(place)
            hand("dy", layer)
            pl.when(s == 0)(low_swap.start)
        if i % 2 == 1:
            hand("du%d" % (i // 2), layer)
        if i == 3:
            load("up0", "up1", "up2", "up3", layer=layer)
            if layer == 1:
                load("slope", layer=0)

    def sum_down(layer, half):
        if half == 0:
            loaded("active", layer=layer)
            exchange("dy", layer).wait_recv()
        rows = slice(half * 96, half * 96 + 96)
        sums = summed(t_active[:, :, rows, :], dy[...], far_dy[...])
        h_down[layer, :, rows, :] = sums.astype(BF).reshape(8, 96, FEATURES)
        if half == 1:
            done_with("dy", layer)
            if layer == 1:
                load("active", layer=0)

    def to_mixed(layer, q):
        loaded("up%d" % q, layer=layer)
        part = times_transposed(
            du[:, q * 768 : (q + 1) * 768], flat3(m_wide[16 * q : 16 * q + 16])
        )
        d_mixed[...] = part if q == 0 else d_mixed[...] + part
        if layer == 1 and q == 3:
            load("down0", "down1", "down2", "down3", layer=0)

    def sum_up(layer, q):
        if q == 0:
            loaded("mixed", layer=layer)
        if q % 2 == 0:
            exchange("du%d" % (q // 2), layer).wait_recv()
        at = slice(q * 768, (q + 1) * 768)
        sums = summed(t_mixed[...], du[:, at], far_du[:, at])
        h_up[layer, :, :, at] = sums.astype(BF).reshape(8, 48, 768)
        if q % 2 == 1:
            done_with("du%d" % (q // 2), layer)
        if q == 3 and layer == 1:
            load("mixed", layer=0)

    def second_norm(layer):
        loaded("middle", "pack%d" % layer, layer=layer)
        free_to_write("vectors", layer)
        free_to_write("da", layer)
        gain, bias, through = norm_back(d_mixed[...], middle[...], norm_rows(layer)[2])
        vectors[2:3, :] = gain
        vectors[3:4, :] = bias
        grad = total[...] + through
        total[...] = grad
        da[...] = grad.astype(BF)
        hand("da", layer)

    def to_attended(layer):
        matrix = flat(m_pack[layer, :, :, :, HALF:FIRST])
        d_attended[...] = times_transposed(da[...], matrix).astype(BF)
        if layer == 1:
            load("middle", layer=0)

    def through_attention(layer, pair):
        if pair == 0:
            loaded("qk", "values", "probs", layer=layer)
            free_to_write("dqk", layer)
            free_to_write("dv", layer)
        left = lane_index((LEN, 128)) < 64
        at = slice(pair * 128, (pair + 1) * 128)
        key_at = slice(FEATURES + pair * 128, FEATURES + (pair + 1) * 128)
        queries, keys, head_values = qk[:, at], qk[:, key_at], values[:, at]
        grad = d_attended[:, at]
        parts = []
        for head in range(2):
            chosen = left if head == 0 else jnp.logical_not(left)
            soft = probs[2 * pair + head]
            to_soft = times_transposed(
                jnp.where(chosen, head_values, jnp.zeros_like(head_values)), grad
            )
            exact = soft.astype(F32)
            inner = jnp.sum(exact * to_soft, axis=0, keepdims=True)
            to_scores = (exact * (to_soft - inner)).astype(BF)
            parts.append(
                (
                    transposed_times(to_scores, keys),
                    product(to_scores, queries),
                    product(soft, grad),
                )
            )
        of_queries, of_keys, of_values = [
            jnp.where(left, one, other) for one, other in zip(*parts)
        ]
        dqk[:, at] = (of_queries * HD**-0.5).astype(BF)
        dqk[:, key_at] = (of_keys * HD**-0.5).astype(BF)
        if pair < 3:
            dv[:, at] = of_values.astype(BF)
        else:
            there = slice((pair - 3) * 128, (pair - 2) * 128)
            if layer == 1:
                shared_two[:, there] = of_values.astype(BF)
            else:
                dv[:, at] = (of_values + shared_two[:, there].astype(F32)).astype(BF)
        if pair == 5:
            hand("dqk", layer)
            hand("dv", layer)
            if layer == 1:
                load("qk", "values", "probs", layer=0)

    def first_window(part):
        if part == 0:
            window = lambda ref: ref[:, HALF : HALF + 256]
        else:
            window = lambda ref: pltpu.roll(
                ref[:, HALF + 128 :].astype(F32), 192, 1
            ).astype(BF)
        inside = lane_index((LEN, 256)) < 192
        return [
            jnp.where(inside, window(ref), jnp.zeros((LEN, 256), BF)) for ref in (dv, far_dv)
        ]

    def to_normed(layer):
        loaded("qk_matrix", layer=layer)
        grad = times_transposed(dqk[...], flat(m_qk[...]))
        grad = grad + times_transposed(dv[:, :HALF], flat(m_pack[layer, :, :, :, :HALF]))
        if layer == 0:
            for part in range(2):
                grad = grad + times_transposed(
                    first_window(part)[0], flat(m_pack[part, :, :, :, FIRST : FIRST + 256])
                )
        d_mixed[...] = grad
        if layer == 1:
            load("qk_matrix", layer=0)

    def first_norm(layer):
        loaded("entering", layer=layer)
        rows = entering[...].astype(F32)
        gain, bias, through = norm_back(d_mixed[...], rows, norm_rows(layer)[0])
        vectors[0:1, :] = gain
        vectors[1:2, :] = bias
        hand("vectors", layer)
        grads[layer] = (total[...] + through).astype(BF)
        own_grads(layer).start()
        if layer == 1:
            load("entering", layer=0)
        pl.when(s == 1 - layer)(grad_swap.start)

    def sum_out(layer):
        loaded("attended", layer=layer)
        exchange("da", layer).wait_recv()
        sums = summed(t_attended[...], da[...], far_da[...])
        h_pack[layer, :, :, HALF:FIRST] = sums.astype(BF).reshape(8, 48, FEATURES)
        done_with("da", layer)
        if layer == 1:
            load("attended", layer=0)

    def sum_qk(layer):
        loaded("normed", layer=layer)
        exchange("dqk", layer).wait_recv()
        for q in range(2):
            at = slice(q * FEATURES, (q + 1) * FEATURES)
            sums = summed(t_normed[...], dqk[:, at], far_dqk[:, at])
            h_qk[layer, :, :, at] = sums.astype(BF).reshape(8, 48, FEATURES)
        done_with("dqk", layer)

    def sum_pack(layer):
        exchange("dv", layer).wait_recv()
        exchange("vectors", layer).wait_recv()
        sums = summed(t_normed[...], dv[:, :HALF], far_dv[:, :HALF])
        h_pack[layer, :, :, :HALF] = sums.astype(BF).reshape(8, 48, HALF)
        both = vectors[...] + far_vectors[...]
        nothing = jnp.zeros((64, FEATURES), F32)
        tall = jnp.concatenate([nothing, both, nothing[:56]], axis=0)
        columns[layer] = tall.T.astype(BF).reshape(8, 2, 48, 128)
        if layer == 0:
            for part in range(2):
                sums = summed(t_normed[...], *first_window(part)).reshape(8, 48, 256)
                h_pack[part, :, :, FIRST : FIRST + 128] = sums[:, :, :128].astype(BF)
                h_pack[part, :, :, FIRST + 128 :] = (
                    sums[:, :, 128:] + columns[part, :, c].astype(F32)
                ).astype(BF)
        done_with("dv", layer)
        done_with("vectors", layer)
        if layer == 1:
            load("normed", layer=0)

    def own_grads(layer):
        return pltpu.make_async_copy(grads.at[layer], out_grads.at[layer], out_sem.at[6 + layer])

    steps = []

    def step(action, *arguments):
        steps.append(functools.partial(action, *arguments))

    for layer in (1, 0):
        step(begin, layer)
        for i in range(4):
            step(through_active, layer, i)
        for half in range(2):
            step(sum_down, layer, half)
        for q in range(4):
            step(to_mixed, layer, q)
        for q in range(4):
            step(sum_up, layer, q)
        step(second_norm, layer)
        step(to_attended, layer)
        for pair in range(6):
            step(through_attention, layer, pair)
        step(sum_out, layer)
        step(to_normed, layer)
        step(first_norm, layer)
        step(sum_qk, layer)
        step(sum_pack, layer)

    steps = [steps[number] for number in order_of_steps]

    first_slot = [sum(ref.shape[0] for ref in arrived[:g]) for g in range(6)]

    def sum_copy(k, item):
        g, layer, ry, j = item
        rx = int(k // 2 != layer)
        link, there = towards_owner(orders[g, layer], k, rx, ry, j)
        return remote(
            piece_of(held[ARRAY_OF[g]].at[layer, place.block(ry, j)], g),
            arrived[g].at[slots[(g,) + there + (link,)]],
            sum_send.at[g, layer],
            sum_recv.at[first_slot[g] + slots[(g,) + there + (link,)]],
            place.neighbour(link),
        )

    def run_items(k, items):
        for item in items:
            g, layer, ry, j = item
            rx = int(k // 2 != layer)
            mine = piece_of(held[ARRAY_OF[g]].at[layer, place.block(ry, j)], g)
            terms = []
            for link, middle_only in branches(orders[g, layer], rx, ry, j):
                if middle_only and not k % 2:
                    continue
                slot = slots[g, rx, ry, j, link]
                remote(
                    mine,
                    arrived[g].at[slot],
                    sum_send.at[g, layer],
                    sum_recv.at[first_slot[g] + slot],
                    place.neighbour(link),
                ).wait_recv()
                terms.append(arrived[g].at[slot])
            final = (rx, ry, j) == (0, 0, 0)
            target = piece_of(result[ARRAY_OF[g]], g) if final else mine
            if terms or final:
                add_up(target, [mine] + terms)
            if not final:
                sum_copy(k, item).start()
                continue
            out = piece_of(outs[ARRAY_OF[g]], g)
            pltpu.make_async_copy(target, out, out_sem.at[g]).start()

    def add_up(target, terms):
        @pl.loop(0, target.shape[0] // 16)
        def _(i):
            at = pl.ds(pl.multiple_of(i * 16, 16), 16)
            sums = terms[0][at, :].astype(F32)
            for term in terms[1:]:
                sums = sums + term[at, :].astype(F32)
            target[at, :] = sums.astype(target.dtype)

    for number in range(len(steps) + 1):
        for k in range(4):
            if schedule[k][number]:
                pl.when(place.is_class(k))(
                    functools.partial(run_items, k, schedule[k][number])
                )
        if number < len(steps):
            steps[number]()

    for k in range(4):

        def finish(k=k):
            for g in range(6):
                for layer in range(2):
                    own = k // 2 == layer
                    if own:
                        pltpu.make_async_copy(
                            piece_of(result[ARRAY_OF[g]], g),
                            piece_of(outs[ARRAY_OF[g]], g),
                            out_sem.at[g],
                        ).wait()
                    part = piece_of(held[ARRAY_OF[g]].at[layer, 0 : 7 if own else 8], g)
                    remote(
                        part, part, sum_send.at[g, layer], sum_recv.at[0], place.neighbour("x")
                    ).wait_send()

        pl.when(place.is_class(k))(finish)
    for name in shared_names:
        exchange(name, 0).wait_send()
    pl.when(s == 0)(low_swap.wait_send)
    pl.when(s == 1)(low_swap.wait_recv)
    grad_swap.wait()
    for layer in range(2):
        own_grads(layer).wait()


def backward_call(schedule, order_of_steps, orders, weights, kept, turned, inputs, cotangent, lengths):
    slots, counts = slot_table(orders)
    blocks = [(48, 2 * FEATURES), (48, PACK), (48, HIDDEN), (192, FEATURES)]
    pieces = [(48, 1536), (48, PACK), (48, 1536), (48, 1536), (96, FEATURES), (96, FEATURES)]
    rows = (LEN, FEATURES)
    outs = [jax.ShapeDtypeStruct(block, F32) for block in blocks]
    outs += [jax.ShapeDtypeStruct((2,) + rows, BF)] + [jax.ShapeDtypeStruct(rows, BF)] * 2
    pair = [rows, (LEN, HIDDEN), rows, (LEN, 2 * FEATURES), rows]
    scratch = [
        pltpu.VMEM((8, 2, 48, 2 * FEATURES), BF),
        pltpu.VMEM((2, 8, 2, 48, PACK), BF),
        pltpu.VMEM((64, 48, FEATURES), BF),
        pltpu.VMEM((LEN, 2 * FEATURES), BF),
        pltpu.VMEM(rows, BF),
        pltpu.VMEM((HEADS, LEN, LEN), BF),
        pltpu.VMEM((LEN, HIDDEN), BF),
        pltpu.VMEM(rows, F32),
        pltpu.VMEM(rows, BF),
        pltpu.VMEM((2, 8, 48, LEN), BF),
        pltpu.VMEM((2, 8, 48, LEN), BF),
        pltpu.VMEM((2, 8, 48, LEN), BF),
        pltpu.VMEM((2, 8, 192, LEN), BF),
        pltpu.VMEM(rows, BF),
        pltpu.SMEM((2,), jnp.int32),
    ]
    scratch += [pltpu.VMEM(shape, BF) for shape in pair + pair]
    scratch += [
        pltpu.VMEM(rows, F32),
        pltpu.VMEM(rows, F32),
        pltpu.VMEM(rows, BF),
        pltpu.VMEM((LEN, HALF), BF),
        pltpu.VMEM((2,) + rows, BF),
        pltpu.VMEM((8, FEATURES), F32),
        pltpu.VMEM((8, FEATURES), F32),
        pltpu.VMEM((2, 8, 2, 48, 128), BF),
    ]
    scratch += [pltpu.VMEM((2, 8) + block, BF) for block in blocks]
    scratch += [pltpu.VMEM((count,) + piece, BF) for count, piece in zip(counts, pieces)]
    scratch += [pltpu.VMEM(block, F32) for block in blocks]
    scratch += [
        pltpu.SemaphoreType.DMA((22,)),
        pltpu.SemaphoreType.DMA((7,)),
        pltpu.SemaphoreType.DMA((7,)),
        pltpu.SemaphoreType.REGULAR((7,)),
        pltpu.SemaphoreType.DMA((2,)),
        pltpu.SemaphoreType.DMA((2,)),
        pltpu.SemaphoreType.DMA((6, 2)),
        pltpu.SemaphoreType.DMA((sum(counts),)),
        pltpu.SemaphoreType.DMA((9,)),
    ]
    anywhere = pl.BlockSpec(memory_space=pl.ANY)
    operands = [
        weights[0],
        weights[1],
        weights[2].reshape(2, 16, 48, HIDDEN),
        weights[3].reshape(2, 64, 48, FEATURES),
    ]
    operands += list(kept) + list(turned) + [inputs, cotangent]
    return pl.pallas_call(
        functools.partial(backward_kernel, schedule, order_of_steps, orders, slots),
        out_shape=outs,
        in_specs=[anywhere] * (len(operands) + 1),
        out_specs=[anywhere] * len(outs),
        scratch_shapes=scratch,
        compiler_params=pltpu.CompilerParams(
            collective_id=1, has_side_effects=True, vmem_limit_bytes=63 * 2**20
        ),
    )(*operands, lengths)


GATHER = (
    (
        (12000, 13000, 25000, 30000, 35000, 20000, 2001, 31000, 22000, 11000, 5010, 14000, 1100,
        10, 0, 1000, 2000, 3000, 4000, 5000, 35010, 10000, 32000, 24000, 10010, 1, 23000, 20001,
        2010, 15010, 4010, 12010, 32010, 21000, 3100, 2100, 1001, 11, 2, 15000, 5100, 20002,
        33000, 3001, 21100, 35100, 10002, 100, 34000, 10011, 5001, 3002, 10001, 22100, 5011, 12,
        21001, 1101, 25100, 10012, 14010, 2101, 3, 20003, 12001, 23002, 23100, 3101, 1010,
        10003, 2013, 2011, 23101, 15001, 12011, 5002, 1103, 21103, 13, 1003, 21101, 1102, 15002,
        21102, 5012, 4102, 10013, 21003, 34010, 1113, 2012, 1002, 12012, 3110, 1011, 1111, 3103,
        2002, 15012, 21002, 1110, 23001, 111, 22101, 5013, 2103, 1112, 3010, 12002, 12013, 3102,
        1013, 3003, 23003, 3111, 4103, 1012),
        (),
        (15011, 22103, 2003, 4100, 2102),
        (5110, 23103),
        (),
        (101, 4001, 3012, 12003, 4012, 5003, 102, 4011, 112, 2111, 103),
        (15013, 4101, 3011),
        (23102, 15003, 3013, 4111),
        (),
        (22102, 4003),
        (4013, 113, 110, 4002, 4110),
        (2113, 3113),
        (),
        (5102, 25102, 2110),
        (),
        (),
        (4113, 5101, 25101),
        (2112,),
        (),
        (5103, 25103),
        (),
        (),
        (3112, 5112),
        (),
        (),
        (5111, 5113, 4112),
        (),
        (),
        (),
    ),
    (
        (13000, 32000, 24000, 30000, 43000, 15000, 31000, 35000, 42000, 22000, 25000, 11000,
        14000, 40000, 0, 1000, 2000, 3000, 4000, 5000, 1, 40001, 2010, 5001, 12010, 21000, 4010,
        10001, 5010, 14010, 1001, 45000, 41001, 2, 3002, 30002, 20002, 21001, 3, 35010, 5011,
        20000, 41000, 5100, 33002, 20001, 2002, 23002, 1003, 10003, 33000, 15001, 31003, 45010,
        1011, 2011, 30003, 42010, 2100, 20003, 1100, 1002, 44000, 21003, 12011, 1102, 21002,
        21102, 21100, 31002, 1101, 42011, 3012, 2012, 45100, 12012, 2102, 34000, 15011, 44010,
        5101, 4001, 12, 45011, 25100, 5002, 35002, 3100, 13, 2013, 2001, 3001, 44001, 21101,
        43001, 100, 11, 32010, 15010, 10, 5012, 1103, 1013, 42001, 10010, 32013, 21103, 5102,
        12013, 32012, 1110, 34010, 4002, 10011, 5013, 10012, 4012, 15012, 25101, 10000, 101,
        35012, 3101, 3003, 15013, 45001, 1010, 3103, 23000, 23103, 1112, 1113, 1111, 5110, 1012,
        32002, 5003, 10013, 12002, 45101, 33003, 2003, 22100, 35013, 2103),
        (4011, 23001, 10002),
        (103, 12003, 32003, 5111, 22102, 2101, 3113, 4003, 3102),
        (34012, 5103, 34003, 23003, 44011, 35003, 102, 4013),
        (12001, 23102),
        (),
        (3010, 12000),
        (111, 22101, 23101, 4101),
        (34013, 15002, 4111, 3013, 3011, 4102, 23100, 15003, 22103),
        (25103, 110, 34002),
        (35102, 4112, 2110),
        (),
        (25102, 35100, 3112),
        (113, 112),
        (),
        (4100,),
        (2111, 35103),
        (),
        (4110,),
        (3111,),
        (2112, 2113),
        (),
        (3110,),
        (),
        (),
        (4113, 4103),
        (5112, 5113),
        (),
        (),
    ),
    (
        (11100, 20100, 31100, 21100, 34100, 32100, 22100, 13100, 10100, 12100, 23100, 2101,
        33100, 30100, 100, 1100, 2100, 3100, 4100, 5100, 15100, 14100, 4101, 24100, 1000, 24101,
        1101, 101, 22101, 31000, 3000, 33000, 12101, 11101, 3101, 20101, 23101, 10101, 2110,
        1102, 111, 13101, 110, 10110, 35100, 1001, 21001, 4000, 0, 25100, 34000, 21101, 2000,
        1103, 4102, 21102, 2010, 11103, 14102, 21000, 3103, 3102, 13102, 4103, 21103, 4111,
        10111, 11102, 2103, 24103, 23000, 10, 2102, 14101, 1010, 1003, 3110, 1112, 24102, 4010,
        13103, 1002, 1011, 21002, 102, 5110, 34010, 12, 12103, 21003, 103, 4113, 20103, 1110, 1,
        10102, 14111, 3001, 5000, 20102, 1113, 22103, 5010, 14103, 3003, 1012, 4110, 1013, 113,
        12102, 23001, 22102, 2111, 1111, 112, 10103, 3, 13, 2, 3002, 10112, 23002, 11, 10113,
        5101, 3010, 4112, 23003, 2001),
        (2012,),
        (4012,),
        (),
        (),
        (),
        (2002,),
        (2011, 2013),
        (14110, 23103),
        (14112, 4011, 5001, 14113, 3012, 4002, 23102, 5002, 2003, 3011, 5011, 3013, 4001, 2112,
        25101),
        (5012,),
        (),
        (4013, 4003, 5013, 3113, 2113, 5003),
        (),
        (5103, 25103),
        (),
        (3111,),
        (5111,),
        (3112, 5102, 25102),
        (),
        (),
        (),
        (),
        (5113,),
        (),
        (5112,),
        (),
        (),
        (),
    ),
    (
        (42100, 21100, 41100, 20100, 34100, 12100, 10100, 32100, 33100, 1101, 15100, 13100,
        41101, 23100, 100, 1100, 2100, 3100, 4100, 5100, 3000, 43100, 30100, 2102, 23000, 31100,
        1000, 4101, 44100, 1102, 40100, 21000, 41000, 11102, 110, 31102, 11101, 3101, 1103,
        12102, 31103, 21101, 43101, 101, 11100, 24100, 21102, 31000, 40101, 10101, 4102, 13101,
        44101, 34102, 3102, 1001, 41001, 20101, 24101, 23102, 11103, 2101, 3103, 32102, 14100,
        3001, 10110, 1002, 4000, 33103, 103, 33102, 4103, 21001, 3110, 42101, 21002, 102, 1003,
        4111, 34103, 13102, 2103, 2011, 32103, 31003, 31002, 43001, 13103, 44000, 30102, 21003,
        45100, 111, 4110, 30103, 21103, 1013, 12101, 5001, 5101, 3003, 10111, 22102, 1010,
        33000, 1112, 20103, 22101, 43000, 12103, 23001, 3002, 1011, 10103, 14101, 2010, 24102,
        10102, 23002, 2013, 1110, 14111, 23101, 5010, 23003, 4002, 14102, 5011, 4001, 1111,
        45101, 4010, 33002, 12, 33003, 44010, 3, 34000, 20102, 44001, 22103, 35100, 113, 5102,
        10, 4012, 4011, 34012, 13, 1012, 3111, 0, 4112, 4003, 34010, 24103, 14112, 1, 1113, 11,
        2, 3011, 3013, 10113, 44011, 2002, 112, 2012, 5103),
        (10112, 34002, 2003, 3012, 25101),
        (),
        (14110, 22100, 4013, 3010, 25102, 25103, 34013),
        (),
        (),
        (),
        (4113, 34003, 14113, 5000),
        (2000, 23103, 2001, 5012, 2113),
        (5013,),
        (2112, 25100, 5111, 35103),
        (2111,),
        (5002, 14103, 35102, 5003),
        (2110,),
        (5112,),
        (3112,),
        (),
        (),
        (),
        (),
        (5113,),
        (),
        (),
        (3113,),
        (),
        (5110,),
        (),
        (),
        (),
    ),
)

SUMS = (
    (
        (),
        (),
        (),
        (),
        (),
        (),
        (),
        (5102,),
        (),
        (2112, 4113),
        (),
        (),
        (5112,),
        (5111, 2111),
        (),
        (2110,),
        (),
        (),
        (),
        (5113,),
        (),
        (5101,),
        (),
        (),
        (3113, 2113),
        (),
        (),
        (),
        (4103, 110),
        (113,),
        (2101, 3111),
        (),
        (),
        (),
        (),
        (5103,),
        (),
        (112,),
        (),
        (5012, 5013, 3100),
        (),
        (),
        (2013,),
        (4111, 2012),
        (5003, 4012, 3012, 4110, 2011, 3013),
        (4101, 4112, 3102, 2103, 3103),
        (),
        (102, 2102),
        (),
        (),
        (5002,),
        (2003, 5001, 4013),
        (),
        (103,),
        (3010, 4003),
        (111, 12),
        (1013, 2002, 3112, 1113, 100, 5011, 3003, 1012, 13, 1003, 1112, 4102, 11, 1103, 4002,
        4100, 1011, 5100, 3, 4011, 5110, 2, 2001, 3101, 1, 3110, 101, 1111, 3011, 1010, 1102,
        3002, 1002, 4010, 1110, 10, 4001, 2010, 5010, 3000, 1101, 2100, 3001, 1001, 1100, 1000,
        0, 4000, 2000, 5000),
    ),
    (
        (),
        (),
        (),
        (),
        (),
        (),
        (),
        (),
        (),
        (2112, 4113),
        (),
        (2110,),
        (),
        (),
        (2111,),
        (),
        (3100,),
        (),
        (2113,),
        (),
        (),
        (3112,),
        (),
        (),
        (),
        (),
        (),
        (5112,),
        (),
        (110,),
        (112, 4111),
        (),
        (),
        (3110,),
        (),
        (113, 5102, 4112),
        (4100,),
        (111,),
        (),
        (4103,),
        (3103,),
        (2010,),
        (2012,),
        (3012, 3111, 5113, 5103),
        (3113, 3011),
        (4101,),
        (4013, 5110),
        (102, 4011, 5003, 100),
        (),
        (),
        (4110,),
        (3013,),
        (),
        (),
        (5111,),
        (),
        (1111, 5002, 2011, 2013, 5101, 1013, 5012, 1110, 4102, 4003, 2102, 1113, 1012, 103,
        5001, 5013, 2003, 2002, 13, 1103, 1112, 2103, 12, 3003, 11, 3, 1011, 1003, 4010, 4012,
        2101, 3101, 5010, 2100, 1101, 5011, 101, 3001, 4001, 5100, 3010, 2, 1102, 3002, 3102, 1,
        10, 1001, 1002, 2000, 1010, 4002, 2001, 1100, 0, 5000, 4000, 3000, 1000),
    ),
    (
        (),
        (),
        (),
        (),
        (),
        (),
        (),
        (5103,),
        (),
        (2112, 2113, 5112),
        (2111,),
        (5102,),
        (),
        (),
        (),
        (),
        (),
        (),
        (),
        (5101,),
        (),
        (5113,),
        (4113,),
        (),
        (),
        (),
        (),
        (),
        (113,),
        (),
        (2101, 2102),
        (111,),
        (),
        (4010,),
        (),
        (4013, 3113),
        (5011, 4012),
        (),
        (4003,),
        (),
        (),
        (5002, 2011, 4011),
        (),
        (),
        (5012, 2103),
        (2013,),
        (),
        (),
        (),
        (112,),
        (4002, 3013, 3011, 5013),
        (),
        (2001, 5003),
        (2003,),
        (),
        (12,),
        (4103, 1113, 1112, 3012, 3010, 3003, 1013, 4111, 2, 5001, 1103, 13, 1003, 1012, 1010,
        102, 11, 3, 2012, 1002, 3002, 4110, 1011, 3111, 5111, 103, 1, 3001, 3103, 5010, 2002,
        4001, 3000, 10, 4112, 4000, 3112, 1001, 1102, 5110, 4102, 2010, 1111, 3110, 101, 0,
        3102, 5000, 4100, 110, 4101, 3101, 1000, 2110, 2000, 5100, 1101, 3100, 1110, 2100, 100,
        1100),
    ),
    (
        (),
        (),
        (),
        (),
        (),
        (),
        (),
        (),
        (),
        (2112,),
        (),
        (2113, 2110),
        (),
        (),
        (),
        (),
        (2111,),
        (),
        (),
        (),
        (),
        (5112,),
        (),
        (),
        (),
        (),
        (),
        (),
        (112,),
        (),
        (),
        (110,),
        (4011,),
        (),
        (4001,),
        (),
        (113,),
        (5102,),
        (),
        (4113, 4000),
        (5103,),
        (),
        (),
        (),
        (),
        (4010,),
        (2011, 3010),
        (),
        (4013,),
        (),
        (3013, 4003),
        (),
        (),
        (),
        (2102,),
        (5113, 4002, 13),
        (3012, 1112, 5012, 4012, 2013, 1113, 3112, 5111, 5010, 5101, 10, 5013, 4112, 2010, 2103,
        3011, 1013, 5011, 3, 111, 3113, 2003, 4103, 2101, 5003, 12, 3003, 5002, 1011, 5001, 102,
        11, 3002, 1003, 1012, 4111, 2012, 2, 3001, 1001, 103, 5110, 3110, 3103, 3000, 2002,
        4101, 3111, 1, 2001, 5000, 1102, 1002, 1103, 1111, 1010, 2000, 3101, 4102, 0, 101, 4110,
        100, 2100, 5100, 3102, 1101, 1110, 1000, 4100, 3100, 1100),
    ),
)

STEPS = (
    0, 1, 2, 3, 5, 4, 6, 11, 12, 13, 7, 8, 9, 10, 14, 15, 16, 17, 18, 19, 20, 21, 22, 23, 24,
    25, 26, 28, 27, 29, 33, 30, 31, 32, 34, 35, 36, 37, 38, 39, 40, 41, 42, 43, 44, 45, 46, 47,
    48, 49, 50, 51, 52, 53, 54, 55,
)

ORDERS = {
    (0, 0): "zyx",
    (0, 1): "zxy",
    (1, 0): "xzy",
    (1, 1): "xzy",
    (2, 0): "xzy",
    (2, 1): "xzy",
    (3, 0): "zxy",
    (3, 1): "zyx",
    (4, 0): "zyx",
    (4, 1): "zyx",
    (5, 0): "yxz",
    (5, 1): "yxz",
}


def gather(blocks):
    return [
        lax.all_gather(lax.all_gather(block, "dp", axis=0, tiled=True), "section", axis=0)
        for block in blocks
    ]


def scatter(partials):
    results = []
    for pair in partials:
        both = lax.psum_scatter(jnp.stack(pair), "section", scatter_dimension=0, tiled=False)
        results.append(
            lax.psum_scatter(both.astype(F32), "dp", scatter_dimension=0, tiled=True)
        )
    return results


def norm_back(grad, unit, scale, gain):
    scaled = grad * gain
    inner = scaled - jnp.mean(scaled, axis=-1, keepdims=True)
    inner = inner - unit * jnp.mean(scaled * unit, axis=-1, keepdims=True)
    return jnp.sum(grad * unit, axis=0), jnp.sum(grad, axis=0), scale * inner


def by_head(rows):
    return rows.reshape(rows.shape[0], -1, HD)


def forward(hidden, weights, shared, allowed):
    query_key, value, out, up, down, first, norms = weights
    unit_one, scale_one = normalized(hidden)
    normed = (unit_one * norms[0] + norms[1]).astype(BF)
    qk = product(normed, query_key).astype(BF)
    fresh = product(normed, value).astype(BF)
    if shared is None:
        shared = product(normed, first).astype(BF)
    features = hidden.shape[1]
    queries, keys = by_head(qk[:, :features]), by_head(qk[:, features:])
    values = by_head(jnp.concatenate([fresh, shared], axis=1))
    scores = jnp.einsum("qhd,khd->hqk", queries, keys, preferred_element_type=F32) * HD**-0.5
    scores = jnp.where(allowed, scores, -1e30)
    raised = jnp.exp(scores - jnp.max(scores, axis=-1, keepdims=True))
    soft = raised / jnp.sum(raised, axis=-1, keepdims=True)
    probs = soft.astype(BF)
    attended = jnp.einsum("hqk,khd->qhd", probs, values, preferred_element_type=F32)
    attended = attended.reshape(hidden.shape).astype(BF)
    middle = hidden + product(attended, out)
    unit_two, scale_two = normalized(middle)
    mixed = (unit_two * norms[2] + norms[3]).astype(BF)
    upper = product(mixed, up)
    active = jax.nn.gelu(upper, approximate=True).astype(BF)
    output = middle + product(active, down)
    kept = (normed, queries, keys, values, soft, attended, unit_one, scale_one)
    return output, shared, kept + (unit_two, scale_two, mixed, upper, active)


def backward(grad, weights, kept, grad_shared_next):
    query_key, value, out, up, down, first, norms = weights
    normed, queries, keys, values, soft, attended, unit_one, scale_one = kept[:8]
    unit_two, scale_two, mixed, upper, active = kept[8:]
    positions, features = grad.shape
    half = value.shape[1]
    grad_low = grad.astype(BF)
    down_grad = transposed_times(active, grad_low)
    _, gelu_pull = jax.vjp(lambda u: jax.nn.gelu(u, approximate=True), upper)
    grad_upper = gelu_pull(times_transposed(grad_low, down))[0].astype(BF)
    up_grad = transposed_times(mixed, grad_upper)
    grad_mixed = times_transposed(grad_upper, up)
    two_gain, two_bias, through = norm_back(grad_mixed, unit_two, scale_two, norms[2])
    grad_middle = grad + through
    grad_attn = grad_middle.astype(BF)
    out_grad = transposed_times(attended, grad_attn)
    grad_attended = by_head(times_transposed(grad_attn, out).astype(BF))
    grad_soft = jnp.einsum("qhd,khd->hqk", grad_attended, values, preferred_element_type=F32)
    grad_values = jnp.einsum(
        "hqk,qhd->khd", soft.astype(BF), grad_attended, preferred_element_type=F32
    ).reshape(positions, features)
    grad_scores = soft * (grad_soft - jnp.sum(soft * grad_soft, axis=-1, keepdims=True))
    grad_scores = grad_scores.astype(BF)
    grad_queries = jnp.einsum("hqk,khd->qhd", grad_scores, keys, preferred_element_type=F32)
    grad_keys = jnp.einsum("hqk,qhd->khd", grad_scores, queries, preferred_element_type=F32)
    grad_qk = jnp.concatenate(
        [grad_queries.reshape(positions, features), grad_keys.reshape(positions, features)], axis=1
    )
    grad_qk = (grad_qk * HD**-0.5).astype(BF)
    grad_fresh = grad_values[:, :half].astype(BF)
    grad_shared = grad_values[:, half:]
    grad_normed = times_transposed(grad_qk, query_key) + times_transposed(grad_fresh, value)
    if grad_shared_next is not None:
        grad_shared = (grad_shared + grad_shared_next.astype(F32)).astype(BF)
        first_grad = transposed_times(normed, grad_shared)
        grad_normed = grad_normed + times_transposed(grad_shared, first)
    else:
        grad_shared = grad_shared.astype(BF)
        first_grad = None
    one_gain, one_bias, through = norm_back(grad_normed, unit_one, scale_one, norms[0])
    grad_input = (grad_middle + through).astype(BF)
    query_key_grad = transposed_times(normed, grad_qk)
    value_grad = transposed_times(normed, grad_fresh)
    gains = jnp.stack([one_gain, one_bias, two_gain, two_bias], axis=1)
    return grad_input, grad_shared, (
        query_key_grad, value_grad, out_grad, up_grad, down_grad, first_grad, gains
    )


def swapped(block):
    return lax.ppermute(block, "section", [(0, 1), (1, 0)])


def on_any_mesh(
    inputs,
    cotangent,
    lengths,
    norm_one_gain,
    norm_one_bias,
    query_key_weight,
    value_weight,
    out_weight,
    norm_two_gain,
    norm_two_bias,
    up_weight,
    down_weight,
    first_value_weight,
):
    section = lax.axis_index("section")
    first_half = section == 0
    half = value_weight.shape[2]
    features = out_weight.shape[2]
    quarter = first_value_weight.shape[1]
    own_rows = query_key_weight.shape[1]
    norms = jnp.stack([norm_one_gain[0], norm_one_bias[0], norm_two_gain[0], norm_two_bias[0]], axis=1)
    padding = -(half + features + quarter + 4) % 128
    attention = jnp.concatenate(
        [
            value_weight[0],
            out_weight[0],
            first_value_weight,
            norms,
            jnp.zeros((own_rows, padding), BF),
        ],
        axis=1,
    )
    whole = gather([query_key_weight[0], attention, up_weight[0], down_weight[0]])
    after = half + features
    first_matrix = jnp.concatenate(
        [whole[1][0, :, after : after + quarter], whole[1][1, :, after : after + quarter]], axis=1
    )

    def layer_weights(layer):
        packed = whole[1][layer]
        gains = packed[:, after + quarter : after + quarter + 4].astype(F32).T
        return (
            whole[0][layer],
            packed[:, :half],
            packed[:, half:after],
            whole[2][layer],
            whole[3][layer],
            first_matrix,
            gains,
        )

    weights = [layer_weights(0), layer_weights(1)]
    batch_sequences, positions = inputs.shape[1:3]
    hidden = lax.dynamic_index_in_dim(inputs, section, 0, keepdims=False)[0]
    grad = lax.dynamic_index_in_dim(cotangent, section, 0, keepdims=False)[0]
    length = lax.dynamic_index_in_dim(lengths, section, 0, keepdims=False)[0]
    places = jnp.arange(positions)
    live = places < length
    allowed = (places[None, :] <= places[:, None]) & live[None, :]
    output_one, shared, kept_one = forward(hidden.astype(F32), weights[0], None, allowed)
    low_one = output_one.astype(BF)
    output_two, _, kept_two = forward(low_one.astype(F32), weights[1], shared, allowed)
    low_two = output_two.astype(BF)
    outputs_there = swapped(jnp.where(first_half, low_two, low_one))
    outputs_here = jnp.where(first_half, low_one, low_two)
    grad = jnp.where(live[:, None], grad.astype(F32), 0.0)
    grad_one, grad_shared, sums_two = backward(grad, weights[1], kept_two, None)
    grad_zero, _, sums_one = backward(grad_one.astype(F32), weights[0], kept_one, grad_shared)
    grads_there = swapped(jnp.where(first_half, grad_one, grad_zero))
    grads_here = jnp.where(first_half, grad_zero, grad_one)
    first_grad = sums_one[5]

    def packed_sums(sums, first_part):
        return jnp.concatenate(
            [
                sums[1],
                sums[2],
                first_part,
                sums[6],
                jnp.zeros((first_part.shape[0], padding), F32),
            ],
            axis=1,
        ).astype(BF)

    partials = [
        (sums_one[0].astype(BF), sums_two[0].astype(BF)),
        (
            packed_sums(sums_one, first_grad[:, :quarter]),
            packed_sums(sums_two, first_grad[:, quarter:]),
        ),
        (sums_one[3].astype(BF), sums_two[3].astype(BF)),
        (sums_one[4].astype(BF), sums_two[4].astype(BF)),
    ]
    query_key_grad, packed_grad, up_grad, down_grad = scatter(partials)
    gains = packed_grad[:, after + quarter : after + quarter + 4].T

    def both(here, there):
        return jnp.stack(
            [jnp.where(first_half, here, there), jnp.where(first_half, there, here)]
        )[None, :, None]

    return (
        both(outputs_here, outputs_there),
        both(grads_here, grads_there),
        gains[0][None],
        gains[1][None],
        query_key_grad[None],
        packed_grad[:, :half][None],
        packed_grad[:, half:after][None],
        gains[2][None],
        gains[3][None],
        up_grad[None],
        down_grad[None],
        packed_grad[:, after : after + quarter],
    )


def on_device(
    tables,
    inputs,
    cotangent,
    lengths,
    norm_one_gain,
    norm_one_bias,
    query_key_weight,
    value_weight,
    out_weight,
    norm_two_gain,
    norm_two_bias,
    up_weight,
    down_weight,
    first_value_weight,
):
    gather_schedule, sum_schedule, steps, sum_orders = tables
    own = (query_key_weight, value_weight, out_weight, up_weight, down_weight)
    small = (first_value_weight, norm_one_gain, norm_one_bias, norm_two_gain, norm_two_bias)
    lengths = lengths.reshape(-1)
    done = forward_call(gather_schedule, own, small, inputs, lengths)
    weights, kept, turned, one_there = done[:4], done[4:10], done[10:14], done[14]
    back = backward_call(
        sum_schedule, steps, sum_orders, weights, kept, turned, inputs, cotangent, lengths
    )
    return last_call(back, kept[5], one_there)


def last_kernel(
    pack, query_key, up, down, grads, low, one_there, two_there, grad_there,
    out_low, out_grads, out_vector_0, out_vector_1, out_query_key, out_value, out_out,
    out_vector_2, out_vector_3, out_up, out_down, out_first,
    v_query_key, v_up, v_down, v_rows, v_pack, v_first, v_vectors,
    in_sems, out_sems,
):
    s = lax.axis_index("section")
    copies = [
        (query_key, v_query_key, out_query_key.at[0]),
        (up, v_up, out_up.at[0]),
        (down, v_down, out_down.at[0]),
        (low.at[s], v_rows.at[0], out_low.at[0, s, 0]),
        (one_there, v_rows.at[1], out_low.at[0, 1 - s, 0]),
        (grads.at[s], v_rows.at[2], out_grads.at[0, s, 0]),
        (grad_there, v_rows.at[3], out_grads.at[0, 1 - s, 0]),
    ]
    reads = [
        pltpu.make_async_copy(source, held, in_sems.at[i])
        for i, (source, held, _) in enumerate(copies)
    ]
    writes = [
        pltpu.make_async_copy(held, target, out_sems.at[i])
        for i, (_, held, target) in enumerate(copies)
    ]
    for i, read in enumerate(reads):
        if i != 4:
            read.start()
    pl.when(s == 0)(reads[4].start)
    pl.when(s == 1)(pltpu.make_async_copy(two_there, v_rows.at[1], in_sems.at[4]).start)
    read_pack = pltpu.make_async_copy(pack, v_pack, in_sems.at[7])
    read_pack.start()
    for read, write in zip(reads, writes):
        read.wait()
        write.start()
    read_pack.wait()
    v_first[...] = v_pack[:, FIRST:NORMS]
    rows = v_pack[:, NORMS - 64 :].T
    for i in range(4):
        v_vectors[i] = rows[64 + i : 65 + i, :]
    vectors = (out_vector_0, out_vector_1, out_vector_2, out_vector_3)
    rest = [
        (v_pack.at[:, 0:HALF], out_value.at[0]),
        (v_pack.at[:, HALF:FIRST], out_out.at[0]),
        (v_first, out_first),
    ] + [(v_vectors.at[i], vector) for i, vector in enumerate(vectors)]
    for i, (source, target) in enumerate(rest):
        writes.append(pltpu.make_async_copy(source, target, out_sems.at[7 + i]))
        writes[-1].start()
    for write in writes:
        write.wait()


def last_call(back, low, one_there):
    query_key, pack, up, down, grads, two_there, grad_there = back
    anywhere = pl.BlockSpec(memory_space=pl.ANY)
    vector = jax.ShapeDtypeStruct((1, 48), F32)
    rows = jax.ShapeDtypeStruct((1, 2, 1, LEN, FEATURES), BF)

    def block(*shape):
        return jax.ShapeDtypeStruct(shape, F32)

    return pl.pallas_call(
        last_kernel,
        out_shape=[
            rows, rows, vector, vector, block(1, 48, 2 * FEATURES), block(1, 48, HALF),
            block(1, 48, FEATURES), vector, vector, block(1, 48, HIDDEN),
            block(1, 192, FEATURES), block(48, 192),
        ],
        in_specs=[anywhere] * 9,
        out_specs=[anywhere] * 12,
        scratch_shapes=[
            pltpu.VMEM((48, 2 * FEATURES), F32),
            pltpu.VMEM((48, HIDDEN), F32),
            pltpu.VMEM((192, FEATURES), F32),
            pltpu.VMEM((4, LEN, FEATURES), BF),
            pltpu.VMEM((48, PACK), F32),
            pltpu.VMEM((48, 192), F32),
            pltpu.VMEM((4, 1, 48), F32),
            pltpu.SemaphoreType.DMA((8,)),
            pltpu.SemaphoreType.DMA((14,)),
        ],
    )(pack, query_key, up, down, grads, low, one_there, two_there, grad_there)


def solution(mesh):
    placed = (
        P(None, "dp", None, None),
        P(None, "dp", None, None),
        P(None, "dp"),
        P("section", "dp"),
        P("section", "dp"),
        P("section", "dp", None),
        P("section", "dp", None),
        P("section", "dp", None),
        P("section", "dp"),
        P("section", "dp"),
        P("section", "dp", None),
        P("section", "dp", None),
        P("dp", "section"),
    )
    if mesh.shape["dp"] == 16 and mesh.shape["section"] == 2:
        sums = [[[item[1:] for item in items] for items in k] for k in schedule_of(SUMS)]
        body = functools.partial(on_device, (schedule_of(GATHER), sums, STEPS, ORDERS))
    else:
        body = on_any_mesh
    return jax.shard_map(
        body,
        mesh=mesh,
        in_specs=placed,
        out_specs=(
            P("section", None, "dp", None, None),
            P("section", None, "dp", None, None),
            P("section", "dp"),
            P("section", "dp"),
            P("section", "dp", None),
            P("section", "dp", None),
            P("section", "dp", None),
            P("section", "dp"),
            P("section", "dp"),
            P("section", "dp", None),
            P("section", "dp", None),
            P("dp", "section"),
        ),
        check_vma=False,
    )
```

```python
import functools

import jax
import jax.numpy as jnp
from jax import lax
from jax.experimental import pallas as pl
from jax.experimental.pallas import tpu as pltpu
from jax.sharding import PartitionSpec as P

HEADS = 12
HD = 64
EPSILON = 1e-05
BF = jnp.bfloat16
F32 = jnp.float32
MESH = pl.DeviceIdType.MESH
LEN = 256
FEATURES = 768
HALF = 384
HIDDEN = 3072
PACK = 1408
FIRST = HALF + FEATURES
NORMS = FIRST + 192
LINKS = ("x", "y", "near", "far")


class Place:
    def __init__(self):
        self.s = lax.axis_index("section")
        dp = lax.axis_index("dp")
        self.z = dp // 4
        self.y = (dp // 2) % 2
        self.c = dp % 2
        self.mid = (self.z == 1) | (self.z == 2)

    def device(self, s, z, y, c):
        return (s, z * 4 + y * 2 + c)

    def neighbour(self, link):
        s, z, y, c = self.s, self.z, self.y, self.c
        if link == "x":
            return self.device(1 - s, z, y, c)
        if link == "y":
            return self.device(s, z, 1 - y, c)
        if link == "near":
            return self.device(s, z + 1 - 2 * (z % 2), y, c)
        if link == "far":
            return self.device(s, 3 - z, y, c)
        return self.device(s, z, y, 1 - c)

    def along_z(self, j):
        z = self.z
        return (z, z + 1 - 2 * (z % 2), 2 - z // 2, 3 - 3 * (z // 2))[j]

    def block(self, ry, j):
        y = self.y if ry == 0 else 1 - self.y
        return self.along_z(j) * 2 + y

    def is_class(self, k):
        middle = self.mid if k % 2 else jnp.logical_not(self.mid)
        return (self.s == k // 2) & middle


def greet(place):
    barrier = pltpu.get_barrier_semaphore()
    for link in ("x", "y", "near", "core"):
        pl.semaphore_signal(barrier, 1, device_id=place.neighbour(link), device_id_type=MESH)

    @pl.when(place.mid)
    def _():
        pl.semaphore_signal(barrier, 1, device_id=place.neighbour("far"), device_id_type=MESH)


def meet(place):
    barrier = pltpu.get_barrier_semaphore()

    @pl.when(place.mid)
    def _():
        pl.semaphore_wait(barrier, 5)

    @pl.when(jnp.logical_not(place.mid))
    def _():
        pl.semaphore_wait(barrier, 4)


def remote(source, target, send_sem, recv_sem, device):
    return pltpu.make_async_remote_copy(
        src_ref=source,
        dst_ref=target,
        send_sem=send_sem,
        recv_sem=recv_sem,
        device_id=device,
        device_id_type=MESH,
    )


def product(left, right):
    return jnp.dot(left, right, preferred_element_type=F32)


def times_transposed(left, right):
    return lax.dot_general(left, right, (((1,), (1,)), ((), ())), preferred_element_type=F32)


def transposed_times(left, right):
    return lax.dot_general(left, right, (((0,), (0,)), ((), ())), preferred_element_type=F32)


def normalized(rows):
    average = jnp.mean(rows, axis=-1, keepdims=True)
    centred = rows - average
    scale = lax.rsqrt(jnp.mean(centred * centred, axis=-1, keepdims=True) + EPSILON)
    return centred * scale, scale


def lane_index(shape):
    return lax.broadcasted_iota(jnp.int32, shape, 1)


def flat(block):
    return block.reshape(-1, block.shape[-1])


ARRAY_OF = (0, 1, 2, 2, 3, 3)
ROWS = (48, 48, 48, 192)
WIDTH = (2 * FEATURES, PACK, HIDDEN, FEATURES)


def piece_of(ref, g):
    lead = (slice(None),) * (len(ref.shape) - 2)
    if g in (2, 3):
        return ref.at[lead + (slice(None), pl.ds((g - 2) * (HIDDEN // 2), HIDDEN // 2))]
    if g in (4, 5):
        return ref.at[lead + (pl.ds((g - 4) * 96, 96), slice(None))]
    return ref


def forward_kernel(
    schedule,
    own_qk, own_value, own_out, own_up, own_down, first, vector_0, vector_1, vector_2, vector_3,
    inputs, lengths,
    out_qk, out_pack, out_up, out_down,
    kept_qk, kept_values, kept_probs, kept_slope, kept_middle, kept_low,
    turned_normed, turned_attended, turned_mixed, turned_active, swapped_one,
    w_qk, w_pack, w_up, w_down, own_pack, v_first, v_vectors, length,
    x_ref, normed, qk, values, probs, attended, middle, mixed, active, slope, low,
    t_normed, t_attended, t_mixed, t_active,
    recv_sem, send_sem, core_send, core_recv, local_sem, keep_sem, turn_send, turn_recv, fetch_sem, swap_sem,
):
    place = Place()
    s, c = place.s, place.c
    own = (own_qk.at[0], own_pack, own_up.at[0], own_down.at[0])
    whole = (w_qk, w_pack, w_up, w_down)
    whole_out = (out_qk, out_pack, out_up, out_down)

    greet(place)
    fetch = pltpu.make_async_copy(inputs.at[s, 0], x_ref, fetch_sem.at[0])
    fetch.start()
    packing = [
        pltpu.make_async_copy(own_value.at[0], own_pack.at[:, 0:HALF], fetch_sem.at[1]),
        pltpu.make_async_copy(own_out.at[0], own_pack.at[:, HALF:FIRST], fetch_sem.at[2]),
    ]
    small = [pltpu.make_async_copy(first, v_first, fetch_sem.at[3])]
    small += [
        pltpu.make_async_copy(vector, v_vectors.at[i], fetch_sem.at[4 + i])
        for i, vector in enumerate((vector_0, vector_1, vector_2, vector_3))
    ]
    small_length = pltpu.make_async_copy(lengths, length, fetch_sem.at[8])
    for one in packing + small + [small_length]:
        one.start()

    def pack_small():
        for one in small + packing:
            one.wait()
        tall = jnp.concatenate(
            [jnp.zeros((64, 48), F32)]
            + [v_vectors[i].astype(F32) for i in range(4)]
            + [jnp.zeros((60, 48), F32)],
            axis=0,
        )
        own_pack[:, FIRST : FIRST + 128] = v_first[:, :128]
        own_pack[:, FIRST + 128 :] = tall.T.astype(BF)
        own_pack[:, FIRST + 128 : NORMS] = v_first[:, 128:]
        mine[1].start()


    def spot(g, layer, ry, j):
        return piece_of(whole[ARRAY_OF[g]].at[layer, place.block(ry, j), c], g)

    mine = [
        pltpu.make_async_copy(
            piece_of(own[ARRAY_OF[g]], g), spot(g, s, 0, 0), local_sem.at[g]
        )
        for g in range(6)
    ]
    for g, one in enumerate(mine):
        if g != 1:
            one.start()
    meet(place)

    def weight_copy(k, item):
        link, g, layer, ry, j = item
        target = spot(g, layer, ry, j)
        source = target
        if (ry, j) == (0, 0) and layer == k // 2:
            source = piece_of(own[ARRAY_OF[g]], g)
        return remote(
            source,
            target,
            send_sem.at[LINKS.index(link), g, layer],
            recv_sem.at[g, layer, place.block(ry, j)],
            place.neighbour(link),
        )

    def hand_over(g, layer):
        part = piece_of(whole[ARRAY_OF[g]].at[layer, :, c], g)
        return remote(
            part, part, core_send.at[g, layer], core_recv.at[g, layer], place.neighbour("core")
        )

    def from_core(g, layer):
        part = piece_of(whole[ARRAY_OF[g]].at[layer, :, 1 - c], g)
        return remote(
            part, part, core_send.at[g, layer], core_recv.at[g, layer], place.neighbour("core")
        )

    packed = [False] * 4

    def run_items(k, items):
        for item in items:
            link, g, layer, ry, j = item
            if (g, layer, ry, j) == (1, k // 2, 0, 0) and not packed[k]:
                packed[k] = True
                pack_small()
            if link is not None:
                weight_copy(k, item).start()
                continue
            if (ry, j) == (0, 0) and layer == k // 2:
                mine[g].wait()
            else:
                remote(
                    spot(g, layer, ry, j),
                    spot(g, layer, ry, j),
                    send_sem.at[0, g, layer],
                    recv_sem.at[g, layer, place.block(ry, j)],
                    place.neighbour("x"),
                ).wait_recv()
            block = spot(g, layer, ry, j)
            remote(
                block,
                block,
                core_send.at[g, layer],
                core_recv.at[g, layer],
                place.neighbour("core"),
            ).start()

    swap = remote(low.at[0], swapped_one, swap_sem.at[0], swap_sem.at[1], place.neighbour("x"))
    kept = []

    def keep(source, target):
        copy = pltpu.make_async_copy(source, target, keep_sem.at[len(kept)])
        kept.append(copy)
        copy.start()

    turned = []

    def turn_over(number, layer, source, target):
        copy = pltpu.make_async_copy(source.at[:, c], target.at[layer, 0], keep_sem.at[len(kept)])
        kept.append(copy)
        copy.start()
        other = remote(
            source.at[:, 1 - c],
            target.at[layer, 1],
            turn_send.at[number, layer],
            turn_recv.at[number, layer],
            place.neighbour("core"),
        )
        other.start()
        turned.append(other)

    def norm_vectors(layer):
        window = flat(w_pack[layer, :, :, :, NORMS - 64 : NORMS + 64]).astype(F32)
        rows = window.T
        return [rows[64 + i : 65 + i, :] for i in range(4)]

    def residual(layer):
        return (x_ref if layer == 0 else low.at[0])[...].astype(F32)

    def front(layer):
        for g, l in ((0, 0), (1, 0), (1, 1)) if layer == 0 else ((0, 1),):
            from_core(g, l).wait_recv()
            keep(whole[g].at[l], whole_out[g].at[l])
        if layer == 0:
            fetch.wait()
            small_length.wait()
        vectors = norm_vectors(layer)
        unit, _ = normalized(residual(layer))
        rows = (unit * vectors[0] + vectors[1]).astype(BF)
        normed[...] = rows
        for i in range(3):
            at = slice(i * 512, (i + 1) * 512)
            qk[layer, :, at] = product(rows, flat(w_qk[layer, :, :, :, at])).astype(BF)
        keep(qk.at[layer], kept_qk.at[layer])

    def front_values(layer):
        rows = normed[...]
        values[layer, :, :HALF] = product(rows, flat(w_pack[layer, :, :, :, :HALF])).astype(BF)
        if layer == 0:
            window = slice(FIRST, FIRST + 256)
            part = [product(rows, flat(w_pack[l, :, :, :, window])) for l in range(2)]
            moved = pltpu.roll(part[1], 64, 1)
            between = jnp.where(lane_index((LEN, 128)) < 64, part[0][:, 128:], moved[:, :128])
            values[0, :, HALF : HALF + 128] = part[0][:, :128].astype(BF)
            values[0, :, HALF + 128 : HALF + 256] = between.astype(BF)
            values[0, :, HALF + 256 :] = moved[:, 128:].astype(BF)
        else:
            values[1, :, HALF:] = values[0, :, HALF:]
        keep(values.at[layer], kept_values.at[layer])
        t_normed[layer] = rows.T.reshape(8, 2, 48, LEN)
        turn_over(0, layer, t_normed.at[layer], turned_normed)

    def attend(layer, pairs):
        count = length[s]
        key = lax.broadcasted_iota(jnp.int32, (LEN, LEN), 0)
        query = lax.broadcasted_iota(jnp.int32, (LEN, LEN), 1)
        allowed = (key <= query) & (key < count)
        left = lane_index((LEN, 128)) < 64
        for pair in pairs:
            at = slice(pair * 128, (pair + 1) * 128)
            queries = qk[layer, :, at] * jnp.asarray(HD**-0.5, BF)
            keys = qk[layer, :, FEATURES + pair * 128 : FEATURES + (pair + 1) * 128]
            head_values = values[layer, :, at]
            parts = []
            for head in range(2):
                chosen = left if head == 0 else jnp.logical_not(left)
                scores = times_transposed(jnp.where(chosen, keys, jnp.zeros_like(keys)), queries)
                scores = jnp.where(allowed, scores, -1e30)
                raised = jnp.exp(scores - jnp.max(scores, axis=0, keepdims=True))
                soft = (raised / jnp.sum(raised, axis=0, keepdims=True)).astype(BF)
                probs[layer, 2 * pair + head] = soft
                parts.append(transposed_times(soft, head_values))
            attended[:, at] = jnp.where(left, parts[0], parts[1]).astype(BF)

    def project_out(layer):
        keep(probs.at[layer], kept_probs.at[layer])
        rows = attended[...]
        total = residual(layer) + product(
            rows, flat(w_pack[layer, :, :, :, HALF : HALF + FEATURES])
        )
        middle[layer] = total
        keep(middle.at[layer], kept_middle.at[layer])
        vectors = norm_vectors(layer)
        unit, _ = normalized(total)
        after = (unit * vectors[2] + vectors[3]).astype(BF)
        mixed[...] = after
        t_attended[layer] = rows.T.reshape(8, 2, 48, LEN)
        turn_over(1, layer, t_attended.at[layer], turned_attended)
        t_mixed[layer] = after.T.reshape(8, 2, 48, LEN)
        turn_over(2, layer, t_mixed.at[layer], turned_mixed)

    def widen(layer, i):
        if i % 2 == 0:
            from_core(2 + i // 2, layer).wait_recv()
        at = slice(i * 768, (i + 1) * 768)
        upper = product(mixed[...], flat(w_up[layer, :, :, :, at]))
        inner = upper * (0.7978845608028654 + 0.03567740813636141 * (upper * upper))
        bent = jnp.tanh(inner)
        half = 0.5 * (1.0 + bent)
        grown = (upper * half).astype(BF)
        active[:, at] = grown
        steep = 0.7978845608028654 + 0.10703222440908423 * (upper * upper)
        slope[layer, :, at] = (half + 0.5 * upper * (1.0 - bent * bent) * steep).astype(BF)
        t_active[layer, 2 * i : 2 * i + 2] = grown.T.reshape(2, 2, 192, LEN)

    def narrow(layer):
        keep(slope.at[layer], kept_slope.at[layer])
        turn_over(3, layer, t_active.at[layer], turned_active)
        keep(w_up.at[layer], out_up.at[layer])
        from_core(4, layer).wait_recv()
        from_core(5, layer).wait_recv()
        keep(w_down.at[layer], out_down.at[layer])
        total = middle[layer] + product(active[...], flat(w_down[layer]))
        low[layer] = total.astype(BF)
        keep(low.at[layer], kept_low.at[layer])
        if layer == 0:
            pl.when(s == 1)(swap.start)

    steps = []
    for layer in range(2):
        steps.append(functools.partial(front, layer))
        steps.append(functools.partial(front_values, layer))
        for i in range(6):
            steps.append(functools.partial(attend, layer, (i,)))
        steps.append(functools.partial(project_out, layer))
        for i in range(4):
            steps.append(functools.partial(widen, layer, i))
        steps.append(functools.partial(narrow, layer))

    for number in range(len(steps) + 1):
        for k in range(4):
            if schedule[k][number]:
                pl.when(place.is_class(k))(
                    functools.partial(run_items, k, schedule[k][number])
                )
        if number < len(steps):
            steps[number]()

    for k in range(4):

        def finish(k=k):
            sent = [item[:3] for items in schedule[k] for item in items if item[0] is not None]
            for link, g, layer in sorted(set(sent)):
                blocks = whole[ARRAY_OF[g]].at[layer, 0 : sent.count((link, g, layer)), 0]
                part = piece_of(blocks, g)
                sem = send_sem.at[LINKS.index(link), g, layer]
                remote(part, part, sem, recv_sem.at[g, layer, 0], place.neighbour("x")).wait_send()

        pl.when(place.is_class(k))(finish)
    for g in range(6):
        for layer in range(2):
            hand_over(g, layer).wait_send()
    for copy in kept:
        copy.wait()
    for copy in turned:
        copy.wait()
    pl.when(s == 0)(swap.wait_recv)
    pl.when(s == 1)(swap.wait_send)


def forward_call(schedule, own, small, inputs, length):
    def hbm(shape, dtype=BF):
        return jax.ShapeDtypeStruct(shape, dtype)

    def turn(rows):
        return (2, 2, 8, rows, LEN)

    weights = [(2, 8, 2, ROWS[a], WIDTH[a]) for a in range(4)]
    kept = [
        hbm((2, LEN, 2 * FEATURES)),
        hbm((2, LEN, FEATURES)),
        hbm((2, HEADS, LEN, LEN)),
        hbm((2, LEN, HIDDEN)),
        hbm((2, LEN, FEATURES), F32),
        hbm((2, LEN, FEATURES)),
    ]
    outs = [hbm(shape) for shape in weights] + kept
    outs += [hbm(turn(48)), hbm(turn(48)), hbm(turn(48)), hbm(turn(192)), hbm((LEN, FEATURES))]
    scratch = [pltpu.VMEM(shape, BF) for shape in weights]
    scratch += [
        pltpu.VMEM((48, PACK), BF),
        pltpu.VMEM((48, 192), BF),
        pltpu.VMEM((4, 1, 48), BF),
        pltpu.SMEM((2,), jnp.int32),
        pltpu.VMEM((LEN, FEATURES), BF),
        pltpu.VMEM((LEN, FEATURES), BF),
        pltpu.VMEM((2, LEN, 2 * FEATURES), BF),
        pltpu.VMEM((2, LEN, FEATURES), BF),
        pltpu.VMEM((2, HEADS, LEN, LEN), BF),
        pltpu.VMEM((LEN, FEATURES), BF),
        pltpu.VMEM((2, LEN, FEATURES), F32),
        pltpu.VMEM((LEN, FEATURES), BF),
        pltpu.VMEM((LEN, HIDDEN), BF),
        pltpu.VMEM((2, LEN, HIDDEN), BF),
        pltpu.VMEM((2, LEN, FEATURES), BF),
        pltpu.VMEM((2, 8, 2, 48, LEN), BF),
        pltpu.VMEM((2, 8, 2, 48, LEN), BF),
        pltpu.VMEM((2, 8, 2, 48, LEN), BF),
        pltpu.VMEM((2, 8, 2, 192, LEN), BF),
        pltpu.SemaphoreType.DMA((6, 2, 8)),
        pltpu.SemaphoreType.DMA((4, 6, 2)),
        pltpu.SemaphoreType.DMA((6, 2)),
        pltpu.SemaphoreType.DMA((6, 2)),
        pltpu.SemaphoreType.DMA((6,)),
        pltpu.SemaphoreType.DMA((28,)),
        pltpu.SemaphoreType.DMA((4, 2)),
        pltpu.SemaphoreType.DMA((4, 2)),
        pltpu.SemaphoreType.DMA((9,)),
        pltpu.SemaphoreType.DMA((2,)),
    ]
    anywhere = pl.BlockSpec(memory_space=pl.ANY)
    return pl.pallas_call(
        functools.partial(forward_kernel, schedule),
        out_shape=outs,
        in_specs=[anywhere] * 12,
        out_specs=[anywhere] * len(outs),
        scratch_shapes=scratch,
        compiler_params=pltpu.CompilerParams(
            collective_id=0, has_side_effects=True, vmem_limit_bytes=62 * 2**20
        ),
    )(*own, *small, inputs, length)


def schedule_of(codes):
    result = []
    for per_class in codes:
        result.append([])
        for numbers in per_class:
            items = []
            for n in numbers:
                link = None if n < 10000 else LINKS[n // 10000 - 1]
                items.append((link, n // 1000 % 10, n // 100 % 10, n // 10 % 10, n % 10))
            result[-1].append(items)
    return result


def branches(order, rx, ry, j):
    apart = {"x": rx != 0, "y": ry != 0, "z": j != 0}
    last = max([i for i, axis in enumerate(order) if apart[axis]], default=-1)
    links = []
    for i, axis in enumerate(order):
        if i < last:
            continue
        if axis != "z":
            if i > last:
                links.append((axis, False))
        elif i > last:
            links += [("near", False), ("far", True)]
        else:
            links.append(("far" if j == 1 else "near", True))
    return links


def slot_table(orders):
    table, counts = {}, []
    for g in range(6):
        number = 0
        for rx in range(2):
            for ry in range(2):
                for j in range(4):
                    links = []
                    for layer in range(2):
                        for link, _ in branches(orders[g, layer], rx, ry, j):
                            if link not in links:
                                links.append(link)
                    for link in links:
                        table[g, rx, ry, j, link] = number
                        number += 1
        counts.append(number)
    return table, counts


def towards_owner(order, k, rx, ry, j):
    apart = {"x": rx != 0, "y": ry != 0, "z": j != 0}
    axis = [axis for axis in order if apart[axis]][-1]
    if axis == "x":
        return "x", (0, ry, j)
    if axis == "y":
        return "y", (rx, 0, j)
    if j == 1:
        return "near", (rx, ry, 0)
    if k % 2:
        return "far", (rx, ry, 0 if j == 2 else 1)
    return "near", (rx, ry, j)


def backward_kernel(
    schedule, order_of_steps, orders, slots,
    w_qk, w_pack, w_up, w_down,
    kept_qk, kept_values, kept_probs, kept_slope, kept_middle, kept_low,
    turned_normed, turned_attended, turned_mixed, turned_active,
    inputs, cotangent, lengths,
    out_qk, out_pack, out_up, out_down, out_grads, swapped_low, swapped_grad,
    m_qk, m_pack, m_wide,
    qk, values, probs, slope, middle, entering, t_normed, t_attended, t_mixed, t_active,
    cot, length,
    dy, du, da, dqk, dv,
    far_dy, far_du, far_da, far_dqk, far_dv,
    total, d_mixed, d_attended, shared_two, grads, vectors, far_vectors, columns,
    h_qk, h_pack, h_up, h_down,
    arrived_0, arrived_1, arrived_2, arrived_3, arrived_4, arrived_5,
    r_qk, r_pack, r_up, r_down,
    load_sem, pair_send, pair_recv, credit, swap_send, swap_recv, sum_send, sum_recv, out_sem,
):
    place = Place()
    s, c = place.s, place.c
    held = (h_qk, h_pack, h_up, h_down)
    arrived = (arrived_0, arrived_1, arrived_2, arrived_3, arrived_4, arrived_5)
    result = (r_qk, r_pack, r_up, r_down)
    outs = (out_qk, out_pack, out_up, out_down)

    sources = {
        "qk_matrix": (m_qk, lambda l: w_qk.at[l]),
        "pack0": (m_pack.at[0], lambda l: w_pack.at[0]),
        "pack1": (m_pack.at[1], lambda l: w_pack.at[1]),
        "down0": (m_wide.at[0:16], lambda l: w_down.at[l, pl.ds(0, 16)]),
        "down1": (m_wide.at[16:32], lambda l: w_down.at[l, pl.ds(16, 16)]),
        "down2": (m_wide.at[32:48], lambda l: w_down.at[l, pl.ds(32, 16)]),
        "down3": (m_wide.at[48:64], lambda l: w_down.at[l, pl.ds(48, 16)]),
        "up0": (m_wide.at[0:16], lambda l: w_up.at[l, :, :, pl.ds(0, 768)]),
        "up1": (m_wide.at[16:32], lambda l: w_up.at[l, :, :, pl.ds(768, 768)]),
        "up2": (m_wide.at[32:48], lambda l: w_up.at[l, :, :, pl.ds(1536, 768)]),
        "up3": (m_wide.at[48:64], lambda l: w_up.at[l, :, :, pl.ds(2304, 768)]),
        "qk": (qk, lambda l: kept_qk.at[l]),
        "values": (values, lambda l: kept_values.at[l]),
        "probs": (probs, lambda l: kept_probs.at[l]),
        "slope": (slope, lambda l: kept_slope.at[l]),
        "middle": (middle, lambda l: kept_middle.at[l]),
        "entering": (entering, lambda l: inputs.at[s, 0] if l == 0 else kept_low.at[0]),
        "normed": (t_normed, lambda l: turned_normed.at[l]),
        "attended": (t_attended, lambda l: turned_attended.at[l]),
        "mixed": (t_mixed, lambda l: turned_mixed.at[l]),
        "active": (t_active, lambda l: turned_active.at[l]),
        "cotangent": (cot, lambda l: cotangent.at[s, 0]),
    }
    names = list(sources)

    def loading(name, layer):
        target, source = sources[name]
        return pltpu.make_async_copy(
            source(layer), target, load_sem.at[names.index(name)]
        )

    def load(*which, layer):
        for name in which:
            loading(name, layer).start()

    def loaded(*which, layer):
        for name in which:
            loading(name, layer).wait()

    fetch_length = pltpu.make_async_copy(lengths, length, out_sem.at[8])
    fetch_length.start()
    load("cotangent", "down0", "slope", "down1", "down2", "down3", layer=1)
    greet(place)

    across = place.neighbour("x")
    low_swap = remote(kept_low.at[1], swapped_low, swap_send.at[0], swap_recv.at[0], across)
    grad_swap = remote(grads.at[1 - s], swapped_grad, swap_send.at[1], swap_recv.at[1], across)

    shared = {
        "dy": (dy, far_dy),
        "du0": (du.at[:, 0:1536], far_du.at[:, 0:1536]),
        "du1": (du.at[:, 1536:3072], far_du.at[:, 1536:3072]),
        "da": (da, far_da),
        "dqk": (dqk, far_dqk),
        "dv": (dv, far_dv),
        "vectors": (vectors, far_vectors),
    }
    shared_names = list(shared)

    def exchange(name, layer):
        n = shared_names.index(name)
        return remote(
            *shared[name], pair_send.at[n], pair_recv.at[n], place.neighbour("core")
        )

    def hand(name, layer):
        if layer == 0:
            pl.semaphore_wait(credit.at[shared_names.index(name)], 1)
        exchange(name, layer).start()

    def done_with(name, layer):
        if layer == 1:
            pl.semaphore_signal(
                credit.at[shared_names.index(name)],
                1,
                device_id=place.neighbour("core"),
                device_id_type=MESH,
            )

    def free_to_write(name, layer):
        if layer == 0:
            exchange(name, 1).wait_send()

    def summed(left, right, far_right):
        return product(flat3(left[0]), right) + product(flat3(left[1]), far_right)

    def flat3(block):
        return block.reshape(-1, block.shape[-1])

    def norm_rows(layer):
        window = flat(m_pack[layer, :, :, :, NORMS - 64 : NORMS + 64]).astype(F32)
        rows = window.T
        return [rows[64 + i : 65 + i, :] for i in range(4)]

    def norm_back(grad, rows, gain):
        unit, scale = normalized(rows)
        scaled = grad * gain
        inner = scaled - jnp.mean(scaled, axis=-1, keepdims=True)
        inner = inner - unit * jnp.mean(scaled * unit, axis=-1, keepdims=True)
        return (
            jnp.sum(grad * unit, axis=0, keepdims=True),
            jnp.sum(grad, axis=0, keepdims=True),
            scale * inner,
        )

    def begin(layer):
        if layer == 1:
            vectors[...] = jnp.zeros_like(vectors)
            loaded("cotangent", layer=1)
            fetch_length.wait()
            position = lax.broadcasted_iota(jnp.int32, (LEN, FEATURES), 0)
            grad = jnp.where(position < length[s], cot[...].astype(F32), 0.0)
        else:
            grad = grads[1].astype(F32)
        free_to_write("dy", layer)
        total[...] = grad
        dy[...] = grad.astype(BF)
        if layer == 0:
            hand("dy", layer)

    def through_active(layer, i):
        if i == 0:
            loaded("slope", layer=layer)
            if layer == 1:
                load("active", "mixed", "middle", "pack1", "qk", "values", layer=1)
                load("probs", "attended", "entering", "qk_matrix", "normed", layer=1)
                load("pack0", layer=0)
        if i % 2 == 0:
            free_to_write("du%d" % (i // 2), layer)
        loaded("down%d" % i, layer=layer)
        at = slice(i * 768, (i + 1) * 768)
        grad = times_transposed(dy[...], flat3(m_wide[16 * i : 16 * i + 16]))
        du[:, at] = (grad * slope[:, at].astype(F32)).astype(BF)
        if i == 0 and layer == 1:
            meet(place)
            hand("dy", layer)
            pl.when(s == 0)(low_swap.start)
        if i % 2 == 1:
            hand("du%d" % (i // 2), layer)
        if i == 3:
            load("up0", "up1", "up2", "up3", layer=layer)
            if layer == 1:
                load("slope", layer=0)

    def sum_down(layer, half):
        if half == 0:
            loaded("active", layer=layer)
            exchange("dy", layer).wait_recv()
        rows = slice(half * 96, half * 96 + 96)
        sums = summed(t_active[:, :, rows, :], dy[...], far_dy[...])
        h_down[layer, :, rows, :] = sums.astype(BF).reshape(8, 96, FEATURES)
        if half == 1:
            done_with("dy", layer)
            if layer == 1:
                load("active", layer=0)

    def to_mixed(layer, q):
        loaded("up%d" % q, layer=layer)
        part = times_transposed(
            du[:, q * 768 : (q + 1) * 768], flat3(m_wide[16 * q : 16 * q + 16])
        )
        d_mixed[...] = part if q == 0 else d_mixed[...] + part
        if layer == 1 and q == 3:
            load("down0", "down1", "down2", "down3", layer=0)

    def sum_up(layer, q):
        if q == 0:
            loaded("mixed", layer=layer)
        if q % 2 == 0:
            exchange("du%d" % (q // 2), layer).wait_recv()
        at = slice(q * 768, (q + 1) * 768)
        sums = summed(t_mixed[...], du[:, at], far_du[:, at])
        h_up[layer, :, :, at] = sums.astype(BF).reshape(8, 48, 768)
        if q % 2 == 1:
            done_with("du%d" % (q // 2), layer)
        if q == 3 and layer == 1:
            load("mixed", layer=0)

    def second_norm(layer):
        loaded("middle", "pack%d" % layer, layer=layer)
        free_to_write("vectors", layer)
        free_to_write("da", layer)
        gain, bias, through = norm_back(d_mixed[...], middle[...], norm_rows(layer)[2])
        vectors[2:3, :] = gain
        vectors[3:4, :] = bias
        grad = total[...] + through
        total[...] = grad
        da[...] = grad.astype(BF)
        hand("da", layer)

    def to_attended(layer):
        matrix = flat(m_pack[layer, :, :, :, HALF:FIRST])
        d_attended[...] = times_transposed(da[...], matrix).astype(BF)
        if layer == 1:
            load("middle", layer=0)

    def through_attention(layer, pair):
        if pair == 0:
            loaded("qk", "values", "probs", layer=layer)
            free_to_write("dqk", layer)
            free_to_write("dv", layer)
        left = lane_index((LEN, 128)) < 64
        at = slice(pair * 128, (pair + 1) * 128)
        key_at = slice(FEATURES + pair * 128, FEATURES + (pair + 1) * 128)
        queries, keys, head_values = qk[:, at], qk[:, key_at], values[:, at]
        grad = d_attended[:, at]
        parts = []
        for head in range(2):
            chosen = left if head == 0 else jnp.logical_not(left)
            soft = probs[2 * pair + head]
            to_soft = times_transposed(
                jnp.where(chosen, head_values, jnp.zeros_like(head_values)), grad
            )
            exact = soft.astype(F32)
            inner = jnp.sum(exact * to_soft, axis=0, keepdims=True)
            to_scores = (exact * (to_soft - inner)).astype(BF)
            parts.append(
                (
                    transposed_times(to_scores, keys),
                    product(to_scores, queries),
                    product(soft, grad),
                )
            )
        of_queries, of_keys, of_values = [
            jnp.where(left, one, other) for one, other in zip(*parts)
        ]
        dqk[:, at] = (of_queries * HD**-0.5).astype(BF)
        dqk[:, key_at] = (of_keys * HD**-0.5).astype(BF)
        if pair < 3:
            dv[:, at] = of_values.astype(BF)
        else:
            there = slice((pair - 3) * 128, (pair - 2) * 128)
            if layer == 1:
                shared_two[:, there] = of_values.astype(BF)
            else:
                dv[:, at] = (of_values + shared_two[:, there].astype(F32)).astype(BF)
        if pair == 5:
            hand("dqk", layer)
            hand("dv", layer)
            if layer == 1:
                load("qk", "values", "probs", layer=0)

    def first_window(part):
        if part == 0:
            window = lambda ref: ref[:, HALF : HALF + 256]
        else:
            window = lambda ref: pltpu.roll(
                ref[:, HALF + 128 :].astype(F32), 192, 1
            ).astype(BF)
        inside = lane_index((LEN, 256)) < 192
        return [
            jnp.where(inside, window(ref), jnp.zeros((LEN, 256), BF)) for ref in (dv, far_dv)
        ]

    def to_normed(layer):
        loaded("qk_matrix", layer=layer)
        grad = times_transposed(dqk[...], flat(m_qk[...]))
        grad = grad + times_transposed(dv[:, :HALF], flat(m_pack[layer, :, :, :, :HALF]))
        if layer == 0:
            for part in range(2):
                grad = grad + times_transposed(
                    first_window(part)[0], flat(m_pack[part, :, :, :, FIRST : FIRST + 256])
                )
        d_mixed[...] = grad
        if layer == 1:
            load("qk_matrix", layer=0)

    def first_norm(layer):
        loaded("entering", layer=layer)
        rows = entering[...].astype(F32)
        gain, bias, through = norm_back(d_mixed[...], rows, norm_rows(layer)[0])
        vectors[0:1, :] = gain
        vectors[1:2, :] = bias
        hand("vectors", layer)
        grads[layer] = (total[...] + through).astype(BF)
        own_grads(layer).start()
        if layer == 1:
            load("entering", layer=0)
        pl.when(s == 1 - layer)(grad_swap.start)

    def sum_out(layer):
        loaded("attended", layer=layer)
        exchange("da", layer).wait_recv()
        sums = summed(t_attended[...], da[...], far_da[...])
        h_pack[layer, :, :, HALF:FIRST] = sums.astype(BF).reshape(8, 48, FEATURES)
        done_with("da", layer)
        if layer == 1:
            load("attended", layer=0)

    def sum_qk(layer):
        loaded("normed", layer=layer)
        exchange("dqk", layer).wait_recv()
        for q in range(2):
            at = slice(q * FEATURES, (q + 1) * FEATURES)
            sums = summed(t_normed[...], dqk[:, at], far_dqk[:, at])
            h_qk[layer, :, :, at] = sums.astype(BF).reshape(8, 48, FEATURES)
        done_with("dqk", layer)

    def sum_pack(layer):
        exchange("dv", layer).wait_recv()
        exchange("vectors", layer).wait_recv()
        sums = summed(t_normed[...], dv[:, :HALF], far_dv[:, :HALF])
        h_pack[layer, :, :, :HALF] = sums.astype(BF).reshape(8, 48, HALF)
        both = vectors[...] + far_vectors[...]
        nothing = jnp.zeros((64, FEATURES), F32)
        tall = jnp.concatenate([nothing, both, nothing[:56]], axis=0)
        columns[layer] = tall.T.astype(BF).reshape(8, 2, 48, 128)
        if layer == 0:
            for part in range(2):
                sums = summed(t_normed[...], *first_window(part)).reshape(8, 48, 256)
                h_pack[part, :, :, FIRST : FIRST + 128] = sums[:, :, :128].astype(BF)
                h_pack[part, :, :, FIRST + 128 :] = (
                    sums[:, :, 128:] + columns[part, :, c].astype(F32)
                ).astype(BF)
        done_with("dv", layer)
        done_with("vectors", layer)
        if layer == 1:
            load("normed", layer=0)

    def own_grads(layer):
        return pltpu.make_async_copy(grads.at[layer], out_grads.at[layer], out_sem.at[6 + layer])

    steps = []

    def step(action, *arguments):
        steps.append(functools.partial(action, *arguments))

    for layer in (1, 0):
        step(begin, layer)
        for i in range(4):
            step(through_active, layer, i)
        for half in range(2):
            step(sum_down, layer, half)
        for q in range(4):
            step(to_mixed, layer, q)
        for q in range(4):
            step(sum_up, layer, q)
        step(second_norm, layer)
        step(to_attended, layer)
        for pair in range(6):
            step(through_attention, layer, pair)
        step(sum_out, layer)
        step(to_normed, layer)
        step(first_norm, layer)
        step(sum_qk, layer)
        step(sum_pack, layer)

    steps = [steps[number] for number in order_of_steps]

    first_slot = [sum(ref.shape[0] for ref in arrived[:g]) for g in range(6)]

    def sum_copy(k, item):
        g, layer, ry, j = item
        rx = int(k // 2 != layer)
        link, there = towards_owner(orders[g, layer], k, rx, ry, j)
        return remote(
            piece_of(held[ARRAY_OF[g]].at[layer, place.block(ry, j)], g),
            arrived[g].at[slots[(g,) + there + (link,)]],
            sum_send.at[g, layer],
            sum_recv.at[first_slot[g] + slots[(g,) + there + (link,)]],
            place.neighbour(link),
        )

    def run_items(k, items):
        for item in items:
            g, layer, ry, j = item
            rx = int(k // 2 != layer)
            mine = piece_of(held[ARRAY_OF[g]].at[layer, place.block(ry, j)], g)
            terms = []
            for link, middle_only in branches(orders[g, layer], rx, ry, j):
                if middle_only and not k % 2:
                    continue
                slot = slots[g, rx, ry, j, link]
                remote(
                    mine,
                    arrived[g].at[slot],
                    sum_send.at[g, layer],
                    sum_recv.at[first_slot[g] + slot],
                    place.neighbour(link),
                ).wait_recv()
                terms.append(arrived[g].at[slot])
            final = (rx, ry, j) == (0, 0, 0)
            target = piece_of(result[ARRAY_OF[g]], g) if final else mine
            if terms or final:
                add_up(target, [mine] + terms)
            if not final:
                sum_copy(k, item).start()
                continue
            out = piece_of(outs[ARRAY_OF[g]], g)
            pltpu.make_async_copy(target, out, out_sem.at[g]).start()

    def add_up(target, terms):
        @pl.loop(0, target.shape[0] // 16)
        def _(i):
            at = pl.ds(pl.multiple_of(i * 16, 16), 16)
            sums = terms[0][at, :].astype(F32)
            for term in terms[1:]:
                sums = sums + term[at, :].astype(F32)
            target[at, :] = sums.astype(target.dtype)

    for number in range(len(steps) + 1):
        for k in range(4):
            if schedule[k][number]:
                pl.when(place.is_class(k))(
                    functools.partial(run_items, k, schedule[k][number])
                )
        if number < len(steps):
            steps[number]()

    for k in range(4):

        def finish(k=k):
            for g in range(6):
                for layer in range(2):
                    own = k // 2 == layer
                    if own:
                        pltpu.make_async_copy(
                            piece_of(result[ARRAY_OF[g]], g),
                            piece_of(outs[ARRAY_OF[g]], g),
                            out_sem.at[g],
                        ).wait()
                    part = piece_of(held[ARRAY_OF[g]].at[layer, 0 : 7 if own else 8], g)
                    remote(
                        part, part, sum_send.at[g, layer], sum_recv.at[0], place.neighbour("x")
                    ).wait_send()

        pl.when(place.is_class(k))(finish)
    for name in shared_names:
        exchange(name, 0).wait_send()
    pl.when(s == 0)(low_swap.wait_send)
    pl.when(s == 1)(low_swap.wait_recv)
    grad_swap.wait()
    for layer in range(2):
        own_grads(layer).wait()


def backward_call(schedule, order_of_steps, orders, weights, kept, turned, inputs, cotangent, lengths):
    slots, counts = slot_table(orders)
    blocks = [(48, 2 * FEATURES), (48, PACK), (48, HIDDEN), (192, FEATURES)]
    pieces = [(48, 1536), (48, PACK), (48, 1536), (48, 1536), (96, FEATURES), (96, FEATURES)]
    rows = (LEN, FEATURES)
    outs = [jax.ShapeDtypeStruct(block, F32) for block in blocks]
    outs += [jax.ShapeDtypeStruct((2,) + rows, BF)] + [jax.ShapeDtypeStruct(rows, BF)] * 2
    pair = [rows, (LEN, HIDDEN), rows, (LEN, 2 * FEATURES), rows]
    scratch = [
        pltpu.VMEM((8, 2, 48, 2 * FEATURES), BF),
        pltpu.VMEM((2, 8, 2, 48, PACK), BF),
        pltpu.VMEM((64, 48, FEATURES), BF),
        pltpu.VMEM((LEN, 2 * FEATURES), BF),
        pltpu.VMEM(rows, BF),
        pltpu.VMEM((HEADS, LEN, LEN), BF),
        pltpu.VMEM((LEN, HIDDEN), BF),
        pltpu.VMEM(rows, F32),
        pltpu.VMEM(rows, BF),
        pltpu.VMEM((2, 8, 48, LEN), BF),
        pltpu.VMEM((2, 8, 48, LEN), BF),
        pltpu.VMEM((2, 8, 48, LEN), BF),
        pltpu.VMEM((2, 8, 192, LEN), BF),
        pltpu.VMEM(rows, BF),
        pltpu.SMEM((2,), jnp.int32),
    ]
    scratch += [pltpu.VMEM(shape, BF) for shape in pair + pair]
    scratch += [
        pltpu.VMEM(rows, F32),
        pltpu.VMEM(rows, F32),
        pltpu.VMEM(rows, BF),
        pltpu.VMEM((LEN, HALF), BF),
        pltpu.VMEM((2,) + rows, BF),
        pltpu.VMEM((8, FEATURES), F32),
        pltpu.VMEM((8, FEATURES), F32),
        pltpu.VMEM((2, 8, 2, 48, 128), BF),
    ]
    scratch += [pltpu.VMEM((2, 8) + block, BF) for block in blocks]
    scratch += [pltpu.VMEM((count,) + piece, BF) for count, piece in zip(counts, pieces)]
    scratch += [pltpu.VMEM(block, F32) for block in blocks]
    scratch += [
        pltpu.SemaphoreType.DMA((22,)),
        pltpu.SemaphoreType.DMA((7,)),
        pltpu.SemaphoreType.DMA((7,)),
        pltpu.SemaphoreType.REGULAR((7,)),
        pltpu.SemaphoreType.DMA((2,)),
        pltpu.SemaphoreType.DMA((2,)),
        pltpu.SemaphoreType.DMA((6, 2)),
        pltpu.SemaphoreType.DMA((sum(counts),)),
        pltpu.SemaphoreType.DMA((9,)),
    ]
    anywhere = pl.BlockSpec(memory_space=pl.ANY)
    operands = [
        weights[0],
        weights[1],
        weights[2].reshape(2, 16, 48, HIDDEN),
        weights[3].reshape(2, 64, 48, FEATURES),
    ]
    operands += list(kept) + list(turned) + [inputs, cotangent]
    return pl.pallas_call(
        functools.partial(backward_kernel, schedule, order_of_steps, orders, slots),
        out_shape=outs,
        in_specs=[anywhere] * (len(operands) + 1),
        out_specs=[anywhere] * len(outs),
        scratch_shapes=scratch,
        compiler_params=pltpu.CompilerParams(
            collective_id=1, has_side_effects=True, vmem_limit_bytes=63 * 2**20
        ),
    )(*operands, lengths)


GATHER = (
    (
        (12000, 13000, 25000, 30000, 35000, 20000, 2001, 31000, 22000, 11000, 5010, 14000, 1100,
        10, 0, 1000, 2000, 3000, 4000, 5000, 35010, 10000, 32000, 24000, 10010, 1, 23000, 20001,
        2010, 15010, 4010, 12010, 32010, 21000, 3100, 2100, 1001, 11, 2, 15000, 5100, 20002,
        33000, 3001, 21100, 35100, 10002, 100, 34000, 10011, 5001, 3002, 10001, 22100, 5011, 12,
        21001, 1101, 25100, 10012, 14010, 2101, 3, 20003, 12001, 23002, 23100, 3101, 1010,
        10003, 2013, 2011, 23101, 15001, 12011, 5002, 1103, 21103, 13, 1003, 21101, 1102, 15002,
        21102, 5012, 4102, 10013, 21003, 34010, 1113, 2012, 1002, 12012, 3110, 1011, 1111, 3103,
        2002, 15012, 21002, 1110, 23001, 111, 22101, 5013, 2103, 1112, 3010, 12002, 12013, 3102,
        1013, 3003, 23003, 3111, 4103, 1012),
        (),
        (15011, 22103, 2003, 4100, 2102),
        (5110, 23103),
        (),
        (101, 4001, 3012, 12003, 4012, 5003, 102, 4011, 112, 2111, 103),
        (15013, 4101, 3011),
        (23102, 15003, 3013, 4111),
        (),
        (22102, 4003),
        (4013, 113, 110, 4002, 4110),
        (2113, 3113),
        (),
        (5102, 25102, 2110),
        (),
        (),
        (4113, 5101, 25101),
        (2112,),
        (),
        (5103, 25103),
        (),
        (),
        (3112, 5112),
        (),
        (),
        (5111, 5113, 4112),
        (),
        (),
        (),
    ),
    (
        (13000, 32000, 24000, 30000, 43000, 15000, 31000, 35000, 42000, 22000, 25000, 11000,
        14000, 40000, 0, 1000, 2000, 3000, 4000, 5000, 1, 40001, 2010, 5001, 12010, 21000, 4010,
        10001, 5010, 14010, 1001, 45000, 41001, 2, 3002, 30002, 20002, 21001, 3, 35010, 5011,
        20000, 41000, 5100, 33002, 20001, 2002, 23002, 1003, 10003, 33000, 15001, 31003, 45010,
        1011, 2011, 30003, 42010, 2100, 20003, 1100, 1002, 44000, 21003, 12011, 1102, 21002,
        21102, 21100, 31002, 1101, 42011, 3012, 2012, 45100, 12012, 2102, 34000, 15011, 44010,
        5101, 4001, 12, 45011, 25100, 5002, 35002, 3100, 13, 2013, 2001, 3001, 44001, 21101,
        43001, 100, 11, 32010, 15010, 10, 5012, 1103, 1013, 42001, 10010, 32013, 21103, 5102,
        12013, 32012, 1110, 34010, 4002, 10011, 5013, 10012, 4012, 15012, 25101, 10000, 101,
        35012, 3101, 3003, 15013, 45001, 1010, 3103, 23000, 23103, 1112, 1113, 1111, 5110, 1012,
        32002, 5003, 10013, 12002, 45101, 33003, 2003, 22100, 35013, 2103),
        (4011, 23001, 10002),
        (103, 12003, 32003, 5111, 22102, 2101, 3113, 4003, 3102),
        (34012, 5103, 34003, 23003, 44011, 35003, 102, 4013),
        (12001, 23102),
        (),
        (3010, 12000),
        (111, 22101, 23101, 4101),
        (34013, 15002, 4111, 3013, 3011, 4102, 23100, 15003, 22103),
        (25103, 110, 34002),
        (35102, 4112, 2110),
        (),
        (25102, 35100, 3112),
        (113, 112),
        (),
        (4100,),
        (2111, 35103),
        (),
        (4110,),
        (3111,),
        (2112, 2113),
        (),
        (3110,),
        (),
        (),
        (4113, 4103),
        (5112, 5113),
        (),
        (),
    ),
    (
        (11100, 20100, 31100, 21100, 34100, 32100, 22100, 13100, 10100, 12100, 23100, 2101,
        33100, 30100, 100, 1100, 2100, 3100, 4100, 5100, 15100, 14100, 4101, 24100, 1000, 24101,
        1101, 101, 22101, 31000, 3000, 33000, 12101, 11101, 3101, 20101, 23101, 10101, 2110,
        1102, 111, 13101, 110, 10110, 35100, 1001, 21001, 4000, 0, 25100, 34000, 21101, 2000,
        1103, 4102, 21102, 2010, 11103, 14102, 21000, 3103, 3102, 13102, 4103, 21103, 4111,
        10111, 11102, 2103, 24103, 23000, 10, 2102, 14101, 1010, 1003, 3110, 1112, 24102, 4010,
        13103, 1002, 1011, 21002, 102, 5110, 34010, 12, 12103, 21003, 103, 4113, 20103, 1110, 1,
        10102, 14111, 3001, 5000, 20102, 1113, 22103, 5010, 14103, 3003, 1012, 4110, 1013, 113,
        12102, 23001, 22102, 2111, 1111, 112, 10103, 3, 13, 2, 3002, 10112, 23002, 11, 10113,
        5101, 3010, 4112, 23003, 2001),
        (2012,),
        (4012,),
        (),
        (),
        (),
        (2002,),
        (2011, 2013),
        (14110, 23103),
        (14112, 4011, 5001, 14113, 3012, 4002, 23102, 5002, 2003, 3011, 5011, 3013, 4001, 2112,
        25101),
        (5012,),
        (),
        (4013, 4003, 5013, 3113, 2113, 5003),
        (),
        (5103, 25103),
        (),
        (3111,),
        (5111,),
        (3112, 5102, 25102),
        (),
        (),
        (),
        (),
        (5113,),
        (),
        (5112,),
        (),
        (),
        (),
    ),
    (
        (42100, 21100, 41100, 20100, 34100, 12100, 10100, 32100, 33100, 1101, 15100, 13100,
        41101, 23100, 100, 1100, 2100, 3100, 4100, 5100, 3000, 43100, 30100, 2102, 23000, 31100,
        1000, 4101, 44100, 1102, 40100, 21000, 41000, 11102, 110, 31102, 11101, 3101, 1103,
        12102, 31103, 21101, 43101, 101, 11100, 24100, 21102, 31000, 40101, 10101, 4102, 13101,
        44101, 34102, 3102, 1001, 41001, 20101, 24101, 23102, 11103, 2101, 3103, 32102, 14100,
        3001, 10110, 1002, 4000, 33103, 103, 33102, 4103, 21001, 3110, 42101, 21002, 102, 1003,
        4111, 34103, 13102, 2103, 2011, 32103, 31003, 31002, 43001, 13103, 44000, 30102, 21003,
        45100, 111, 4110, 30103, 21103, 1013, 12101, 5001, 5101, 3003, 10111, 22102, 1010,
        33000, 1112, 20103, 22101, 43000, 12103, 23001, 3002, 1011, 10103, 14101, 2010, 24102,
        10102, 23002, 2013, 1110, 14111, 23101, 5010, 23003, 4002, 14102, 5011, 4001, 1111,
        45101, 4010, 33002, 12, 33003, 44010, 3, 34000, 20102, 44001, 22103, 35100, 113, 5102,
        10, 4012, 4011, 34012, 13, 1012, 3111, 0, 4112, 4003, 34010, 24103, 14112, 1, 1113, 11,
        2, 3011, 3013, 10113, 44011, 2002, 112, 2012, 5103),
        (10112, 34002, 2003, 3012, 25101),
        (),
        (14110, 22100, 4013, 3010, 25102, 25103, 34013),
        (),
        (),
        (),
        (4113, 34003, 14113, 5000),
        (2000, 23103, 2001, 5012, 2113),
        (5013,),
        (2112, 25100, 5111, 35103),
        (2111,),
        (5002, 14103, 35102, 5003),
        (2110,),
        (5112,),
        (3112,),
        (),
        (),
        (),
        (),
        (5113,),
        (),
        (),
        (3113,),
        (),
        (5110,),
        (),
        (),
        (),
    ),
)

SUMS = (
    (
        (),
        (),
        (),
        (4102,),
        (5110, 5113),
        (),
        (),
        (4101, 4111),
        (),
        (5111,),
        (2113,),
        (4113,),
        (),
        (),
        (),
        (),
        (3113,),
        (3103, 2110, 2112),
        (),
        (4103, 5112),
        (),
        (),
        (),
        (3112, 4112),
        (2103,),
        (),
        (),
        (),
        (),
        (4002, 2111),
        (4001,),
        (),
        (),
        (),
        (2012, 4013),
        (2102,),
        (),
        (),
        (3111,),
        (),
        (112, 2011, 102),
        (4011, 2013),
        (),
        (5102,),
        (),
        (4003, 2002, 3012, 5103, 113, 2101, 5012),
        (),
        (),
        (),
        (),
        (100,),
        (),
        (5013,),
        (),
        (4012,),
        (),
        (1113, 3013, 110, 1111, 1110, 101, 5101, 2003, 5003, 1112, 3110, 1101, 111, 1103, 5011,
        1013, 3003, 5002, 5010, 3002, 2100, 1102, 13, 1012, 3102, 3, 1003, 3011, 3100, 1011,
        4110, 5001, 12, 103, 2010, 2001, 1001, 1002, 3010, 11, 5100, 3101, 10, 4010, 1100, 4100,
        2, 3001, 1, 5000, 1010, 2000, 4000, 0, 3000, 1000),
    ),
    (
        (),
        (),
        (),
        (),
        (5111,),
        (),
        (5112,),
        (),
        (),
        (),
        (2112,),
        (2111, 5110),
        (),
        (),
        (3113,),
        (),
        (2113,),
        (2110, 3101),
        (),
        (5113,),
        (),
        (),
        (),
        (3112, 3110),
        (),
        (),
        (),
        (),
        (4103,),
        (),
        (),
        (),
        (4112, 2012),
        (4110,),
        (),
        (4113, 102, 2013, 4102, 5012, 3111, 113),
        (),
        (),
        (),
        (3011,),
        (),
        (5013,),
        (2102, 5103),
        (),
        (),
        (3013,),
        (4013,),
        (),
        (2103, 4002),
        (112, 3012, 5010, 2011, 5101),
        (4011, 2002),
        (),
        (3102,),
        (2101, 111, 101),
        (2100,),
        (),
        (1113, 4012, 4003, 1111, 5003, 1011, 1012, 5102, 11, 13, 4100, 4001, 5011, 3103, 1112,
        1013, 2010, 103, 110, 2003, 1110, 1010, 4111, 12, 1103, 3003, 4101, 3002, 5001, 5002,
        1101, 1102, 100, 3100, 3001, 2001, 5100, 3, 1003, 3010, 1100, 1002, 4010, 1, 1001, 5000,
        2, 10, 3000, 2000, 4000, 1000, 0),
    ),
    (
        (),
        (),
        (),
        (4113,),
        (5110,),
        (),
        (),
        (4112, 5112),
        (),
        (4111,),
        (4103,),
        (2113,),
        (),
        (2112, 4102, 2111),
        (),
        (5111,),
        (4101,),
        (),
        (),
        (),
        (),
        (),
        (),
        (),
        (),
        (),
        (),
        (),
        (),
        (4003,),
        (5013, 5113),
        (5012,),
        (2103, 4001, 5010, 5011),
        (5003,),
        (4013, 2013),
        (),
        (4012,),
        (3113,),
        (),
        (),
        (),
        (3013, 3010, 4002, 2003),
        (4011,),
        (),
        (),
        (2102,),
        (),
        (5000,),
        (),
        (),
        (2012,),
        (5002, 112, 3003),
        (),
        (),
        (3012,),
        (),
        (3011, 5103, 3103, 1113, 3002, 12, 3, 13, 102, 113, 2002, 2011, 10, 3111, 1112, 5102, 1,
        11, 5001, 1012, 1103, 3000, 1102, 1013, 1002, 2001, 1111, 4010, 111, 1010, 3112, 1011,
        1003, 2, 0, 2101, 2010, 5101, 1110, 110, 3102, 103, 2110, 101, 3001, 3110, 4000, 1001,
        3101, 4110, 2000, 5100, 1101, 1000, 3100, 1100, 2100, 100, 4100),
    ),
    (
        (),
        (),
        (),
        (),
        (5111,),
        (5110,),
        (),
        (),
        (),
        (),
        (),
        (),
        (),
        (2111,),
        (),
        (),
        (2112, 5112),
        (),
        (),
        (),
        (),
        (),
        (),
        (),
        (2113,),
        (),
        (),
        (),
        (),
        (),
        (5003,),
        (5113,),
        (),
        (5012,),
        (2110,),
        (),
        (5001,),
        (),
        (5013,),
        (),
        (),
        (3110, 3012, 5002),
        (4003,),
        (4112, 5000, 3013, 2010, 2103, 2012, 4103),
        (),
        (3112, 5011),
        (),
        (),
        (),
        (4102, 4013),
        (),
        (2011, 5010),
        (),
        (3011,),
        (),
        (4101, 4113, 4002, 11),
        (2013, 2102, 3010, 3113, 5103, 112, 1013, 13, 4012, 4001, 1011, 1113, 4000, 2101, 12,
        3002, 2003, 4011, 1112, 4111, 2001, 2002, 10, 5101, 5102, 3111, 3003, 102, 3001, 1,
        3103, 1111, 3, 113, 4010, 1103, 1012, 2000, 0, 110, 111, 1010, 1003, 1002, 1001, 2,
        2100, 3101, 4110, 103, 1101, 3102, 5100, 3000, 1102, 1110, 100, 101, 1000, 4100, 3100,
        1100),
    ),
)

STEPS = (
    0, 1, 5, 6, 2, 3, 4, 11, 12, 7, 8, 13, 14, 9, 10, 15, 16, 17, 18, 19, 20, 21, 22, 24, 25,
    28, 29, 30, 33, 34, 39, 40, 31, 26, 23, 32, 35, 41, 42, 36, 37, 38, 27, 43, 44, 45, 46, 47,
    48, 49, 50, 51, 52, 54, 53, 55,
)

ORDERS = {
    (0, 0): "zyx",
    (0, 1): "zyx",
    (1, 0): "xzy",
    (1, 1): "xzy",
    (2, 0): "xzy",
    (2, 1): "xzy",
    (3, 0): "zxy",
    (3, 1): "zyx",
    (4, 0): "yxz",
    (4, 1): "yxz",
    (5, 0): "zyx",
    (5, 1): "zxy",
}


def gather(blocks):
    return [
        lax.all_gather(lax.all_gather(block, "dp", axis=0, tiled=True), "section", axis=0)
        for block in blocks
    ]


def scatter(partials):
    results = []
    for pair in partials:
        both = lax.psum_scatter(jnp.stack(pair), "section", scatter_dimension=0, tiled=False)
        results.append(
            lax.psum_scatter(both.astype(F32), "dp", scatter_dimension=0, tiled=True)
        )
    return results


def norm_back(grad, unit, scale, gain):
    scaled = grad * gain
    inner = scaled - jnp.mean(scaled, axis=-1, keepdims=True)
    inner = inner - unit * jnp.mean(scaled * unit, axis=-1, keepdims=True)
    return jnp.sum(grad * unit, axis=0), jnp.sum(grad, axis=0), scale * inner


def by_head(rows):
    return rows.reshape(rows.shape[0], -1, HD)


def forward(hidden, weights, shared, allowed):
    query_key, value, out, up, down, first, norms = weights
    unit_one, scale_one = normalized(hidden)
    normed = (unit_one * norms[0] + norms[1]).astype(BF)
    qk = product(normed, query_key).astype(BF)
    fresh = product(normed, value).astype(BF)
    if shared is None:
        shared = product(normed, first).astype(BF)
    features = hidden.shape[1]
    queries, keys = by_head(qk[:, :features]), by_head(qk[:, features:])
    values = by_head(jnp.concatenate([fresh, shared], axis=1))
    scores = jnp.einsum("qhd,khd->hqk", queries, keys, preferred_element_type=F32) * HD**-0.5
    scores = jnp.where(allowed, scores, -1e30)
    raised = jnp.exp(scores - jnp.max(scores, axis=-1, keepdims=True))
    soft = raised / jnp.sum(raised, axis=-1, keepdims=True)
    probs = soft.astype(BF)
    attended = jnp.einsum("hqk,khd->qhd", probs, values, preferred_element_type=F32)
    attended = attended.reshape(hidden.shape).astype(BF)
    middle = hidden + product(attended, out)
    unit_two, scale_two = normalized(middle)
    mixed = (unit_two * norms[2] + norms[3]).astype(BF)
    upper = product(mixed, up)
    active = jax.nn.gelu(upper, approximate=True).astype(BF)
    output = middle + product(active, down)
    kept = (normed, queries, keys, values, soft, attended, unit_one, scale_one)
    return output, shared, kept + (unit_two, scale_two, mixed, upper, active)


def backward(grad, weights, kept, grad_shared_next):
    query_key, value, out, up, down, first, norms = weights
    normed, queries, keys, values, soft, attended, unit_one, scale_one = kept[:8]
    unit_two, scale_two, mixed, upper, active = kept[8:]
    positions, features = grad.shape
    half = value.shape[1]
    grad_low = grad.astype(BF)
    down_grad = transposed_times(active, grad_low)
    _, gelu_pull = jax.vjp(lambda u: jax.nn.gelu(u, approximate=True), upper)
    grad_upper = gelu_pull(times_transposed(grad_low, down))[0].astype(BF)
    up_grad = transposed_times(mixed, grad_upper)
    grad_mixed = times_transposed(grad_upper, up)
    two_gain, two_bias, through = norm_back(grad_mixed, unit_two, scale_two, norms[2])
    grad_middle = grad + through
    grad_attn = grad_middle.astype(BF)
    out_grad = transposed_times(attended, grad_attn)
    grad_attended = by_head(times_transposed(grad_attn, out).astype(BF))
    grad_soft = jnp.einsum("qhd,khd->hqk", grad_attended, values, preferred_element_type=F32)
    grad_values = jnp.einsum(
        "hqk,qhd->khd", soft.astype(BF), grad_attended, preferred_element_type=F32
    ).reshape(positions, features)
    grad_scores = soft * (grad_soft - jnp.sum(soft * grad_soft, axis=-1, keepdims=True))
    grad_scores = grad_scores.astype(BF)
    grad_queries = jnp.einsum("hqk,khd->qhd", grad_scores, keys, preferred_element_type=F32)
    grad_keys = jnp.einsum("hqk,qhd->khd", grad_scores, queries, preferred_element_type=F32)
    grad_qk = jnp.concatenate(
        [grad_queries.reshape(positions, features), grad_keys.reshape(positions, features)], axis=1
    )
    grad_qk = (grad_qk * HD**-0.5).astype(BF)
    grad_fresh = grad_values[:, :half].astype(BF)
    grad_shared = grad_values[:, half:]
    grad_normed = times_transposed(grad_qk, query_key) + times_transposed(grad_fresh, value)
    if grad_shared_next is not None:
        grad_shared = (grad_shared + grad_shared_next.astype(F32)).astype(BF)
        first_grad = transposed_times(normed, grad_shared)
        grad_normed = grad_normed + times_transposed(grad_shared, first)
    else:
        grad_shared = grad_shared.astype(BF)
        first_grad = None
    one_gain, one_bias, through = norm_back(grad_normed, unit_one, scale_one, norms[0])
    grad_input = (grad_middle + through).astype(BF)
    query_key_grad = transposed_times(normed, grad_qk)
    value_grad = transposed_times(normed, grad_fresh)
    gains = jnp.stack([one_gain, one_bias, two_gain, two_bias], axis=1)
    return grad_input, grad_shared, (
        query_key_grad, value_grad, out_grad, up_grad, down_grad, first_grad, gains
    )


def swapped(block):
    return lax.ppermute(block, "section", [(0, 1), (1, 0)])


def on_any_mesh(
    inputs,
    cotangent,
    lengths,
    norm_one_gain,
    norm_one_bias,
    query_key_weight,
    value_weight,
    out_weight,
    norm_two_gain,
    norm_two_bias,
    up_weight,
    down_weight,
    first_value_weight,
):
    section = lax.axis_index("section")
    first_half = section == 0
    half = value_weight.shape[2]
    features = out_weight.shape[2]
    quarter = first_value_weight.shape[1]
    own_rows = query_key_weight.shape[1]
    norms = jnp.stack([norm_one_gain[0], norm_one_bias[0], norm_two_gain[0], norm_two_bias[0]], axis=1)
    padding = -(half + features + quarter + 4) % 128
    attention = jnp.concatenate(
        [
            value_weight[0],
            out_weight[0],
            first_value_weight,
            norms,
            jnp.zeros((own_rows, padding), BF),
        ],
        axis=1,
    )
    whole = gather([query_key_weight[0], attention, up_weight[0], down_weight[0]])
    after = half + features
    first_matrix = jnp.concatenate(
        [whole[1][0, :, after : after + quarter], whole[1][1, :, after : after + quarter]], axis=1
    )

    def layer_weights(layer):
        packed = whole[1][layer]
        gains = packed[:, after + quarter : after + quarter + 4].astype(F32).T
        return (
            whole[0][layer],
            packed[:, :half],
            packed[:, half:after],
            whole[2][layer],
            whole[3][layer],
            first_matrix,
            gains,
        )

    weights = [layer_weights(0), layer_weights(1)]
    batch_sequences, positions = inputs.shape[1:3]
    hidden = lax.dynamic_index_in_dim(inputs, section, 0, keepdims=False)[0]
    grad = lax.dynamic_index_in_dim(cotangent, section, 0, keepdims=False)[0]
    length = lax.dynamic_index_in_dim(lengths, section, 0, keepdims=False)[0]
    places = jnp.arange(positions)
    live = places < length
    allowed = (places[None, :] <= places[:, None]) & live[None, :]
    output_one, shared, kept_one = forward(hidden.astype(F32), weights[0], None, allowed)
    low_one = output_one.astype(BF)
    output_two, _, kept_two = forward(low_one.astype(F32), weights[1], shared, allowed)
    low_two = output_two.astype(BF)
    outputs_there = swapped(jnp.where(first_half, low_two, low_one))
    outputs_here = jnp.where(first_half, low_one, low_two)
    grad = jnp.where(live[:, None], grad.astype(F32), 0.0)
    grad_one, grad_shared, sums_two = backward(grad, weights[1], kept_two, None)
    grad_zero, _, sums_one = backward(grad_one.astype(F32), weights[0], kept_one, grad_shared)
    grads_there = swapped(jnp.where(first_half, grad_one, grad_zero))
    grads_here = jnp.where(first_half, grad_zero, grad_one)
    first_grad = sums_one[5]

    def packed_sums(sums, first_part):
        return jnp.concatenate(
            [
                sums[1],
                sums[2],
                first_part,
                sums[6],
                jnp.zeros((first_part.shape[0], padding), F32),
            ],
            axis=1,
        ).astype(BF)

    partials = [
        (sums_one[0].astype(BF), sums_two[0].astype(BF)),
        (
            packed_sums(sums_one, first_grad[:, :quarter]),
            packed_sums(sums_two, first_grad[:, quarter:]),
        ),
        (sums_one[3].astype(BF), sums_two[3].astype(BF)),
        (sums_one[4].astype(BF), sums_two[4].astype(BF)),
    ]
    query_key_grad, packed_grad, up_grad, down_grad = scatter(partials)
    gains = packed_grad[:, after + quarter : after + quarter + 4].T

    def both(here, there):
        return jnp.stack(
            [jnp.where(first_half, here, there), jnp.where(first_half, there, here)]
        )[None, :, None]

    return (
        both(outputs_here, outputs_there),
        both(grads_here, grads_there),
        gains[0][None],
        gains[1][None],
        query_key_grad[None],
        packed_grad[:, :half][None],
        packed_grad[:, half:after][None],
        gains[2][None],
        gains[3][None],
        up_grad[None],
        down_grad[None],
        packed_grad[:, after : after + quarter],
    )


def on_device(
    tables,
    inputs,
    cotangent,
    lengths,
    norm_one_gain,
    norm_one_bias,
    query_key_weight,
    value_weight,
    out_weight,
    norm_two_gain,
    norm_two_bias,
    up_weight,
    down_weight,
    first_value_weight,
):
    gather_schedule, sum_schedule, steps, sum_orders = tables
    own = (query_key_weight, value_weight, out_weight, up_weight, down_weight)
    small = (first_value_weight, norm_one_gain, norm_one_bias, norm_two_gain, norm_two_bias)
    lengths = lengths.reshape(-1)
    done = forward_call(gather_schedule, own, small, inputs, lengths)
    weights, kept, turned, one_there = done[:4], done[4:10], done[10:14], done[14]
    back = backward_call(
        sum_schedule, steps, sum_orders, weights, kept, turned, inputs, cotangent, lengths
    )
    return last_call(back, kept[5], one_there)


def last_kernel(
    pack, query_key, up, down, grads, low, one_there, two_there, grad_there,
    out_low, out_grads, out_vector_0, out_vector_1, out_query_key, out_value, out_out,
    out_vector_2, out_vector_3, out_up, out_down, out_first,
    v_query_key, v_up, v_down, v_rows, v_pack, v_first, v_vectors,
    in_sems, out_sems,
):
    s = lax.axis_index("section")
    copies = [
        (query_key, v_query_key, out_query_key.at[0]),
        (up, v_up, out_up.at[0]),
        (down, v_down, out_down.at[0]),
        (low.at[s], v_rows.at[0], out_low.at[0, s, 0]),
        (one_there, v_rows.at[1], out_low.at[0, 1 - s, 0]),
        (grads.at[s], v_rows.at[2], out_grads.at[0, s, 0]),
        (grad_there, v_rows.at[3], out_grads.at[0, 1 - s, 0]),
    ]
    reads = [
        pltpu.make_async_copy(source, held, in_sems.at[i])
        for i, (source, held, _) in enumerate(copies)
    ]
    writes = [
        pltpu.make_async_copy(held, target, out_sems.at[i])
        for i, (_, held, target) in enumerate(copies)
    ]
    for i, read in enumerate(reads):
        if i != 4:
            read.start()
    pl.when(s == 0)(reads[4].start)
    pl.when(s == 1)(pltpu.make_async_copy(two_there, v_rows.at[1], in_sems.at[4]).start)
    read_pack = pltpu.make_async_copy(pack, v_pack, in_sems.at[7])
    read_pack.start()
    for read, write in zip(reads, writes):
        read.wait()
        write.start()
    read_pack.wait()
    v_first[...] = v_pack[:, FIRST:NORMS]
    rows = v_pack[:, NORMS - 64 :].T
    for i in range(4):
        v_vectors[i] = rows[64 + i : 65 + i, :]
    vectors = (out_vector_0, out_vector_1, out_vector_2, out_vector_3)
    rest = [
        (v_pack.at[:, 0:HALF], out_value.at[0]),
        (v_pack.at[:, HALF:FIRST], out_out.at[0]),
        (v_first, out_first),
    ] + [(v_vectors.at[i], vector) for i, vector in enumerate(vectors)]
    for i, (source, target) in enumerate(rest):
        writes.append(pltpu.make_async_copy(source, target, out_sems.at[7 + i]))
        writes[-1].start()
    for write in writes:
        write.wait()


def last_call(back, low, one_there):
    query_key, pack, up, down, grads, two_there, grad_there = back
    anywhere = pl.BlockSpec(memory_space=pl.ANY)
    vector = jax.ShapeDtypeStruct((1, 48), F32)
    rows = jax.ShapeDtypeStruct((1, 2, 1, LEN, FEATURES), BF)

    def block(*shape):
        return jax.ShapeDtypeStruct(shape, F32)

    return pl.pallas_call(
        last_kernel,
        out_shape=[
            rows, rows, vector, vector, block(1, 48, 2 * FEATURES), block(1, 48, HALF),
            block(1, 48, FEATURES), vector, vector, block(1, 48, HIDDEN),
            block(1, 192, FEATURES), block(48, 192),
        ],
        in_specs=[anywhere] * 9,
        out_specs=[anywhere] * 12,
        scratch_shapes=[
            pltpu.VMEM((48, 2 * FEATURES), F32),
            pltpu.VMEM((48, HIDDEN), F32),
            pltpu.VMEM((192, FEATURES), F32),
            pltpu.VMEM((4, LEN, FEATURES), BF),
            pltpu.VMEM((48, PACK), F32),
            pltpu.VMEM((48, 192), F32),
            pltpu.VMEM((4, 1, 48), F32),
            pltpu.SemaphoreType.DMA((8,)),
            pltpu.SemaphoreType.DMA((14,)),
        ],
    )(pack, query_key, up, down, grads, low, one_there, two_there, grad_there)


def solution(mesh):
    placed = (
        P(None, "dp", None, None),
        P(None, "dp", None, None),
        P(None, "dp"),
        P("section", "dp"),
        P("section", "dp"),
        P("section", "dp", None),
        P("section", "dp", None),
        P("section", "dp", None),
        P("section", "dp"),
        P("section", "dp"),
        P("section", "dp", None),
        P("section", "dp", None),
        P("dp", "section"),
    )
    if mesh.shape["dp"] == 16 and mesh.shape["section"] == 2:
        sums = [[[item[1:] for item in items] for items in k] for k in schedule_of(SUMS)]
        body = functools.partial(on_device, (schedule_of(GATHER), sums, STEPS, ORDERS))
    else:
        body = on_any_mesh
    return jax.shard_map(
        body,
        mesh=mesh,
        in_specs=placed,
        out_specs=(
            P("section", None, "dp", None, None),
            P("section", None, "dp", None, None),
            P("section", "dp"),
            P("section", "dp"),
            P("section", "dp", None),
            P("section", "dp", None),
            P("section", "dp", None),
            P("section", "dp"),
            P("section", "dp"),
            P("section", "dp", None),
            P("section", "dp", None),
            P("dp", "section"),
        ),
        check_vma=False,
    )
```
